32 devices in a mesh: ctx: 8 (over z, y), head: 4 (over x, core).
Axes of the slice: x: 2, y: 2, z: 4, core: 2. Of those that a mesh axis runs over, the one named last changes fastest.
Arguments:
- queries: bfloat16 [3072, 1024], P('ctx', 'head'), may hold values from -6 to 6
- keys: bfloat16 [3072, 1024], P('ctx', 'head'), may hold values from -6 to 6
- values: bfloat16 [3072, 1024], P('ctx', 'head'), may hold values from -6 to 6
- out_weight: bfloat16 [1024, 5120], P('head'), may hold values from -1.1953125 to 1.1953125
- neighbours: int32 [8, 7], P('ctx'), may hold values from -1 to 7, as said below
- counts: int32 [8], P('ctx'), may hold values from 1 to 7
Outputs:
- projected: bfloat16 [3072, 5120], P(('ctx', 'head'))
The draws below stay inside these ranges and needn't reach their ends.
Inputs may be any that keep to these rules, and one draw needn't show every extreme that they name: `neighbours`: for query tile g the first counts[g] entries are distinct tiles within 3 of g, g itself among them; the other entries are -1. Some tile lists 7 tiles.
All inputs are finite; a program needn't handle non-finite values.
Results may differ from the reference program's by a relative error of at most 0.019.
Values may be sent and summed in bfloat16 or wider, within the bound.
No kernel may reach another device: no remote copies, remote signals or barrier semaphores. Data moves between devices by JAX's collectives and lax.ppermute only.
A program may use at most 64 MiB of HBM per device.

```python
import math
import jax
import jax.numpy as jnp
from jax import lax

D = 5120
HD = 128
HEADS_DEV = 2
TILE = 384
REACH = 3
HEADS = 8
NTILES = 8
TOKENS = 3072
N_HEAD = 4


def draw_queries(key, part):
    drawn = jnp.clip(1.5 * jax.random.normal(jax.random.fold_in(key, 13), (TOKENS, HEADS * HD), jnp.float32), -6.0, 6.0)
    return drawn.astype(jnp.bfloat16)


def draw_keys(key, part):
    drawn = jnp.clip(jax.random.normal(jax.random.fold_in(key, 11), (TOKENS, HEADS * HD), jnp.float32), -6.0, 6.0)
    return drawn.astype(jnp.bfloat16)


def tile_listing(key):
    window_tiles = 2 * REACH + 1
    tiles = jnp.arange(NTILES, dtype=jnp.int32)[:, None]
    offsets = jnp.arange(window_tiles, dtype=jnp.int32)[None, :] - REACH
    target = tiles + offsets
    in_range = (target >= 0) & (target < NTILES)
    slot_index = jnp.broadcast_to(jnp.arange(window_tiles, dtype=jnp.int32)[None, :], (NTILES, window_tiles))
    priority = jax.random.randint(jax.random.fold_in(key, 3), (NTILES, window_tiles), 0, 1 << 20) * window_tiles + slot_index
    priority = jnp.where(offsets == 0, (1 << 20) * window_tiles + window_tiles, priority)
    priority = jnp.where(in_range, priority, -1 - slot_index)
    unused, ranking = lax.top_k(priority, window_tiles)
    ranked_tiles = jnp.take_along_axis(target, ranking, axis=1)
    in_count = jnp.sum(in_range.astype(jnp.int32), axis=1)
    slot_count = jax.random.randint(jax.random.fold_in(key, 5), (NTILES,), 1, window_tiles + 1)
    slot_count = jnp.minimum(slot_count, in_count)
    slot_count = jnp.where(jnp.arange(NTILES, dtype=jnp.int32) == NTILES // 2, window_tiles, slot_count)
    listing = jnp.where(slot_index < slot_count[:, None], ranked_tiles, -1)
    return (listing.astype(jnp.int32), slot_count.astype(jnp.int32))


def draw_neighbours(key, part):
    listing, slot_count = tile_listing(key)
    return listing


def draw_counts(key, part):
    listing, slot_count = tile_listing(key)
    return slot_count


def shard_levels(rng, extent, shards, smallest, largest):
    loudness = 1.0
    for dim, blocks in shards:
        steps = jax.random.uniform(jax.random.fold_in(jax.random.fold_in(rng, 6), dim), (blocks,), jnp.float32, smallest / len(shards), largest / len(shards))
        loudness = loudness * jnp.repeat(jnp.exp(steps), extent[dim] // blocks).reshape((-1,) + (1,) * (len(extent) - 1 - dim))
    return loudness


def normal_values(rng, dims, scale, bound, shards=(), kind=jnp.bfloat16):
    loudness = shard_levels(rng, dims, shards, -0.22, 0.18) if shards else 1.0
    array = jax.random.normal(rng, dims, jnp.float32) * scale * loudness
    return jnp.minimum(jnp.maximum(array, -bound), bound).astype(kind)


def setup_inputs(seed: int = 0) -> dict:
    splits = jax.random.split(jax.random.key(seed), 7)
    queries = draw_queries(jax.random.fold_in(splits[6], 71), 0)
    keys = draw_keys(jax.random.fold_in(splits[6], 71), 0)
    values = normal_values(splits[2], (TOKENS, HEADS * HD), 1.0, 6.0, ((0, 8), (1, 4)))
    out_weight = normal_values(splits[3], (HEADS * HD, D), 0.2, 1.1953125, ((0, 4),))
    neighbours = draw_neighbours(jax.random.fold_in(splits[6], 71), 0)
    counts = draw_counts(jax.random.fold_in(splits[6], 71), 0)
    return {"queries": queries, "keys": keys, "values": values, "out_weight": out_weight, "neighbours": neighbours, "counts": counts}


def reference(queries, keys, values, out_weight, neighbours, counts):
    window_tiles = 2 * REACH + 1
    tile_total = counts.shape[0]
    feat_width = HEADS * HD
    padding = jnp.zeros((REACH * TILE, feat_width), keys.dtype)
    keys_padded = jnp.concatenate([padding, keys, padding], axis=0)
    values_padded = jnp.concatenate([padding, values, padding], axis=0)
    offsets = jnp.arange(window_tiles, dtype=jnp.int32) - REACH
    slot_index = jnp.arange(window_tiles, dtype=jnp.int32)
    scale = 1.0 / math.sqrt(HD)

    def one_tile(tile_index):
        target = tile_index + offsets
        listing = lax.dynamic_index_in_dim(neighbours, tile_index, 0, keepdims=False)
        slot_count = lax.dynamic_index_in_dim(counts, tile_index, 0, keepdims=False)
        member = jnp.any((listing[None, :] == target[:, None]) & (slot_index[None, :] < slot_count), axis=1)
        allowed = member & (target >= 0) & (target < tile_total)
        key_mask = jnp.repeat(allowed, TILE)
        q_tile = lax.dynamic_slice_in_dim(queries, (tile_index * TILE).astype(jnp.int32), TILE, 0)
        k_tile = lax.dynamic_slice_in_dim(keys_padded, (tile_index * TILE).astype(jnp.int32), window_tiles * TILE, 0)
        v_tile = lax.dynamic_slice_in_dim(values_padded, (tile_index * TILE).astype(jnp.int32), window_tiles * TILE, 0)
        q_heads = q_tile.reshape(TILE, HEADS, HD).astype(jnp.float32)
        k_heads = k_tile.reshape(window_tiles * TILE, HEADS, HD).astype(jnp.float32)
        v_heads = v_tile.reshape(window_tiles * TILE, HEADS, HD).astype(jnp.float32)
        scores = jnp.einsum('qhd,khd->hqk', q_heads, k_heads) * scale
        scores = jnp.where(key_mask[None, None, :], scores, -1e+30)
        row_max = lax.optimization_barrier(jnp.max(scores, axis=2, keepdims=True))
        weights = jnp.where(key_mask[None, None, :], jnp.exp(scores - row_max), 0.0)
        weight_sum = lax.optimization_barrier(jnp.sum(weights, axis=2))
        weights_low = weights.astype(jnp.bfloat16).astype(jnp.float32)
        mixed = jnp.einsum('hqk,khd->qhd', weights_low, v_heads)
        mixed = mixed / jnp.transpose(weight_sum)[:, :, None]
        return mixed.reshape(TILE, feat_width).astype(jnp.bfloat16)
    attended = lax.map(one_tile, jnp.arange(tile_total, dtype=jnp.int32)).reshape(tile_total * TILE, feat_width)
    group_width = HEADS_DEV * HD
    summed = jnp.zeros((attended.shape[0], out_weight.shape[1]), jnp.float32)
    for head_group in range(N_HEAD):
        block_cols = attended[:, head_group * group_width:(head_group + 1) * group_width]
        block_rows = out_weight[head_group * group_width:(head_group + 1) * group_width]
        partial_term = jnp.dot(block_cols, block_rows, preferred_element_type=jnp.float32)
        rounded = lax.optimization_barrier(partial_term.astype(jnp.bfloat16))
        summed = summed + rounded.astype(jnp.float32)
    return summed.astype(jnp.bfloat16)
```

```python
import functools
import math

import jax
import jax.numpy as jnp
from jax import lax
from jax.experimental import pallas as pl
from jax.experimental.pallas import tpu as pltpu
from jax.sharding import PartitionSpec as P

HD = 128
REACH = 3
NEG = -1e30
GATHERED = 2560


def attend_kernel(tile_ref, list_ref, count_ref, q_ref, *refs):
    tiles, out_ref = refs[: 2 * REACH + 1], refs[2 * REACH + 1]
    max_ref, sum_ref, acc_ref = refs[2 * REACH + 2 :]
    rows, width = q_ref.shape
    heads = width // HD
    tile_index = tile_ref[0]
    max_ref[...] = jnp.full_like(max_ref, NEG)
    sum_ref[...] = jnp.zeros_like(sum_ref)
    acc_ref[...] = jnp.zeros_like(acc_ref)
    for offset in range(-REACH, REACH + 1):
        target = tile_index + offset
        listed = jnp.bool_(False)
        for slot in range(list_ref.shape[1]):
            listed |= (list_ref[0, slot] == target) & (slot < count_ref[0])
        tile = tiles[offset + REACH]

        @pl.when(listed & (target >= 0))
        def _():
            for head in range(heads):
                cols = slice(head * HD, (head + 1) * HD)
                k_head = tile[:, cols]
                v_head = tile[:, slice(width + head * HD, width + (head + 1) * HD)]
                scores = lax.dot_general(
                    q_ref[:, cols],
                    k_head,
                    (((1,), (1,)), ((), ())),
                    preferred_element_type=jnp.float32,
                ) * (1.0 / math.sqrt(HD))
                old = max_ref[:, head : head + 1]
                new = jnp.maximum(old, jnp.max(scores, axis=1, keepdims=True))
                weights = jnp.exp(scores - new)
                shrink = jnp.exp(old - new)
                sum_ref[:, head : head + 1] = sum_ref[:, head : head + 1] * shrink + jnp.sum(
                    weights, axis=1, keepdims=True
                )
                max_ref[:, head : head + 1] = new
                acc_ref[:, cols] = acc_ref[:, cols] * shrink + jnp.dot(
                    weights.astype(jnp.bfloat16), v_head, preferred_element_type=jnp.float32
                )

    for head in range(heads):
        cols = slice(head * HD, (head + 1) * HD)
        out_ref[:, cols] = (acc_ref[:, cols] / sum_ref[:, head : head + 1]).astype(out_ref.dtype)


def attend(tile_index, neighbours, counts, queries, tiles):
    rows, width = queries.shape
    heads = width // HD
    area = rows * rows * len(tiles) * heads
    smem = pl.BlockSpec(memory_space=pltpu.SMEM)
    vmem = pl.BlockSpec(memory_space=pltpu.VMEM)
    return pl.pallas_call(
        attend_kernel,
        out_shape=jax.ShapeDtypeStruct((rows, width), jnp.bfloat16),
        in_specs=[smem] * 3 + [vmem] * (1 + len(tiles)),
        out_specs=vmem,
        scratch_shapes=[
            pltpu.VMEM((rows, heads), jnp.float32),
            pltpu.VMEM((rows, heads), jnp.float32),
            pltpu.VMEM((rows, width), jnp.float32),
        ],
        compiler_params=pltpu.CompilerParams(vmem_limit_bytes=32 * 1024 * 1024),
        cost_estimate=pl.CostEstimate(
            flops=4 * area * HD,
            bytes_accessed=2 * rows * width * (2 + 2 * len(tiles)),
            transcendentals=area,
        ),
    )(tile_index, neighbours, counts, queries, *tiles)


def shifted(value, axis, steps):
    count = lax.axis_size(axis)
    first, last = (max(0, -steps), min(count, count - steps))
    return lax.ppermute(value, axis, [(source, source + steps) for source in range(first, last)])


def swap_cores(value):
    count = lax.axis_size("head")
    return lax.ppermute(value, "head", [(i, i ^ 1) for i in range(count)])


def from_chip(value, steps):
    count = lax.axis_size("head")
    return lax.ppermute(value, "head", [((i + 2 * steps) % count, i) for i in range(count)])


def local(queries, keys, values, out_weight, neighbours, counts):
    rows, width = queries.shape
    n_head = lax.axis_size("head")
    chips = n_head // 2
    own_rows = rows // n_head
    head_index = lax.axis_index("head")
    chip, core = head_index // 2, head_index % 2
    model = out_weight.shape[1]
    gathered = GATHERED if chips == 2 else 0
    f32 = jnp.float32

    both = jnp.concatenate([keys, values], axis=1)
    tiles = {0: both}
    for distance in range(REACH, 0, -1):
        tiles[-distance] = shifted(both, "ctx", distance)
        tiles[distance] = shifted(both, "ctx", -distance)

    weight_pair = swap_cores(out_weight)
    far = []
    for steps in range(1, chips):
        if gathered:
            other = from_chip(out_weight[:, :gathered], steps)
            far.append((other, swap_cores(other)))

    tile_index = lax.axis_index("ctx").astype(jnp.int32).reshape(1)
    attended = attend(
        tile_index,
        neighbours,
        counts,
        queries,
        [tiles[offset] for offset in range(-REACH, REACH + 1)],
    )

    blocks = attended.reshape(chips, 2, own_rows, width)
    mine = lax.dynamic_index_in_dim(blocks, core, 1, keepdims=False)
    theirs = lax.dynamic_index_in_dim(blocks, 1 - core, 1, keepdims=False)
    joined = jnp.concatenate([mine, swap_cores(theirs)], axis=2)

    def project(block, weights):
        return jnp.dot(block[:, :width], weights[0], preferred_element_type=f32) + jnp.dot(
            block[:, width:], weights[1], preferred_element_type=f32
        )

    near = (out_weight, weight_pair)
    right = [weight[:, gathered:] for weight in near]
    received, received_blocks = [], []
    for steps in range(1, chips):
        block = lax.dynamic_index_in_dim(joined, (chip - steps) % chips, 0, keepdims=False)
        received.append(from_chip(project(block, right).astype(jnp.bfloat16), steps))
        if gathered:
            received_blocks.append(from_chip(block, steps))
    own = lax.dynamic_index_in_dim(joined, chip, 0, keepdims=False)
    total = project(own, right)
    for partial in received:
        total = total + partial.astype(f32)
    total = total.astype(jnp.bfloat16)
    if gathered:
        left = project(own, [weight[:, :gathered] for weight in near])
        for block, weights in zip(received_blocks, far):
            left = left + project(block, weights)
        total = jnp.concatenate([left.astype(jnp.bfloat16), total], axis=1)
    return total


def solution(mesh):
    placed = (
        P("ctx", "head"),
        P("ctx", "head"),
        P("ctx", "head"),
        P("head", None),
        P("ctx", None),
        P("ctx"),
    )
    return jax.shard_map(
        local, mesh=mesh, in_specs=placed, out_specs=P(("ctx", "head"), None), check_vma=False
    )
```

```python
import functools
import math

import jax
import jax.numpy as jnp
from jax import lax
from jax.experimental import pallas as pl
from jax.experimental.pallas import tpu as pltpu
from jax.sharding import PartitionSpec as P

HD = 128
REACH = 3
NEG = -1e30
FLAGS = 16
GATHERED = 2560
STATE = HD + 8
EXPONENT = math.log2(math.e) / math.sqrt(HD)
BF16, F32 = jnp.bfloat16, jnp.float32

SMEM = pl.BlockSpec(memory_space=pltpu.SMEM)
VMEM = pl.BlockSpec(memory_space=pltpu.VMEM)
HBM = pl.BlockSpec(memory_space=pltpu.HBM)


def call(kernel, outs, ins, flops=0, exps=0, moved=1 << 20, scratch=(), alias=None, in_hbm=()):
    scalars = [x.dtype == jnp.int32 for x in ins]
    return pl.pallas_call(
        kernel,
        out_shape=outs,
        in_specs=[SMEM if s else (HBM if i in in_hbm else VMEM) for i, s in enumerate(scalars)],
        out_specs=jax.tree.map(lambda _: VMEM, outs),
        scratch_shapes=list(scratch),
        input_output_aliases=alias or {},
        compiler_params=pltpu.CompilerParams(vmem_limit_bytes=24 * 1024 * 1024),
        cost_estimate=pl.CostEstimate(flops=flops, bytes_accessed=moved, transcendentals=exps),
    )(*ins)


def shape(dims, dtype=BF16):
    return jax.ShapeDtypeStruct(dims, dtype)


def pack_kernel(
    tile_ref, list_ref, count_ref, q_ref, k_ref, v_ref, w_ref, keep_ref, send_ref, left_ref, sem
):
    parity = tile_ref[0] & 1
    rows = q_ref.shape[0]
    cut = pltpu.make_async_copy(w_ref.at[:, pl.ds(0, left_ref.shape[1])], left_ref, sem)
    cut.start()
    for i, ref in enumerate((q_ref, k_ref, v_ref)):
        for out, head in ((send_ref, 1 - parity), (keep_ref, parity)):
            out[i * rows : (i + 1) * rows, :] = ref[:, pl.ds(pl.multiple_of(head * HD, HD), HD)]
    lane = lax.broadcasted_iota(jnp.int32, (FLAGS, HD), 1)
    flags = jnp.zeros((FLAGS, HD), F32)
    for offset in range(-REACH, REACH + 1):
        listed = jnp.int32(0)
        for slot in range(list_ref.shape[1]):
            found = (list_ref[0, slot] == tile_ref[0] + offset) & (slot < count_ref[0])
            listed = jnp.where(found, 1, listed)
        flags = jnp.where(lane == offset + REACH, listed.astype(F32), flags)
    keep_ref[3 * rows :, :] = flags.astype(BF16)
    send_ref[3 * rows :, :] = flags.astype(BF16)
    cut.wait()


def merge_kernel(tile_ref, keep_ref, came_ref, flag_ref, q_ref, both_ref, even_ref, odd_ref):
    parity = tile_ref[0] & 1
    rows = q_ref.shape[1]
    for place, ref in ((parity, keep_ref), (1 - parity, came_ref)):
        q_ref[place] = ref[0:rows, :]
        both_ref[2 * place] = ref[rows : 2 * rows, :]
        both_ref[2 * place + 1] = ref[2 * rows : 3 * rows, :]
    even_ref[...] = both_ref[0:2]
    odd_ref[...] = both_ref[2:4]
    own = keep_ref[3 * rows :, :].astype(F32)
    other = came_ref[3 * rows :, :].astype(F32)
    even = jnp.where(parity == 0, own, other)[0:8]
    odd = jnp.where(parity == 0, other, own)[0:8]
    row = lax.broadcasted_iota(jnp.int32, (8, HD), 0)
    flag_ref[...] = jnp.where(row == 0, even, odd).astype(jnp.int32)


def step(query, key, value, state_ref, a):
    scores = lax.dot_general(
        key, query, (((1,), (1,)), ((), ())), preferred_element_type=F32
    )
    old = state_ref[a, HD : HD + 1, :]
    new = jnp.maximum(old, jnp.max(scores, axis=0, keepdims=True))
    weights = jnp.exp2((scores - new) * EXPONENT)
    shrink = jnp.exp2((old - new) * EXPONENT)
    state_ref[a, HD : HD + 1, :] = new
    state_ref[a, HD + 1 : HD + 2, :] = state_ref[a, HD + 1 : HD + 2, :] * shrink + jnp.sum(
        weights, axis=0, keepdims=True
    )
    state_ref[a, 0:HD, :] = state_ref[a, 0:HD, :] * shrink + lax.dot_general(
        value, weights.astype(BF16), (((0,), (0,)), ((), ())), preferred_element_type=F32
    )


def visit(flag_ref, q_ref, state_ref, pairs):
    for a, offset, ref, at in pairs:

        @pl.when(flag_ref[a, offset - a + REACH] > 0)
        def _():
            step(q_ref[a], ref[at], ref[at + 1], state_ref, a)


def first_kernel(flag_ref, q_ref, both_ref, state_ref):
    state_ref[...] = jnp.zeros_like(state_ref)
    for a in range(2):
        state_ref[a, HD : HD + 1, :] = jnp.full((1, state_ref.shape[2]), NEG, F32)
    visit(flag_ref, q_ref, state_ref, [(a, t, both_ref, 2 * t) for t in range(2) for a in range(2)])


def second_kernel(flag_ref, q_ref, below_ref, above_ref, _, state_ref):
    pairs = [(a, t - 2, below_ref, 2 * t) for t in range(2) for a in range(2)]
    pairs += [(a, t + 2, above_ref, 2 * t) for t in range(2) for a in range(2)]
    visit(flag_ref, q_ref, state_ref, pairs)


def third_kernel(flag_ref, tile_ref, head_ref, q_ref, below_ref, above_ref, state_ref, *refs):
    outs, last = refs[:-1], refs[-1]
    last[...] = state_ref[...]
    visit(flag_ref, q_ref, last, [(0, -3, below_ref, 0), (1, 4, above_ref, 0)])
    parity = tile_ref[0] & 1
    core = head_ref[0] & 1
    for i, a in enumerate((parity, 1 - parity)):
        done = last[a, 0:HD, :] / last[a, HD + 1 : HD + 2, :]
        rows = done.T.astype(BF16)
        if len(outs) == 2:
            outs[i][...] = rows
        else:
            half = outs[0].shape[1]
            for chip in range(2):
                even = rows[(2 * chip) * half : (2 * chip + 1) * half]
                odd = rows[(2 * chip + 1) * half : (2 * chip + 2) * half]
                outs[2 * i][chip] = jnp.where(core == 0, even, odd)
                outs[2 * i + 1][chip] = jnp.where(core == 0, odd, even)


CHUNK = 512


def multiply(left, weights, start, stop):
    depth = weights[0].shape[0]
    return sum(
        jnp.dot(
            left[:, i * depth : (i + 1) * depth], w[:, start:stop], preferred_element_type=F32
        )
        for i, w in enumerate(weights)
    )


def send_kernel(
    tile_ref, head_ref, own_ref, y_ref, core_ref, cross_ref, w_ref, wp_ref, a_ref, far_ref, part_ref
):
    parity = tile_ref[0] & 1
    chip = head_ref[0] >> 1
    for out, which in ((a_ref, chip), (far_ref, 1 - chip)):
        for group, (mine, others) in enumerate(((own_ref, y_ref), (core_ref, cross_ref))):
            base = group * 2 * HD
            out[:, pl.ds(pl.multiple_of(base + parity * HD, HD), HD)] = mine[which]
            out[:, pl.ds(pl.multiple_of(base + (1 - parity) * HD, HD), HD)] = others[which]
    far = far_ref[...]
    gathered = w_ref.shape[1] - part_ref.shape[1]
    for start in range(0, part_ref.shape[1], CHUNK):
        stop = min(start + CHUNK, part_ref.shape[1])
        part_ref[:, start:stop] = multiply(
            far, (w_ref, wp_ref), gathered + start, gathered + stop
        ).astype(BF16)


def near_kernel(a_ref, w_ref, wp_ref, near_ref):
    own = a_ref[...]
    for start in range(0, w_ref.shape[1], CHUNK):
        near_ref[:, start : start + CHUNK] = multiply(own, (w_ref, wp_ref), start, start + CHUNK)


def last_kernel(near_ref, far_ref, wx_ref, wxp_ref, part_ref, out_ref):
    far = far_ref[...]
    gathered = wx_ref.shape[1]
    for start in range(0, gathered, CHUNK):
        stop = min(start + CHUNK, gathered)
        out_ref[:, start:stop] = (
            near_ref[:, start:stop] + multiply(far, (wx_ref, wxp_ref), start, stop)
        ).astype(BF16)
    out_ref[:, gathered:] = (near_ref[:, gathered:] + part_ref[...].astype(F32)).astype(BF16)


def shifted(value, steps):
    count = lax.axis_size("ctx")
    first, last = (max(0, -steps), min(count, count - steps))
    return lax.ppermute(value, "ctx", [(source, source + steps) for source in range(first, last)])


def swap_tiles(value):
    return lax.ppermute(value, "ctx", [(i, i ^ 1) for i in range(lax.axis_size("ctx"))])


def swap_cores(value):
    return lax.ppermute(value, "head", [(i, i ^ 1) for i in range(lax.axis_size("head"))])


def swap_both(value):
    heads = lax.axis_size("head")
    count = lax.axis_size("ctx") * heads
    pairs = [(i, ((i // heads) ^ 1) * heads + ((i % heads) ^ 1)) for i in range(count)]
    return lax.ppermute(value, ("ctx", "head"), pairs)


def from_chip(value, steps):
    count = lax.axis_size("head")
    return lax.ppermute(value, "head", [((i + 2 * steps) % count, i) for i in range(count)])


def project_any(attended, out_weight, weight_pair, head_index):
    rows, width = attended.shape
    n_head = lax.axis_size("head")
    chips, own_rows = n_head // 2, rows // n_head
    chip, core = head_index // 2, head_index % 2
    blocks = attended.reshape(chips, 2, own_rows, width)
    mine = lax.dynamic_index_in_dim(blocks, core, 1, keepdims=False)
    theirs = lax.dynamic_index_in_dim(blocks, 1 - core, 1, keepdims=False)
    joined = jnp.concatenate([mine, swap_cores(theirs)], axis=2)

    def project(steps):
        block = lax.dynamic_index_in_dim(joined, (chip - steps) % chips, 0, keepdims=False)
        return multiply(block, (out_weight, weight_pair), 0, out_weight.shape[1])

    total = project(0)
    for steps in range(1, chips):
        total = total + from_chip(project(steps).astype(BF16), steps).astype(F32)
    return total.astype(BF16)


def local(queries, keys, values, out_weight, neighbours, counts):
    rows, width = queries.shape
    n_head = lax.axis_size("head")
    own_rows = rows // n_head
    model = out_weight.shape[1]
    small = n_head == 4 and own_rows % 16 == 0
    head_index = lax.axis_index("head").astype(jnp.int32)
    head = head_index.reshape(1)
    tile = lax.axis_index("ctx").astype(jnp.int32).reshape(1)

    one = (rows, HD)
    gathered = GATHERED if small else CHUNK
    payload = shape((3 * rows + FLAGS, HD))
    keep, send, left_weight = call(
        pack_kernel,
        (payload, payload, shape((width, gathered))),
        (tile, neighbours, counts, queries, keys, values, out_weight),
        scratch=(pltpu.SemaphoreType.DMA,),
        in_hbm=(6,),
    )
    came = swap_tiles(send)
    weight_ready, _ = lax.optimization_barrier((out_weight, send))
    weight_pair = swap_cores(weight_ready)
    came, weight_pair = lax.optimization_barrier((came, weight_pair))
    if small:
        far_weight = from_chip(left_weight, 1)

    flags, q_pair, both, even, odd = call(
        merge_kernel,
        (shape((8, HD), jnp.int32), shape((2,) + one), shape((4,) + one))
        + (shape((2,) + one),) * 2,
        (tile, keep, came),
    )
    below, above = shifted(both, 2), shifted(both, -2)
    far_below, far_above = shifted(odd, 4), shifted(even, -4)

    state = shape((2, STATE, rows), F32)
    area = rows * rows
    held = call(first_kernel, state, (flags, q_pair, both), 16 * area * HD, 4 * area)
    held = call(
        second_kernel,
        state,
        (flags, q_pair, below, above, held),
        32 * area * HD,
        8 * area,
        alias={4: 0},
    )
    block = (2, own_rows, HD)
    attended = call(
        third_kernel,
        (shape(block),) * 4 if small else (shape(one),) * 2,
        (flags, tile, head, q_pair, far_below, far_above, held),
        8 * area * HD,
        2 * area,
        scratch=(pltpu.VMEM(state.shape, F32),),
    )
    if not small:
        mine, theirs = attended
        got = swap_tiles(theirs)
        even_tile = tile[0] % 2 == 0
        joined = jnp.concatenate(
            [jnp.where(even_tile, mine, got), jnp.where(even_tile, got, mine)], axis=1
        )
        return project_any(joined, out_weight, weight_pair, head_index)

    far_weight, attended = lax.optimization_barrier((far_weight, attended))
    far_pair = swap_cores(far_weight)
    mine, mine_other, theirs, theirs_other = attended
    from_cross = swap_both(theirs_other)
    from_y = swap_tiles(theirs)
    from_core = swap_cores(mine_other)

    flops = 2 * own_rows * 2 * width * model
    near_weights = (out_weight, weight_pair)
    own_a, far_a, part = call(
        send_kernel,
        (shape((own_rows, 2 * width)),) * 2 + (shape((own_rows, model - GATHERED)),),
        (tile, head, mine, from_y, from_core, from_cross) + near_weights,
        flops // 2,
    )
    got_part = from_chip(part, 1)
    got_a = from_chip(far_a, 1)
    near = call(
        near_kernel, shape((own_rows, model), F32), (own_a,) + near_weights, flops
    )
    return call(
        last_kernel,
        shape((own_rows, model)),
        (near, got_a, far_weight, far_pair, got_part),
        flops // 2,
    )


def solution(mesh):
    placed = (
        P("ctx", "head"),
        P("ctx", "head"),
        P("ctx", "head"),
        P("head", None),
        P("ctx", None),
        P("ctx"),
    )
    return jax.shard_map(
        local, mesh=mesh, in_specs=placed, out_specs=P(("ctx", "head"), None), check_vma=False
    )
```

```python
import functools
import math

import jax
import jax.numpy as jnp
from jax import lax
from jax.experimental import pallas as pl
from jax.experimental.pallas import tpu as pltpu
from jax.sharding import PartitionSpec as P

HD = 128
REACH = 3
NEG = -1e30
FLAGS = 16
GATHERED = 2560
STATE = HD + 8
EXPONENT = math.log2(math.e) / math.sqrt(HD)
BF16, F32 = jnp.bfloat16, jnp.float32

SMEM = pl.BlockSpec(memory_space=pltpu.SMEM)
VMEM = pl.BlockSpec(memory_space=pltpu.VMEM)
HBM = pl.BlockSpec(memory_space=pltpu.HBM)


def call(
    kernel, outs, ins, flops=0, exps=0, moved=1 << 20, scratch=(), alias=None, in_hbm=(), out_hbm=False, vmem=24
):
    scalars = [x.dtype == jnp.int32 for x in ins]
    return pl.pallas_call(
        kernel,
        out_shape=outs,
        in_specs=[SMEM if s else (HBM if i in in_hbm else VMEM) for i, s in enumerate(scalars)],
        out_specs=jax.tree.map(lambda _: HBM if out_hbm else VMEM, outs),
        scratch_shapes=list(scratch),
        input_output_aliases=alias or {},
        compiler_params=pltpu.CompilerParams(vmem_limit_bytes=vmem << 20),
        cost_estimate=pl.CostEstimate(flops=flops, bytes_accessed=moved, transcendentals=exps),
    )(*ins)


def shape(dims, dtype=BF16):
    return jax.ShapeDtypeStruct(dims, dtype)


def pack_kernel(
    tile_ref, list_ref, count_ref, q_ref, k_ref, v_ref,
    keep_q_ref, keep_kv_ref, send_ref, flag_ref, sems,
):
    parity = tile_ref[0] & 1
    rows = q_ref.shape[0]
    copies = []
    for head, kv_out, q_out, q_at in (
        (1 - parity, send_ref, send_ref, 2 * rows),
        (parity, keep_kv_ref, keep_q_ref, 0),
    ):
        columns = pl.ds(pl.multiple_of(head * HD, HD), HD)
        for ref, out, at in ((k_ref, kv_out, 0), (v_ref, kv_out, rows), (q_ref, q_out, q_at)):
            copies.append(
                pltpu.make_async_copy(
                    ref.at[:, columns], out.at[pl.ds(at, rows)], sems.at[len(copies)]
                )
            )
            copies[-1].start()
    lane = lax.broadcasted_iota(jnp.int32, (FLAGS, HD), 1)
    flags = jnp.zeros((FLAGS, HD), F32)
    for offset in range(-REACH, REACH + 1):
        listed = jnp.int32(0)
        for slot in range(list_ref.shape[1]):
            found = (list_ref[0, slot] == tile_ref[0] + offset) & (slot < count_ref[0])
            listed = jnp.where(found, 1, listed)
        flags = jnp.where(lane == offset + REACH, listed.astype(F32), flags)
    flag_ref[...] = flags.astype(BF16)
    for out, at in ((keep_q_ref, rows), (send_ref, 3 * rows)):
        copies.append(
            pltpu.make_async_copy(flag_ref, out.at[pl.ds(at, FLAGS)], sems.at[len(copies)])
        )
        copies[-1].start()
    for each in copies:
        each.wait()


def cut_kernel(w_ref, left_ref, sem):
    copy = pltpu.make_async_copy(w_ref.at[:, pl.ds(0, left_ref.shape[1])], left_ref, sem)
    copy.start()
    copy.wait()


def merge_kernel(tile_ref, keep_ref, came_ref, flag_ref, q_ref, kv_ref):
    parity = tile_ref[0] & 1
    rows = q_ref.shape[1]
    kv_ref[...] = came_ref[0 : 2 * rows, :]
    q_ref[parity] = keep_ref[0:rows, :]
    q_ref[1 - parity] = came_ref[2 * rows : 3 * rows, :]
    own = keep_ref[rows:, :].astype(F32)
    other = came_ref[3 * rows :, :].astype(F32)
    even = jnp.where(parity == 0, own, other)[0:8]
    odd = jnp.where(parity == 0, other, own)[0:8]
    row = lax.broadcasted_iota(jnp.int32, (8, HD), 0)
    flag_ref[...] = jnp.where(row == 0, even, odd).astype(jnp.int32)


def pick_kernel(choice_ref, zero_ref, one_ref, out_ref):
    @pl.when(choice_ref[0] == 0)
    def _():
        out_ref[...] = zero_ref[...]

    @pl.when(choice_ref[0] != 0)
    def _():
        out_ref[...] = one_ref[...]


def step(query, key, value, state_ref, a):
    scores = lax.dot_general(
        key, query, (((1,), (1,)), ((), ())), preferred_element_type=F32
    )
    old = state_ref[a, HD : HD + 1, :]
    new = jnp.maximum(old, jnp.max(scores, axis=0, keepdims=True))
    weights = jnp.exp2((scores - new) * EXPONENT)
    shrink = jnp.exp2((old - new) * EXPONENT)
    state_ref[a, HD : HD + 1, :] = new
    state_ref[a, HD + 1 : HD + 2, :] = state_ref[a, HD + 1 : HD + 2, :] * shrink + jnp.sum(
        weights, axis=0, keepdims=True
    )
    state_ref[a, 0:HD, :] = state_ref[a, 0:HD, :] * shrink + lax.dot_general(
        value, weights.astype(BF16), (((0,), (0,)), ((), ())), preferred_element_type=F32
    )


def visit(flag_ref, q_ref, state_ref, pairs):
    rows = q_ref.shape[1]
    for a, tile, ref in pairs:

        @pl.when(flag_ref[a, tile - a + REACH] > 0)
        def _():
            step(q_ref[a], ref[0:rows, :], ref[rows : 2 * rows, :], state_ref, a)


def first_kernel(flag_ref, tile_ref, q_ref, own_ref, came_ref, below_ref, above_ref, state_ref):
    parity = tile_ref[0] & 1
    state_ref[...] = jnp.zeros_like(state_ref)
    for a in range(2):
        state_ref[a, HD : HD + 1, :] = jnp.full((1, state_ref.shape[2]), NEG, F32)
    tiles = [(parity, own_ref), (1 - parity, came_ref)]
    tiles += [(parity - 2, below_ref), (parity + 2, above_ref)]
    visit(flag_ref, q_ref, state_ref, [(a, t, ref) for t, ref in tiles for a in range(2)])


def far_tile(parity):
    return parity, jnp.where(parity == 0, -3, 4)


def second_kernel(flag_ref, tile_ref, q_ref, below_ref, above_ref, _, state_ref):
    parity = tile_ref[0] & 1
    tiles = [(-1 - parity, below_ref), (3 - parity, above_ref)]
    visit(flag_ref, q_ref, state_ref, [(a, t, ref) for t, ref in tiles for a in range(2)])


def third_kernel(flag_ref, tile_ref, head_ref, q_ref, kept_ref, came_ref, state_ref, *refs):
    outs, last = refs[:-1], refs[-1]
    last[...] = state_ref[...]
    own = tile_ref[0] & 1
    pairs = [far_tile(1 - own) + (kept_ref,), far_tile(own) + (came_ref,)]
    visit(flag_ref, q_ref, last, pairs)
    parity = tile_ref[0] & 1
    core = head_ref[0] & 1
    for i, a in enumerate((parity, 1 - parity)):
        done = last[a, 0:HD, :] / last[a, HD + 1 : HD + 2, :]
        rows = done.T.astype(BF16)
        if len(outs) == 2:
            outs[i][...] = rows
        else:
            half = outs[0].shape[1]
            for chip in range(2):
                even = rows[(2 * chip) * half : (2 * chip + 1) * half]
                odd = rows[(2 * chip + 1) * half : (2 * chip + 2) * half]
                outs[2 * i][chip] = jnp.where(core == 0, even, odd)
                outs[2 * i + 1][chip] = jnp.where(core == 0, odd, even)


CHUNK = 512


def multiply(left, weights, start, stop):
    depth = weights[0].shape[0]
    return sum(
        jnp.dot(
            left[:, i * depth : (i + 1) * depth], w[:, start:stop], preferred_element_type=F32
        )
        for i, w in enumerate(weights)
    )


def join_kernel(tile_ref, head_ref, own_ref, y_ref, core_ref, cross_ref, a_ref, far_ref):
    parity = tile_ref[0] & 1
    chip = head_ref[0] >> 1
    for out, which in ((a_ref, chip), (far_ref, 1 - chip)):
        for group, (mine, others) in enumerate(((own_ref, y_ref), (core_ref, cross_ref))):
            base = group * 2 * HD
            out[:, pl.ds(pl.multiple_of(base + parity * HD, HD), HD)] = mine[which]
            out[:, pl.ds(pl.multiple_of(base + (1 - parity) * HD, HD), HD)] = others[which]


def send_kernel(far_ref, w_ref, wp_ref, part_ref):
    far = far_ref[...]
    gathered = w_ref.shape[1] - part_ref.shape[1]
    for start in range(0, part_ref.shape[1], CHUNK):
        stop = min(start + CHUNK, part_ref.shape[1])
        part_ref[:, start:stop] = multiply(
            far, (w_ref, wp_ref), gathered + start, gathered + stop
        ).astype(BF16)


def near_kernel(a_ref, w_ref, wp_ref, near_ref):
    own = a_ref[...]
    for start in range(0, w_ref.shape[1], CHUNK):
        near_ref[:, start : start + CHUNK] = multiply(own, (w_ref, wp_ref), start, start + CHUNK)


def far_kernel(near_ref, far_ref, wx_ref, wxp_ref, out_ref, left, sem):
    far = far_ref[...]
    gathered = wx_ref.shape[1]
    for start in range(0, gathered, CHUNK):
        stop = min(start + CHUNK, gathered)
        left[:, start:stop] = (
            near_ref[:, start:stop] + multiply(far, (wx_ref, wxp_ref), start, stop)
        ).astype(BF16)
    copy = pltpu.make_async_copy(left, out_ref.at[:, pl.ds(0, gathered)], sem)
    copy.start()
    copy.wait()


def last_kernel(near_ref, part_ref, _, out_ref, right, sem):
    width = part_ref.shape[1]
    gathered = near_ref.shape[1] - width
    right[...] = (near_ref[:, gathered:] + part_ref[...].astype(F32)).astype(BF16)
    copy = pltpu.make_async_copy(right, out_ref.at[:, pl.ds(gathered, width)], sem)
    copy.start()
    copy.wait()


def shifted(value, steps):
    count = lax.axis_size("ctx")
    first, last = (max(0, -steps), min(count, count - steps))
    return lax.ppermute(value, "ctx", [(source, source + steps) for source in range(first, last)])


def passed_on(value, crossed):
    count = lax.axis_size("ctx")
    pairs = [(i, i + 2 if (i + crossed) % 2 else i - 2) for i in range(count)]
    return lax.ppermute(value, "ctx", [(i, j) for i, j in pairs if 0 <= j < count])


def swap_tiles(value):
    return lax.ppermute(value, "ctx", [(i, i ^ 1) for i in range(lax.axis_size("ctx"))])


def swap_cores(value):
    return lax.ppermute(value, "head", [(i, i ^ 1) for i in range(lax.axis_size("head"))])


def swap_both(value):
    heads = lax.axis_size("head")
    count = lax.axis_size("ctx") * heads
    pairs = [(i, ((i // heads) ^ 1) * heads + ((i % heads) ^ 1)) for i in range(count)]
    return lax.ppermute(value, ("ctx", "head"), pairs)


def from_chip(value, steps):
    count = lax.axis_size("head")
    return lax.ppermute(value, "head", [((i + 2 * steps) % count, i) for i in range(count)])


def project_any(attended, out_weight, weight_pair, head_index):
    rows, width = attended.shape
    n_head = lax.axis_size("head")
    chips, own_rows = n_head // 2, rows // n_head
    chip, core = head_index // 2, head_index % 2
    blocks = attended.reshape(chips, 2, own_rows, width)
    mine = lax.dynamic_index_in_dim(blocks, core, 1, keepdims=False)
    theirs = lax.dynamic_index_in_dim(blocks, 1 - core, 1, keepdims=False)
    joined = jnp.concatenate([mine, swap_cores(theirs)], axis=2)

    def project(steps):
        block = lax.dynamic_index_in_dim(joined, (chip - steps) % chips, 0, keepdims=False)
        return multiply(block, (out_weight, weight_pair), 0, out_weight.shape[1])

    total = project(0)
    for steps in range(1, chips):
        total = total + from_chip(project(steps).astype(BF16), steps).astype(F32)
    return total.astype(BF16)


def local(queries, keys, values, out_weight, neighbours, counts):
    rows, width = queries.shape
    n_head = lax.axis_size("head")
    own_rows = rows // n_head
    model = out_weight.shape[1]
    small = n_head == 4 and own_rows % 16 == 0
    head_index = lax.axis_index("head").astype(jnp.int32)
    head = head_index.reshape(1)
    tile = lax.axis_index("ctx").astype(jnp.int32).reshape(1)

    one = (rows, HD)
    kv_shape, q_shape = shape((2 * rows, HD)), shape((rows + FLAGS, HD))
    keep_q, keep_kv, send = call(
        pack_kernel,
        (q_shape, kv_shape, shape((3 * rows + FLAGS, HD))),
        (tile, neighbours, counts, queries, keys, values),
        scratch=(pltpu.VMEM((FLAGS, HD), BF16), pltpu.SemaphoreType.DMA((8,))),
        in_hbm=(3, 4, 5),
        out_hbm=True,
        vmem=60,
    )
    came = swap_tiles(send)
    below, above = shifted(keep_kv, 2), shifted(keep_kv, -2)
    weight_ready, keep_kv = lax.optimization_barrier((out_weight, keep_kv))
    weight_pair = swap_cores(weight_ready)
    if small:
        left_weight = call(
            cut_kernel,
            shape((width, GATHERED)),
            (weight_ready,),
            scratch=(pltpu.SemaphoreType.DMA,),
            in_hbm=(0,),
            out_hbm=True,
            vmem=60,
        )
        far_weight = from_chip(left_weight, 1)
    came, below, above, weight_pair = lax.optimization_barrier((came, below, above, weight_pair))

    parity = tile & 1
    flags, q_pair, came_kv = call(
        merge_kernel,
        (shape((8, HD), jnp.int32), shape((2,) + one), kv_shape),
        (tile, keep_q, came),
    )
    far_kept = passed_on(call(pick_kernel, kv_shape, (parity, above, below)), 0)
    below_came, above_came = shifted(came_kv, 2), shifted(came_kv, -2)

    state = shape((2, STATE, rows), F32)
    area = rows * rows
    held = call(
        first_kernel,
        state,
        (flags, tile, q_pair, keep_kv, came_kv, below, above),
        32 * area * HD,
        8 * area,
    )
    below_came, above_came, held = lax.optimization_barrier((below_came, above_came, held))
    far_came = passed_on(call(pick_kernel, kv_shape, (parity, below_came, above_came)), 1)
    held = call(
        second_kernel,
        state,
        (flags, tile, q_pair, below_came, above_came, held),
        16 * area * HD,
        4 * area,
        alias={5: 0},
    )
    block = (2, own_rows, HD)
    attended = call(
        third_kernel,
        (shape(block),) * 4 if small else (shape(one),) * 2,
        (flags, tile, head, q_pair, far_kept, far_came, held),
        8 * area * HD,
        2 * area,
        scratch=(pltpu.VMEM(state.shape, F32),),
    )
    if not small:
        mine, theirs = attended
        got = swap_tiles(theirs)
        even_tile = tile[0] % 2 == 0
        joined = jnp.concatenate(
            [jnp.where(even_tile, mine, got), jnp.where(even_tile, got, mine)], axis=1
        )
        return project_any(joined, out_weight, weight_pair, head_index)

    mine, mine_other, theirs, theirs_other = attended
    from_cross = swap_both(theirs_other)
    from_y = swap_tiles(theirs)
    from_core = swap_cores(mine_other)

    flops = 2 * own_rows * 2 * width * model
    near_weights = (out_weight, weight_pair)
    own_a, far_a = call(
        join_kernel,
        (shape((own_rows, 2 * width)),) * 2,
        (tile, head, mine, from_y, from_core, from_cross),
    )
    far_weight, far_a = lax.optimization_barrier((far_weight, far_a))
    far_pair = swap_cores(far_weight)
    got_a = from_chip(far_a, 1)
    part = call(
        send_kernel, shape((own_rows, model - GATHERED)), (far_a,) + near_weights, flops // 2
    )
    got_part = from_chip(part, 1)
    near = call(near_kernel, shape((own_rows, model), F32), (own_a,) + near_weights, flops)
    out = shape((own_rows, model))
    done = call(
        far_kernel,
        out,
        (near, got_a, far_weight, far_pair),
        flops // 2,
        scratch=(pltpu.VMEM((own_rows, GATHERED), BF16), pltpu.SemaphoreType.DMA),
        out_hbm=True,
    )
    return call(
        last_kernel,
        out,
        (near, got_part, done),
        scratch=(pltpu.VMEM((own_rows, model - GATHERED), BF16), pltpu.SemaphoreType.DMA),
        alias={2: 0},
        in_hbm=(2,),
        out_hbm=True,
    )


def solution(mesh):
    placed = (
        P("ctx", "head"),
        P("ctx", "head"),
        P("ctx", "head"),
        P("head", None),
        P("ctx", None),
        P("ctx"),
    )
    return jax.shard_map(
        local, mesh=mesh, in_specs=placed, out_specs=P(("ctx", "head"), None), check_vma=False
    )
```

```python
import functools
import math

import jax
import jax.numpy as jnp
from jax import lax
from jax.experimental import pallas as pl
from jax.experimental.pallas import tpu as pltpu
from jax.sharding import PartitionSpec as P

HD = 128
REACH = 3
NEG = -1e30
FLAGS = 16
SIDE = 768
COMMON = 1792
PACK = 58
STATE = HD + 8
EXPONENT = math.log2(math.e) / math.sqrt(HD)
BF16, F32 = jnp.bfloat16, jnp.float32

SMEM = pl.BlockSpec(memory_space=pltpu.SMEM)
VMEM = pl.BlockSpec(memory_space=pltpu.VMEM)
HBM = pl.BlockSpec(memory_space=pltpu.HBM)


def call(
    kernel, outs, ins, flops=0, exps=0, moved=1 << 20, scratch=(), alias=None, in_hbm=(), out_hbm=False, vmem=24
):
    scalars = [x.dtype == jnp.int32 for x in ins]
    return pl.pallas_call(
        kernel,
        out_shape=outs,
        in_specs=[SMEM if s else (HBM if i in in_hbm else VMEM) for i, s in enumerate(scalars)],
        out_specs=jax.tree.map(lambda _: HBM if out_hbm else VMEM, outs),
        scratch_shapes=list(scratch),
        input_output_aliases=alias or {},
        compiler_params=pltpu.CompilerParams(vmem_limit_bytes=vmem << 20),
        cost_estimate=pl.CostEstimate(flops=flops, bytes_accessed=moved, transcendentals=exps),
    )(*ins)


def shape(dims, dtype=BF16):
    return jax.ShapeDtypeStruct(dims, dtype)


def pack_kernel(
    tile_ref, list_ref, count_ref, q_ref, k_ref, v_ref, w_ref,
    keep_ref, send_ref, side_ref, common_ref, sems,
):
    parity = tile_ref[0] & 1
    rows = q_ref.shape[0]
    copies = []

    def copy(source, target):
        copies.append(pltpu.make_async_copy(source, target, sems.at[len(copies)]))
        copies[-1].start()

    for out, head in ((send_ref, 1 - parity), (keep_ref, parity)):
        columns = pl.ds(pl.multiple_of(head * HD, HD), HD)
        for i, ref in enumerate((k_ref, v_ref, q_ref)):
            copy(ref.at[:, columns], out.at[pl.ds(i * rows, rows)])
    side = side_ref.shape[1]
    copy(w_ref.at[:, pl.ds(pl.multiple_of(parity * side, HD), side)], side_ref)
    copy(w_ref.at[:, pl.ds(2 * side, common_ref.shape[1])], common_ref)
    lane = lax.broadcasted_iota(jnp.int32, (FLAGS, HD), 1)
    flags = jnp.zeros((FLAGS, HD), F32)
    for offset in range(-REACH, REACH + 1):
        listed = jnp.int32(0)
        for slot in range(list_ref.shape[1]):
            found = (list_ref[0, slot] == tile_ref[0] + offset) & (slot < count_ref[0])
            listed = jnp.where(found, 1, listed)
        flags = jnp.where(lane == offset + REACH, listed.astype(F32), flags)
    keep_ref[3 * rows :, :] = flags.astype(BF16)
    send_ref[3 * rows :, :] = flags.astype(BF16)
    for each in copies:
        each.wait()


def merge_kernel(tile_ref, keep_ref, came_ref, flag_ref, q_ref, both_ref, odd_ref, even_ref):
    parity = tile_ref[0] & 1
    rows = q_ref.shape[1]
    both_ref[0 : 2 * rows, :] = keep_ref[0 : 2 * rows, :]
    both_ref[2 * rows :, :] = came_ref[0 : 2 * rows, :]
    up = (tile_ref[0] & 4) == 0

    def place(out, own):
        @pl.when(own)
        def _():
            out[...] = keep_ref[0 : 2 * rows, :]

        @pl.when(jnp.logical_not(own))
        def _():
            out[...] = came_ref[0 : 2 * rows, :]

    place(odd_ref, up == (parity == 1))
    if even_ref is not None:
        place(even_ref, up == (parity == 0))
    q_ref[parity] = keep_ref[2 * rows : 3 * rows, :]
    q_ref[1 - parity] = came_ref[2 * rows : 3 * rows, :]
    own = keep_ref[3 * rows :, :].astype(F32)
    other = came_ref[3 * rows :, :].astype(F32)
    even = jnp.where(parity == 0, own, other)[0:8]
    odd = jnp.where(parity == 0, other, own)[0:8]
    row = lax.broadcasted_iota(jnp.int32, (8, HD), 0)
    flag_ref[...] = jnp.where(row == 0, even, odd).astype(jnp.int32)


def step(query, key, value, state_ref, a):
    scores = lax.dot_general(
        key, query, (((1,), (1,)), ((), ())), preferred_element_type=F32
    )
    old = state_ref[a, HD : HD + 1, :]
    new = jnp.maximum(old, jnp.max(scores, axis=0, keepdims=True))
    weights = jnp.exp2((scores - new) * EXPONENT)
    shrink = jnp.exp2((old - new) * EXPONENT)
    state_ref[a, HD : HD + 1, :] = new
    state_ref[a, HD + 1 : HD + 2, :] = state_ref[a, HD + 1 : HD + 2, :] * shrink + jnp.sum(
        weights, axis=0, keepdims=True
    )
    state_ref[a, 0:HD, :] = state_ref[a, 0:HD, :] * shrink + lax.dot_general(
        value, weights.astype(BF16), (((0,), (0,)), ((), ())), preferred_element_type=F32
    )


def visit(flag_ref, q_ref, state_ref, pairs):
    rows = q_ref.shape[1]
    for a, tile, ref, at in pairs:

        @pl.when(flag_ref[a, tile - a + REACH] > 0)
        def _():
            key, value = ref[at : at + rows, :], ref[at + rows : at + 2 * rows, :]
            step(q_ref[a], key, value, state_ref, a)


def visit_pair(flag_ref, tile_ref, q_ref, state_ref, base, ref):
    parity = tile_ref[0] & 1
    rows = q_ref.shape[1]
    tiles = ((base + parity, 0), (base + 1 - parity, 2 * rows))
    visit(flag_ref, q_ref, state_ref, [(a, t, ref, at) for t, at in tiles for a in range(2)])


def first_kernel(flag_ref, tile_ref, q_ref, both_ref, state_ref):
    state_ref[...] = jnp.zeros_like(state_ref)
    for a in range(2):
        state_ref[a, HD : HD + 1, :] = jnp.full((1, state_ref.shape[2]), NEG, F32)
    visit_pair(flag_ref, tile_ref, q_ref, state_ref, 0, both_ref)


def second_kernel(flag_ref, tile_ref, q_ref, first_ref, second_ref, _, state_ref):
    base = jnp.where((tile_ref[0] & 2) == 0, 2, -2)
    visit_pair(flag_ref, tile_ref, q_ref, state_ref, base, first_ref)
    visit_pair(flag_ref, tile_ref, q_ref, state_ref, -base, second_ref)


def third_kernel(flag_ref, tile_ref, head_ref, q_ref, state_ref, *refs, far):
    outs, last = refs[far:-1], refs[-1]
    last[...] = state_ref[...]
    for i in range(far):
        above = ((tile_ref[0] & 4) == 0) == (i == 0)
        which = (jnp.where(above, 1, 0), jnp.where(above, 4, -3), refs[i], 0)
        visit(flag_ref, q_ref, last, [which])
    parity = tile_ref[0] & 1
    core = head_ref[0] & 1
    for i, a in enumerate((parity, 1 - parity)):
        done = last[a, 0:HD, :] / last[a, HD + 1 : HD + 2, :]
        rows = done.T.astype(BF16)
        if len(outs) == 2:
            outs[i][...] = rows
        else:
            half = outs[0].shape[1]
            for chip in range(2):
                even = rows[(2 * chip) * half : (2 * chip + 1) * half]
                odd = rows[(2 * chip + 1) * half : (2 * chip + 2) * half]
                outs[2 * i][chip] = jnp.where(core == 0, even, odd)
                outs[2 * i + 1][chip] = jnp.where(core == 0, odd, even)


CHUNK = 512


def multiply(left, weights, start, stop):
    depth = weights[0].shape[0]
    return sum(
        jnp.dot(
            left[:, i * depth : (i + 1) * depth], w[:, start:stop], preferred_element_type=F32
        )
        for i, w in enumerate(weights)
    )


def send_kernel(
    tile_ref, head_ref, own_ref, y_ref, core_ref, cross_ref, w_ref, wp_ref, a_ref, far_ref
):
    parity = tile_ref[0] & 1
    chip = head_ref[0] >> 1
    deep = a_ref.shape[1]
    for out, which in ((a_ref, chip), (far_ref, 1 - chip)):
        for group, (mine, others) in enumerate(((own_ref, y_ref), (core_ref, cross_ref))):
            base = group * 2 * HD
            out[:, pl.ds(pl.multiple_of(base + parity * HD, HD), HD)] = mine[which]
            out[:, pl.ds(pl.multiple_of(base + (1 - parity) * HD, HD), HD)] = others[which]
    far = far_ref[:, 0:deep]
    term = far_ref.shape[1] - deep
    gathered = w_ref.shape[1] - term
    for start in range(0, term, CHUNK):
        stop = min(start + CHUNK, term)
        far_ref[:, deep + start : deep + stop] = multiply(
            far, (w_ref, wp_ref), gathered + start, gathered + stop
        ).astype(BF16)


def near_kernel(a_ref, w_ref, wp_ref, near_ref):
    own = a_ref[...]
    for start in range(0, w_ref.shape[1], CHUNK):
        near_ref[:, start : start + CHUNK] = multiply(own, (w_ref, wp_ref), start, start + CHUNK)


def last_kernel(tile_ref, near_ref, far_ref, *refs):
    weights, out_ref = refs[:-1], refs[-1]
    parity = tile_ref[0] & 1
    deep = 2 * weights[0].shape[0]
    side = weights[0].shape[1]
    far = far_ref[:, 0:deep]
    places = (parity * side, (1 - parity) * side, 2 * side)
    for i, at in enumerate(places):
        pair = weights[2 * i : 2 * i + 2]
        for start in range(0, pair[0].shape[1], CHUNK):
            stop = min(start + CHUNK, pair[0].shape[1])
            columns = pl.ds(at + start, stop - start)
            if i < 2:
                columns = pl.ds(pl.multiple_of(at + start, HD), stop - start)
            out_ref[:, columns] = (
                near_ref[:, columns] + multiply(far, pair, start, stop)
            ).astype(BF16)
    gathered = 2 * side + weights[4].shape[1]
    out_ref[:, gathered:] = (near_ref[:, gathered:] + far_ref[:, deep:].astype(F32)).astype(BF16)


def swap_pairs(value, distance, phase):
    count = lax.axis_size("ctx")
    pairs = []
    for i in range(count - 2 * distance):
        if (i // 2 // distance) % 2 == phase:
            pairs += [(i, i + 2 * distance), (i + 2 * distance, i)]
    return lax.ppermute(value, "ctx", pairs)


def swap_tiles(value):
    return lax.ppermute(value, "ctx", [(i, i ^ 1) for i in range(lax.axis_size("ctx"))])


def swap_cores(value):
    return lax.ppermute(value, "head", [(i, i ^ 1) for i in range(lax.axis_size("head"))])


def swap_both(value):
    heads = lax.axis_size("head")
    count = lax.axis_size("ctx") * heads
    pairs = [(i, ((i // heads) ^ 1) * heads + ((i % heads) ^ 1)) for i in range(count)]
    return lax.ppermute(value, ("ctx", "head"), pairs)


def from_chip(value, steps):
    count = lax.axis_size("head")
    return lax.ppermute(value, "head", [((i + 2 * steps) % count, i) for i in range(count)])


def project_any(attended, out_weight, weight_pair, head_index):
    rows, width = attended.shape
    n_head = lax.axis_size("head")
    chips, own_rows = n_head // 2, rows // n_head
    chip, core = head_index // 2, head_index % 2
    blocks = attended.reshape(chips, 2, own_rows, width)
    mine = lax.dynamic_index_in_dim(blocks, core, 1, keepdims=False)
    theirs = lax.dynamic_index_in_dim(blocks, 1 - core, 1, keepdims=False)
    joined = jnp.concatenate([mine, swap_cores(theirs)], axis=2)

    def project(steps):
        block = lax.dynamic_index_in_dim(joined, (chip - steps) % chips, 0, keepdims=False)
        return multiply(block, (out_weight, weight_pair), 0, out_weight.shape[1])

    total = project(0)
    for steps in range(1, chips):
        total = total + from_chip(project(steps).astype(BF16), steps).astype(F32)
    return total.astype(BF16)


def local(queries, keys, values, out_weight, neighbours, counts):
    rows, width = queries.shape
    n_head = lax.axis_size("head")
    own_rows = rows // n_head
    model = out_weight.shape[1]
    small = n_head == 4 and own_rows % 16 == 0
    head_index = lax.axis_index("head").astype(jnp.int32)
    head = head_index.reshape(1)
    tile = lax.axis_index("ctx").astype(jnp.int32).reshape(1)

    one = (rows, HD)
    payload, kv_shape = shape((3 * rows + FLAGS, HD)), shape((2 * rows, HD))
    keep, send, side_weight, common_weight = call(
        pack_kernel,
        (payload, payload, shape((width, SIDE)), shape((width, COMMON))),
        (tile, neighbours, counts, queries, keys, values, out_weight),
        scratch=(pltpu.SemaphoreType.DMA((8,)),),
        in_hbm=(3, 4, 5, 6),
        vmem=PACK,
    )
    came = swap_tiles(send)
    weight_ready, keep = lax.optimization_barrier((out_weight, keep))
    weight_pair = swap_cores(weight_ready)
    came, weight_pair = lax.optimization_barrier((came, weight_pair))
    if small:
        side_own = from_chip(side_weight, 1)

    far = 1 if lax.axis_size("ctx") <= 8 else 2
    flags, q_pair, both, *to_far = call(
        merge_kernel if far == 2 else functools.partial(merge_kernel, even_ref=None),
        (shape((8, HD), jnp.int32), shape((2,) + one), shape((4 * rows, HD))) + (kv_shape,) * far,
        (tile, keep, came),
    )
    nearest = [swap_pairs(both, 1, phase) for phase in range(2)]
    farther = [swap_pairs(to_far[i], 2, i) for i in range(far)]

    state = shape((2, STATE, rows), F32)
    area = rows * rows
    held = call(first_kernel, state, (flags, tile, q_pair, both), 16 * area * HD, 4 * area)
    q_again = q_pair
    if small:
        side_own, q_again = lax.optimization_barrier((side_own, q_pair))
        side_other = swap_tiles(side_own)
        common_ready, _ = lax.optimization_barrier((common_weight, side_own))
        common = from_chip(common_ready, 1)
    held = call(
        second_kernel,
        state,
        (flags, tile, q_again, *nearest, held),
        32 * area * HD,
        8 * area,
        alias={5: 0},
    )
    if small:
        ready, held = lax.optimization_barrier((side_own, held))
        far_weights = [side_own, swap_cores(ready)]
        held, side_other = lax.optimization_barrier((held, side_other))
    block = (2, own_rows, HD)
    attended = call(
        functools.partial(third_kernel, far=far),
        (shape(block),) * 4 if small else (shape(one),) * 2,
        (flags, tile, head, q_pair, held, *farther),
        4 * area * HD,
        area,
        scratch=(pltpu.VMEM(state.shape, F32),),
    )
    if not small:
        mine, theirs = attended
        got = swap_tiles(theirs)
        even_tile = tile[0] % 2 == 0
        joined = jnp.concatenate(
            [jnp.where(even_tile, mine, got), jnp.where(even_tile, got, mine)], axis=1
        )
        return project_any(joined, out_weight, weight_pair, head_index)

    mine, mine_other, theirs, theirs_other = attended
    from_cross = swap_both(theirs_other)
    from_y = swap_tiles(theirs)
    from_core = swap_cores(mine_other)
    ready, _ = lax.optimization_barrier((side_other, mine))
    far_weights += [side_other, swap_cores(ready), common]
    from_cross, from_y, from_core, *far_weights = lax.optimization_barrier(
        (from_cross, from_y, from_core, *far_weights)
    )
    far_weights.append(swap_cores(far_weights[-1]))

    flops = 2 * own_rows * 2 * width * model
    near_weights = (out_weight, weight_pair)
    deep, gathered = 2 * width, 2 * SIDE + COMMON
    own_a, far_a = call(
        send_kernel,
        (shape((own_rows, deep)), shape((own_rows, deep + model - gathered))),
        (tile, head, mine, from_y, from_core, from_cross) + near_weights,
        flops // 4,
    )
    got = from_chip(far_a, 1)
    near = call(near_kernel, shape((own_rows, model), F32), (own_a,) + near_weights, flops)
    return call(
        last_kernel, shape((own_rows, model)), (tile, near, got, *far_weights), flops
    )


def solution(mesh):
    placed = (
        P("ctx", "head"),
        P("ctx", "head"),
        P("ctx", "head"),
        P("head", None),
        P("ctx", None),
        P("ctx"),
    )
    return jax.shard_map(
        local, mesh=mesh, in_specs=placed, out_specs=P(("ctx", "head"), None), check_vma=False
    )
```

```python
import functools
import math

import jax
import jax.numpy as jnp
from jax import lax
from jax.experimental import pallas as pl
from jax.experimental.pallas import tpu as pltpu
from jax.sharding import PartitionSpec as P

HD = 128
REACH = 3
NEG = -1e30
FLAGS = 16
SIDE = 768
COMMON = 1792
STATE = HD + 8
EXPONENT = math.log2(math.e) / math.sqrt(HD)
BF16, F32 = jnp.bfloat16, jnp.float32

SMEM = pl.BlockSpec(memory_space=pltpu.SMEM)
VMEM = pl.BlockSpec(memory_space=pltpu.VMEM)
HBM = pl.BlockSpec(memory_space=pltpu.HBM)


def call(
    kernel, outs, ins, flops=0, exps=0, moved=1 << 20, scratch=(), alias=None, in_hbm=(), out_hbm=False, vmem=24
):
    scalars = [x.dtype == jnp.int32 for x in ins]
    return pl.pallas_call(
        kernel,
        out_shape=outs,
        in_specs=[SMEM if s else (HBM if i in in_hbm else VMEM) for i, s in enumerate(scalars)],
        out_specs=jax.tree.map(lambda _: HBM if out_hbm else VMEM, outs),
        scratch_shapes=list(scratch),
        input_output_aliases=alias or {},
        compiler_params=pltpu.CompilerParams(vmem_limit_bytes=vmem << 20),
        cost_estimate=pl.CostEstimate(flops=flops, bytes_accessed=moved, transcendentals=exps),
    )(*ins)


def shape(dims, dtype=BF16):
    return jax.ShapeDtypeStruct(dims, dtype)


def pack_kernel(
    tile_ref, list_ref, count_ref, q_ref, k_ref, v_ref, w_ref,
    keep_q_ref, keep_kv_ref, send_ref, side_ref, sems,
):
    parity = tile_ref[0] & 1
    rows = q_ref.shape[0]
    copies = []

    def copy(source, target):
        copies.append(pltpu.make_async_copy(source, target, sems.at[len(copies)]))
        copies[-1].start()

    for head, kv_out, q_out, q_at in (
        (1 - parity, send_ref, send_ref, 2 * rows),
        (parity, keep_kv_ref, keep_q_ref, 0),
    ):
        columns = pl.ds(pl.multiple_of(head * HD, HD), HD)
        for ref, out, at in ((k_ref, kv_out, 0), (v_ref, kv_out, rows), (q_ref, q_out, q_at)):
            copy(ref.at[:, columns], out.at[pl.ds(at, rows)])
    side = side_ref.shape[1]
    copy(w_ref.at[:, pl.ds(pl.multiple_of(parity * side, HD), side)], side_ref)
    lane = lax.broadcasted_iota(jnp.int32, (FLAGS, HD), 1)
    flags = jnp.zeros((FLAGS, HD), F32)
    for offset in range(-REACH, REACH + 1):
        listed = jnp.int32(0)
        for slot in range(list_ref.shape[1]):
            found = (list_ref[0, slot] == tile_ref[0] + offset) & (slot < count_ref[0])
            listed = jnp.where(found, 1, listed)
        flags = jnp.where(lane == offset + REACH, listed.astype(F32), flags)
    keep_q_ref[rows:, :] = flags.astype(BF16)
    send_ref[3 * rows :, :] = flags.astype(BF16)
    for each in copies:
        each.wait()


def stage_kernel(keep_q_ref, keep_kv_ref, q_ref, kv_ref):
    q_ref[...] = keep_q_ref[...]
    kv_ref[...] = keep_kv_ref[...]


def cut_kernel(w_ref, common_ref, *, first):
    common_ref[...] = w_ref[:, first : first + common_ref.shape[1]]


def merge_kernel(
    tile_ref, keep_q_ref, keep_kv_ref, came_ref, flag_ref, q_ref, kv_ref, odd_ref, even_ref
):
    parity = tile_ref[0] & 1
    rows = q_ref.shape[1]
    kv_ref[...] = came_ref[0 : 2 * rows, :]
    up = (tile_ref[0] & 4) == 0

    def place(out, own):
        @pl.when(own)
        def _():
            out[...] = keep_kv_ref[...]

        @pl.when(jnp.logical_not(own))
        def _():
            out[...] = came_ref[0 : 2 * rows, :]

    place(odd_ref, up == (parity == 1))
    if even_ref is not None:
        place(even_ref, up == (parity == 0))
    q_ref[parity] = keep_q_ref[0:rows, :]
    q_ref[1 - parity] = came_ref[2 * rows : 3 * rows, :]
    own = keep_q_ref[rows:, :].astype(F32)
    other = came_ref[3 * rows :, :].astype(F32)
    even = jnp.where(parity == 0, own, other)[0:8]
    odd = jnp.where(parity == 0, other, own)[0:8]
    row = lax.broadcasted_iota(jnp.int32, (8, HD), 0)
    flag_ref[...] = jnp.where(row == 0, even, odd).astype(jnp.int32)


def step(query, key, value, state_ref, a):
    scores = lax.dot_general(
        key, query, (((1,), (1,)), ((), ())), preferred_element_type=F32
    )
    old = state_ref[a, HD : HD + 1, :]
    new = jnp.maximum(old, jnp.max(scores, axis=0, keepdims=True))
    weights = jnp.exp2((scores - new) * EXPONENT)
    shrink = jnp.exp2((old - new) * EXPONENT)
    state_ref[a, HD : HD + 1, :] = new
    state_ref[a, HD + 1 : HD + 2, :] = state_ref[a, HD + 1 : HD + 2, :] * shrink + jnp.sum(
        weights, axis=0, keepdims=True
    )
    state_ref[a, 0:HD, :] = state_ref[a, 0:HD, :] * shrink + lax.dot_general(
        value, weights.astype(BF16), (((0,), (0,)), ((), ())), preferred_element_type=F32
    )


def visit(flag_ref, q_ref, state_ref, pairs):
    rows = q_ref.shape[1]
    for a, tile, ref in pairs:

        @pl.when(flag_ref[a, tile - a + REACH] > 0)
        def _():
            step(q_ref[a], ref[0:rows, :], ref[rows : 2 * rows, :], state_ref, a)


def visit_pairs(flag_ref, tile_ref, q_ref, state_ref, tiles):
    parity = tile_ref[0] & 1
    for base, own, ref in tiles:
        tile = base + (parity if own else 1 - parity)
        visit(flag_ref, q_ref, state_ref, [(a, tile, ref) for a in range(2)])


def first_kernel(
    flag_ref, tile_ref, q_ref, own_ref, came_ref, kept_first_ref, kept_second_ref, state_ref
):
    state_ref[...] = jnp.zeros_like(state_ref)
    for a in range(2):
        state_ref[a, HD : HD + 1, :] = jnp.full((1, state_ref.shape[2]), NEG, F32)
    base = jnp.where((tile_ref[0] & 2) == 0, 2, -2)
    tiles = [(0, True, own_ref), (0, False, came_ref)]
    tiles += [(base, True, kept_first_ref), (-base, True, kept_second_ref)]
    visit_pairs(flag_ref, tile_ref, q_ref, state_ref, tiles)


def second_kernel(flag_ref, tile_ref, q_ref, first_ref, second_ref, _, state_ref):
    base = jnp.where((tile_ref[0] & 2) == 0, 2, -2)
    tiles = [(base, False, first_ref), (-base, False, second_ref)]
    visit_pairs(flag_ref, tile_ref, q_ref, state_ref, tiles)


def third_kernel(flag_ref, tile_ref, head_ref, q_ref, state_ref, *refs, far):
    outs, last = refs[far:-1], refs[-1]
    last[...] = state_ref[...]
    for i in range(far):
        above = ((tile_ref[0] & 4) == 0) == (i == 0)
        which = (jnp.where(above, 1, 0), jnp.where(above, 4, -3), refs[i])
        visit(flag_ref, q_ref, last, [which])
    parity = tile_ref[0] & 1
    core = head_ref[0] & 1
    for i, a in enumerate((parity, 1 - parity)):
        done = last[a, 0:HD, :] / last[a, HD + 1 : HD + 2, :]
        rows = done.T.astype(BF16)
        if len(outs) == 2:
            outs[i][...] = rows
        else:
            half = outs[0].shape[1]
            for chip in range(2):
                even = rows[(2 * chip) * half : (2 * chip + 1) * half]
                odd = rows[(2 * chip + 1) * half : (2 * chip + 2) * half]
                outs[2 * i][chip] = jnp.where(core == 0, even, odd)
                outs[2 * i + 1][chip] = jnp.where(core == 0, odd, even)


CHUNK = 512


def multiply(left, weights, start, stop):
    depth = weights[0].shape[0]
    return sum(
        jnp.dot(
            left[:, i * depth : (i + 1) * depth], w[:, start:stop], preferred_element_type=F32
        )
        for i, w in enumerate(weights)
    )


def send_kernel(
    tile_ref, head_ref, own_ref, y_ref, core_ref, cross_ref, w_ref, wp_ref, a_ref, far_ref
):
    parity = tile_ref[0] & 1
    chip = head_ref[0] >> 1
    deep = a_ref.shape[1]
    for out, which in ((a_ref, chip), (far_ref, 1 - chip)):
        for group, (mine, others) in enumerate(((own_ref, y_ref), (core_ref, cross_ref))):
            base = group * 2 * HD
            out[:, pl.ds(pl.multiple_of(base + parity * HD, HD), HD)] = mine[which]
            out[:, pl.ds(pl.multiple_of(base + (1 - parity) * HD, HD), HD)] = others[which]
    far = far_ref[:, 0:deep]
    term = far_ref.shape[1] - deep
    gathered = w_ref.shape[1] - term
    for start in range(0, term, CHUNK):
        stop = min(start + CHUNK, term)
        far_ref[:, deep + start : deep + stop] = multiply(
            far, (w_ref, wp_ref), gathered + start, gathered + stop
        ).astype(BF16)


def near_kernel(a_ref, w_ref, wp_ref, near_ref):
    own = a_ref[...]
    for start in range(0, w_ref.shape[1], CHUNK):
        near_ref[:, start : start + CHUNK] = multiply(own, (w_ref, wp_ref), start, start + CHUNK)


def last_kernel(tile_ref, near_ref, far_ref, *refs):
    weights, out_ref = refs[:-1], refs[-1]
    parity = tile_ref[0] & 1
    deep = 2 * weights[0].shape[0]
    far = far_ref[:, 0:deep]
    side = weights[0].shape[1]
    for i, first in enumerate((parity * side, (1 - parity) * side, 2 * side)):
        pair = weights[2 * i : 2 * i + 2]
        for start in range(0, pair[0].shape[1], CHUNK):
            stop = min(start + CHUNK, pair[0].shape[1])
            columns = pl.ds(pl.multiple_of(first + start, HD), stop - start)
            out_ref[:, columns] = (
                near_ref[:, columns] + multiply(far, pair, start, stop)
            ).astype(BF16)
    gathered = 2 * side + weights[4].shape[1]
    out_ref[:, gathered:] = (near_ref[:, gathered:] + far_ref[:, deep:].astype(F32)).astype(BF16)


def swap_pairs(value, distance, phase):
    count = lax.axis_size("ctx")
    pairs = []
    for i in range(count - 2 * distance):
        if (i // 2 // distance) % 2 == phase:
            pairs += [(i, i + 2 * distance), (i + 2 * distance, i)]
    return lax.ppermute(value, "ctx", pairs)


def swap_tiles(value):
    return lax.ppermute(value, "ctx", [(i, i ^ 1) for i in range(lax.axis_size("ctx"))])


def swap_cores(value):
    return lax.ppermute(value, "head", [(i, i ^ 1) for i in range(lax.axis_size("head"))])


def swap_both(value):
    heads = lax.axis_size("head")
    count = lax.axis_size("ctx") * heads
    pairs = [(i, ((i // heads) ^ 1) * heads + ((i % heads) ^ 1)) for i in range(count)]
    return lax.ppermute(value, ("ctx", "head"), pairs)


def from_chip(value, steps):
    count = lax.axis_size("head")
    return lax.ppermute(value, "head", [((i + 2 * steps) % count, i) for i in range(count)])


def project_any(attended, out_weight, weight_pair, head_index):
    rows, width = attended.shape
    n_head = lax.axis_size("head")
    chips, own_rows = n_head // 2, rows // n_head
    chip, core = head_index // 2, head_index % 2
    blocks = attended.reshape(chips, 2, own_rows, width)
    mine = lax.dynamic_index_in_dim(blocks, core, 1, keepdims=False)
    theirs = lax.dynamic_index_in_dim(blocks, 1 - core, 1, keepdims=False)
    joined = jnp.concatenate([mine, swap_cores(theirs)], axis=2)

    def project(steps):
        block = lax.dynamic_index_in_dim(joined, (chip - steps) % chips, 0, keepdims=False)
        return multiply(block, (out_weight, weight_pair), 0, out_weight.shape[1])

    total = project(0)
    for steps in range(1, chips):
        total = total + from_chip(project(steps).astype(BF16), steps).astype(F32)
    return total.astype(BF16)


def local(queries, keys, values, out_weight, neighbours, counts):
    rows, width = queries.shape
    n_head = lax.axis_size("head")
    own_rows = rows // n_head
    model = out_weight.shape[1]
    small = n_head == 4 and own_rows % 16 == 0
    head_index = lax.axis_index("head").astype(jnp.int32)
    head = head_index.reshape(1)
    tile = lax.axis_index("ctx").astype(jnp.int32).reshape(1)

    one = (rows, HD)
    payload, kv_shape = shape((3 * rows + FLAGS, HD)), shape((2 * rows, HD))
    weight_pair = swap_cores(out_weight)
    keep_q, keep_kv, send, side_weight = call(
        pack_kernel,
        (shape((rows + FLAGS, HD)), kv_shape, payload, shape((width, SIDE))),
        (tile, neighbours, counts, queries, keys, values, out_weight),
        scratch=(pltpu.SemaphoreType.DMA((7,)),),
        in_hbm=(3, 4, 5, 6),
        vmem=58,
    )
    came = swap_tiles(send)
    kept_near = [swap_pairs(keep_kv, 1, phase) for phase in range(2)]
    if small:
        side_own = from_chip(side_weight, 1)

    held_q, held_kv = call(stage_kernel, (shape((rows + FLAGS, HD)), kv_shape), (keep_q, keep_kv))
    came, weight_pair, held_q, held_kv, *kept_near = lax.optimization_barrier(
        (came, weight_pair, held_q, held_kv, *kept_near)
    )
    far = 1 if lax.axis_size("ctx") <= 8 else 2
    flags, q_pair, came_kv, *to_far = call(
        merge_kernel if far == 2 else functools.partial(merge_kernel, even_ref=None),
        (shape((8, HD), jnp.int32), shape((2,) + one), kv_shape) + (kv_shape,) * far,
        (tile, held_q, held_kv, came),
    )
    came_near = [swap_pairs(came_kv, 1, phase) for phase in range(2)]
    farther = [swap_pairs(to_far[i], 2, i) for i in range(far)]

    state = shape((2, STATE, rows), F32)
    area = rows * rows
    held = call(
        first_kernel,
        state,
        (flags, tile, q_pair, held_kv, came_kv, *kept_near),
        32 * area * HD,
        8 * area,
    )
    q_again = q_pair
    if small:
        side_own, q_again = lax.optimization_barrier((side_own, q_pair))
        side_other = swap_tiles(side_own)
        ready, _ = lax.optimization_barrier((out_weight, side_own))
        common_weight = call(
            functools.partial(cut_kernel, first=2 * SIDE), shape((width, COMMON)), (ready,)
        )
        common = from_chip(common_weight, 1)
    held = call(
        second_kernel,
        state,
        (flags, tile, q_again, *came_near, held),
        16 * area * HD,
        4 * area,
        alias={5: 0},
    )
    if small:
        held, side_other = lax.optimization_barrier((held, side_other))
    block = (2, own_rows, HD)
    attended = call(
        functools.partial(third_kernel, far=far),
        (shape(block),) * 4 if small else (shape(one),) * 2,
        (flags, tile, head, q_pair, held, *farther),
        4 * area * HD,
        area,
        scratch=(pltpu.VMEM(state.shape, F32),),
    )
    if not small:
        mine, theirs = attended
        got = swap_tiles(theirs)
        even_tile = tile[0] % 2 == 0
        joined = jnp.concatenate(
            [jnp.where(even_tile, mine, got), jnp.where(even_tile, got, mine)], axis=1
        )
        return project_any(joined, out_weight, weight_pair, head_index)

    mine, mine_other, theirs, theirs_other = attended
    from_cross = swap_both(theirs_other)
    from_y = swap_tiles(theirs)
    from_core = swap_cores(mine_other)
    pieces = [side_own, side_other]
    *ready, _ = lax.optimization_barrier((*pieces, mine))
    swapped = [swap_cores(piece) for piece in ready]
    from_cross, from_y, from_core, common, *swapped = lax.optimization_barrier(
        (from_cross, from_y, from_core, common, *swapped)
    )
    pieces.append(common)
    swapped.append(swap_cores(common))
    far_weights = [each for both in zip(pieces, swapped) for each in both]

    flops = 2 * own_rows * 2 * width * model
    near_weights = (out_weight, weight_pair)
    deep, gathered = 2 * width, 2 * SIDE + COMMON
    own_a, far_a = call(
        send_kernel,
        (shape((own_rows, deep)), shape((own_rows, deep + model - gathered))),
        (tile, head, mine, from_y, from_core, from_cross) + near_weights,
        flops // 4,
    )
    got = from_chip(far_a, 1)
    near = call(near_kernel, shape((own_rows, model), F32), (own_a,) + near_weights, flops)
    return call(
        last_kernel, shape((own_rows, model)), (tile, near, got, *far_weights), flops
    )


def solution(mesh):
    placed = (
        P("ctx", "head"),
        P("ctx", "head"),
        P("ctx", "head"),
        P("head", None),
        P("ctx", None),
        P("ctx"),
    )
    return jax.shard_map(
        local, mesh=mesh, in_specs=placed, out_specs=P(("ctx", "head"), None), check_vma=False
    )
```

```python
import functools
import math

import jax
import jax.numpy as jnp
from jax import lax
from jax.experimental import pallas as pl
from jax.experimental.pallas import tpu as pltpu
from jax.sharding import PartitionSpec as P

HD = 128
REACH = 3
NEG = -1e30
FLAGS = 16
SIDE = 1024
COMMON = 1536
STATE = HD + 8
EXPONENT = math.log2(math.e) / math.sqrt(HD)
BF16, F32 = jnp.bfloat16, jnp.float32

SMEM = pl.BlockSpec(memory_space=pltpu.SMEM)
VMEM = pl.BlockSpec(memory_space=pltpu.VMEM)
HBM = pl.BlockSpec(memory_space=pltpu.HBM)


def call(
    kernel, outs, ins, flops=0, exps=0, moved=1 << 20, scratch=(), alias=None, in_hbm=(), out_hbm=False, vmem=8
):
    scalars = [x.dtype == jnp.int32 for x in ins]
    return pl.pallas_call(
        kernel,
        out_shape=outs,
        in_specs=[SMEM if s else (HBM if i in in_hbm else VMEM) for i, s in enumerate(scalars)],
        out_specs=jax.tree.map(lambda _: HBM if out_hbm else VMEM, outs),
        scratch_shapes=list(scratch),
        input_output_aliases=alias or {},
        compiler_params=pltpu.CompilerParams(vmem_limit_bytes=vmem << 20),
        cost_estimate=pl.CostEstimate(flops=flops, bytes_accessed=moved, transcendentals=exps),
    )(*ins)


def shape(dims, dtype=BF16):
    return jax.ShapeDtypeStruct(dims, dtype)


def pack_kernel(
    tile_ref, list_ref, count_ref, q_ref, k_ref, v_ref, w_ref,
    keep_q_ref, keep_kv_ref, send_ref, side_ref, sems,
):
    parity = tile_ref[0] & 1
    rows = q_ref.shape[0]
    copies = []

    def copy(source, target):
        copies.append(pltpu.make_async_copy(source, target, sems.at[len(copies)]))
        copies[-1].start()

    for head, kv_out, q_out, q_at in (
        (1 - parity, send_ref, send_ref, 2 * rows),
        (parity, keep_kv_ref, keep_q_ref, 0),
    ):
        columns = pl.ds(pl.multiple_of(head * HD, HD), HD)
        for ref, out, at in ((k_ref, kv_out, 0), (v_ref, kv_out, rows), (q_ref, q_out, q_at)):
            copy(ref.at[:, columns], out.at[pl.ds(at, rows)])
    side = side_ref.shape[1]
    copy(w_ref.at[:, pl.ds(pl.multiple_of(parity * side, HD), side)], side_ref)
    lane = lax.broadcasted_iota(jnp.int32, (FLAGS, HD), 1)
    flags = jnp.zeros((FLAGS, HD), F32)
    for offset in range(-REACH, REACH + 1):
        listed = jnp.int32(0)
        for slot in range(list_ref.shape[1]):
            found = (list_ref[0, slot] == tile_ref[0] + offset) & (slot < count_ref[0])
            listed = jnp.where(found, 1, listed)
        flags = jnp.where(lane == offset + REACH, listed.astype(F32), flags)
    keep_q_ref[rows:, :] = flags.astype(BF16)
    send_ref[3 * rows :, :] = flags.astype(BF16)
    for each in copies:
        each.wait()


def stage_kernel(keep_q_ref, keep_kv_ref, q_ref, kv_ref):
    q_ref[...] = keep_q_ref[...]
    kv_ref[...] = keep_kv_ref[...]


def cut_kernel(w_ref, common_ref, *, first):
    common_ref[...] = w_ref[:, first : first + common_ref.shape[1]]


def merge_kernel(
    tile_ref, keep_q_ref, keep_kv_ref, came_ref, flag_ref, q_ref, kv_ref, odd_ref, even_ref
):
    parity = tile_ref[0] & 1
    rows = q_ref.shape[1]
    kv_ref[...] = came_ref[0 : 2 * rows, :]
    up = (tile_ref[0] & 4) == 0

    def place(out, own):
        @pl.when(own)
        def _():
            out[...] = keep_kv_ref[...]

        @pl.when(jnp.logical_not(own))
        def _():
            out[...] = came_ref[0 : 2 * rows, :]

    place(odd_ref, up == (parity == 1))
    if even_ref is not None:
        place(even_ref, up == (parity == 0))
    q_ref[parity] = keep_q_ref[0:rows, :]
    q_ref[1 - parity] = came_ref[2 * rows : 3 * rows, :]
    own = keep_q_ref[rows:, :].astype(F32)
    other = came_ref[3 * rows :, :].astype(F32)
    even = jnp.where(parity == 0, own, other)[0:8]
    odd = jnp.where(parity == 0, other, own)[0:8]
    row = lax.broadcasted_iota(jnp.int32, (8, HD), 0)
    flag_ref[...] = jnp.where(row == 0, even, odd).astype(jnp.int32)


def step(query, key, value, state_ref, a):
    scores = lax.dot_general(
        key, query, (((1,), (1,)), ((), ())), preferred_element_type=F32
    )
    old = state_ref[a, HD : HD + 1, :]
    new = jnp.maximum(old, jnp.max(scores, axis=0, keepdims=True))
    weights = jnp.exp2((scores - new) * EXPONENT)
    shrink = jnp.exp2((old - new) * EXPONENT)
    state_ref[a, HD : HD + 1, :] = new
    state_ref[a, HD + 1 : HD + 2, :] = state_ref[a, HD + 1 : HD + 2, :] * shrink + jnp.sum(
        weights, axis=0, keepdims=True
    )
    state_ref[a, 0:HD, :] = state_ref[a, 0:HD, :] * shrink + lax.dot_general(
        value, weights.astype(BF16), (((0,), (0,)), ((), ())), preferred_element_type=F32
    )


def visit(flag_ref, q_ref, state_ref, pairs):
    rows = q_ref.shape[1]
    for a, tile, ref in pairs:

        @pl.when(flag_ref[a, tile - a + REACH] > 0)
        def _():
            step(q_ref[a], ref[0:rows, :], ref[rows : 2 * rows, :], state_ref, a)


def visit_pairs(flag_ref, tile_ref, q_ref, state_ref, tiles):
    parity = tile_ref[0] & 1
    for base, own, ref in tiles:
        tile = base + (parity if own else 1 - parity)
        visit(flag_ref, q_ref, state_ref, [(a, tile, ref) for a in range(2)])


def first_kernel(
    flag_ref, tile_ref, q_ref, own_ref, came_ref, kept_first_ref, kept_second_ref, state_ref
):
    state_ref[...] = jnp.zeros_like(state_ref)
    for a in range(2):
        state_ref[a, HD : HD + 1, :] = jnp.full((1, state_ref.shape[2]), NEG, F32)
    base = jnp.where((tile_ref[0] & 2) == 0, 2, -2)
    tiles = [(0, True, own_ref), (0, False, came_ref)]
    tiles += [(base, True, kept_first_ref), (-base, True, kept_second_ref)]
    visit_pairs(flag_ref, tile_ref, q_ref, state_ref, tiles)


def second_kernel(flag_ref, tile_ref, q_ref, first_ref, second_ref, _, state_ref):
    base = jnp.where((tile_ref[0] & 2) == 0, 2, -2)
    tiles = [(base, False, first_ref), (-base, False, second_ref)]
    visit_pairs(flag_ref, tile_ref, q_ref, state_ref, tiles)


def third_kernel(flag_ref, tile_ref, head_ref, q_ref, state_ref, *refs, far):
    outs, last = refs[far:-1], refs[-1]
    last[...] = state_ref[...]
    for i in range(far):
        above = ((tile_ref[0] & 4) == 0) == (i == 0)
        which = (jnp.where(above, 1, 0), jnp.where(above, 4, -3), refs[i])
        visit(flag_ref, q_ref, last, [which])
    parity = tile_ref[0] & 1
    core = head_ref[0] & 1
    for i, a in enumerate((parity, 1 - parity)):
        done = last[a, 0:HD, :] / last[a, HD + 1 : HD + 2, :]
        rows = done.T.astype(BF16)
        if len(outs) == 2:
            outs[i][...] = rows
        else:
            half = outs[0].shape[1]
            for chip in range(2):
                even = rows[(2 * chip) * half : (2 * chip + 1) * half]
                odd = rows[(2 * chip + 1) * half : (2 * chip + 2) * half]
                outs[2 * i][chip] = jnp.where(core == 0, even, odd)
                outs[2 * i + 1][chip] = jnp.where(core == 0, odd, even)


CHUNK = 512


def multiply(left, weights, start, stop):
    depth = weights[0].shape[0]
    return sum(
        jnp.dot(
            left[:, i * depth : (i + 1) * depth], w[:, start:stop], preferred_element_type=F32
        )
        for i, w in enumerate(weights)
    )


def send_kernel(
    tile_ref, head_ref, own_ref, y_ref, core_ref, cross_ref, w_ref, wp_ref, a_ref, far_ref
):
    parity = tile_ref[0] & 1
    chip = head_ref[0] >> 1
    deep = a_ref.shape[1]
    for out, which in ((a_ref, chip), (far_ref, 1 - chip)):
        for group, (mine, others) in enumerate(((own_ref, y_ref), (core_ref, cross_ref))):
            base = group * 2 * HD
            out[:, pl.ds(pl.multiple_of(base + parity * HD, HD), HD)] = mine[which]
            out[:, pl.ds(pl.multiple_of(base + (1 - parity) * HD, HD), HD)] = others[which]
    far = far_ref[:, 0:deep]
    term = far_ref.shape[1] - deep
    gathered = w_ref.shape[1] - term
    for start in range(0, term, CHUNK):
        stop = min(start + CHUNK, term)
        far_ref[:, deep + start : deep + stop] = multiply(
            far, (w_ref, wp_ref), gathered + start, gathered + stop
        ).astype(BF16)


def near_kernel(a_ref, w_ref, wp_ref, near_ref):
    own = a_ref[...]
    for start in range(0, w_ref.shape[1], CHUNK):
        near_ref[:, start : start + CHUNK] = multiply(own, (w_ref, wp_ref), start, start + CHUNK)


def last_kernel(tile_ref, near_ref, far_ref, *refs):
    weights, out_ref = refs[:-1], refs[-1]
    parity = tile_ref[0] & 1
    deep = 2 * weights[0].shape[0]
    far = far_ref[:, 0:deep]
    side = weights[0].shape[1]
    for i, first in enumerate((parity * side, (1 - parity) * side, 2 * side)):
        pair = weights[2 * i : 2 * i + 2]
        for start in range(0, pair[0].shape[1], CHUNK):
            stop = min(start + CHUNK, pair[0].shape[1])
            columns = pl.ds(pl.multiple_of(first + start, HD), stop - start)
            out_ref[:, columns] = (
                near_ref[:, columns] + multiply(far, pair, start, stop)
            ).astype(BF16)
    gathered = 2 * side + weights[4].shape[1]
    out_ref[:, gathered:] = (near_ref[:, gathered:] + far_ref[:, deep:].astype(F32)).astype(BF16)


def swap_pairs(value, distance, phase):
    count = lax.axis_size("ctx")
    pairs = []
    for i in range(count - 2 * distance):
        if (i // 2 // distance) % 2 == phase:
            pairs += [(i, i + 2 * distance), (i + 2 * distance, i)]
    return lax.ppermute(value, "ctx", pairs)


def swap_tiles(value):
    return lax.ppermute(value, "ctx", [(i, i ^ 1) for i in range(lax.axis_size("ctx"))])


def swap_cores(value):
    return lax.ppermute(value, "head", [(i, i ^ 1) for i in range(lax.axis_size("head"))])


def swap_both(value):
    heads = lax.axis_size("head")
    count = lax.axis_size("ctx") * heads
    pairs = [(i, ((i // heads) ^ 1) * heads + ((i % heads) ^ 1)) for i in range(count)]
    return lax.ppermute(value, ("ctx", "head"), pairs)


def from_chip(value, steps):
    count = lax.axis_size("head")
    return lax.ppermute(value, "head", [((i + 2 * steps) % count, i) for i in range(count)])


def project_any(attended, out_weight, weight_pair, head_index):
    rows, width = attended.shape
    n_head = lax.axis_size("head")
    chips, own_rows = n_head // 2, rows // n_head
    chip, core = head_index // 2, head_index % 2
    blocks = attended.reshape(chips, 2, own_rows, width)
    mine = lax.dynamic_index_in_dim(blocks, core, 1, keepdims=False)
    theirs = lax.dynamic_index_in_dim(blocks, 1 - core, 1, keepdims=False)
    joined = jnp.concatenate([mine, swap_cores(theirs)], axis=2)

    def project(steps):
        block = lax.dynamic_index_in_dim(joined, (chip - steps) % chips, 0, keepdims=False)
        return multiply(block, (out_weight, weight_pair), 0, out_weight.shape[1])

    total = project(0)
    for steps in range(1, chips):
        total = total + from_chip(project(steps).astype(BF16), steps).astype(F32)
    return total.astype(BF16)


def local(queries, keys, values, out_weight, neighbours, counts):
    rows, width = queries.shape
    n_head = lax.axis_size("head")
    own_rows = rows // n_head
    model = out_weight.shape[1]
    small = n_head == 4 and own_rows % 16 == 0
    head_index = lax.axis_index("head").astype(jnp.int32)
    head = head_index.reshape(1)
    tile = lax.axis_index("ctx").astype(jnp.int32).reshape(1)

    one = (rows, HD)
    payload, kv_shape = shape((3 * rows + FLAGS, HD)), shape((2 * rows, HD))
    keep_q, keep_kv, send, side_weight = call(
        pack_kernel,
        (shape((rows + FLAGS, HD)), kv_shape, payload, shape((width, SIDE))),
        (tile, neighbours, counts, queries, keys, values, out_weight),
        scratch=(pltpu.SemaphoreType.DMA((7,)),),
        in_hbm=(3, 4, 5, 6),
        vmem=58,
    )
    weight_ready, _ = lax.optimization_barrier((out_weight, keep_kv))
    weight_pair = swap_cores(weight_ready)
    came = swap_tiles(send)
    kept_near = [swap_pairs(keep_kv, 1, phase) for phase in range(2)]
    if small:
        side_own = from_chip(side_weight, 1)

    held_q, held_kv = call(stage_kernel, (shape((rows + FLAGS, HD)), kv_shape), (keep_q, keep_kv))
    came, weight_pair, held_q, held_kv, *kept_near = lax.optimization_barrier(
        (came, weight_pair, held_q, held_kv, *kept_near)
    )
    far = 1 if lax.axis_size("ctx") <= 8 else 2
    flags, q_pair, came_kv, *to_far = call(
        merge_kernel if far == 2 else functools.partial(merge_kernel, even_ref=None),
        (shape((8, HD), jnp.int32), shape((2,) + one), kv_shape) + (kv_shape,) * far,
        (tile, held_q, held_kv, came),
    )
    came_near = [swap_pairs(came_kv, 1, phase) for phase in range(2)]
    farther = [swap_pairs(to_far[i], 2, i) for i in range(far)]

    state = shape((2, STATE, rows), F32)
    area = rows * rows
    held = call(
        first_kernel,
        state,
        (flags, tile, q_pair, held_kv, came_kv, *kept_near),
        32 * area * HD,
        8 * area,
    )
    q_again = q_pair
    if small:
        side_own, q_again = lax.optimization_barrier((side_own, q_pair))
        side_other = swap_tiles(side_own)
        ready, _ = lax.optimization_barrier((out_weight, side_own))
        common_weight = call(
            functools.partial(cut_kernel, first=2 * SIDE), shape((width, COMMON)), (ready,)
        )
        common = from_chip(common_weight, 1)
    held = call(
        second_kernel,
        state,
        (flags, tile, q_again, *came_near, held),
        16 * area * HD,
        4 * area,
        alias={5: 0},
    )
    if small:
        held, side_other = lax.optimization_barrier((held, side_other))
    block = (2, own_rows, HD)
    attended = call(
        functools.partial(third_kernel, far=far),
        (shape(block),) * 4 if small else (shape(one),) * 2,
        (flags, tile, head, q_pair, held, *farther),
        4 * area * HD,
        area,
        scratch=(pltpu.VMEM(state.shape, F32),),
    )
    if not small:
        mine, theirs = attended
        got = swap_tiles(theirs)
        even_tile = tile[0] % 2 == 0
        joined = jnp.concatenate(
            [jnp.where(even_tile, mine, got), jnp.where(even_tile, got, mine)], axis=1
        )
        return project_any(joined, out_weight, weight_pair, head_index)

    mine, mine_other, theirs, theirs_other = attended
    from_cross = swap_both(theirs_other)
    from_y = swap_tiles(theirs)
    from_core = swap_cores(mine_other)
    from_cross, from_y, from_core, common = lax.optimization_barrier(
        (from_cross, from_y, from_core, common)
    )

    flops = 2 * own_rows * 2 * width * model
    near_weights = (out_weight, weight_pair)
    deep, gathered = 2 * width, 2 * SIDE + COMMON
    own_a, far_a = call(
        send_kernel,
        (shape((own_rows, deep)), shape((own_rows, deep + model - gathered))),
        (tile, head, mine, from_y, from_core, from_cross) + near_weights,
        flops // 4,
        vmem=16,
    )
    got = from_chip(far_a, 1)
    pieces = [side_own, side_other, common]
    *ready, _ = lax.optimization_barrier((*pieces, own_a))
    far_weights = [each for piece, to in zip(pieces, ready) for each in (piece, swap_cores(to))]
    near = call(near_kernel, shape((own_rows, model), F32), (own_a,) + near_weights, flops, vmem=16)
    return call(
        last_kernel, shape((own_rows, model)), (tile, near, got, *far_weights), flops, vmem=20
    )


def solution(mesh):
    placed = (
        P("ctx", "head"),
        P("ctx", "head"),
        P("ctx", "head"),
        P("head", None),
        P("ctx", None),
        P("ctx"),
    )
    return jax.shard_map(
        local, mesh=mesh, in_specs=placed, out_specs=P(("ctx", "head"), None), check_vma=False
    )
```

```python
import functools
import math

import jax
import jax.numpy as jnp
from jax import lax
from jax.experimental import pallas as pl
from jax.experimental.pallas import tpu as pltpu
from jax.sharding import PartitionSpec as P

HD = 128
REACH = 3
NEG = -1e30
FLAGS = 16
SIDE = 1024
COMMON = 1536
STATE = HD + 8
EXPONENT = math.log2(math.e) / math.sqrt(HD)
BF16, F32 = jnp.bfloat16, jnp.float32

SMEM = pl.BlockSpec(memory_space=pltpu.SMEM)
VMEM = pl.BlockSpec(memory_space=pltpu.VMEM)
HBM = pl.BlockSpec(memory_space=pltpu.HBM)


def call(
    kernel, outs, ins, flops=0, exps=0, moved=1 << 20, scratch=(), alias=None, in_hbm=(), out_hbm=False, vmem=8
):
    scalars = [x.dtype == jnp.int32 for x in ins]
    return pl.pallas_call(
        kernel,
        out_shape=outs,
        in_specs=[SMEM if s else (HBM if i in in_hbm else VMEM) for i, s in enumerate(scalars)],
        out_specs=jax.tree.map(lambda _: HBM if out_hbm else VMEM, outs),
        scratch_shapes=list(scratch),
        input_output_aliases=alias or {},
        compiler_params=pltpu.CompilerParams(vmem_limit_bytes=vmem << 20),
        cost_estimate=pl.CostEstimate(flops=flops, bytes_accessed=moved, transcendentals=exps),
    )(*ins)


def shape(dims, dtype=BF16):
    return jax.ShapeDtypeStruct(dims, dtype)


def pack_kernel(
    index_ref, list_ref, count_ref, q_ref, k_ref, v_ref, w_ref,
    keep_q_ref, keep_kv_ref, send_ref, side_ref, sems,
):
    parity = index_ref[0] & 1
    rows = q_ref.shape[0]
    copies = []

    def copy(source, target):
        copies.append(pltpu.make_async_copy(source, target, sems.at[len(copies)]))
        copies[-1].start()

    for head, kv_out, q_out, q_at in (
        (1 - parity, send_ref, send_ref, 2 * rows),
        (parity, keep_kv_ref, keep_q_ref, 0),
    ):
        columns = pl.ds(pl.multiple_of(head * HD, HD), HD)
        for ref, out, at in ((k_ref, kv_out, 0), (v_ref, kv_out, rows), (q_ref, q_out, q_at)):
            copy(ref.at[:, columns], out.at[pl.ds(at, rows)])
    side = side_ref.shape[1]
    copy(w_ref.at[:, pl.ds(pl.multiple_of(parity * side, HD), side)], side_ref)
    lane = lax.broadcasted_iota(jnp.int32, (FLAGS, HD), 1)
    flags = jnp.zeros((FLAGS, HD), F32)
    for offset in range(-REACH, REACH + 1):
        listed = jnp.int32(0)
        for slot in range(list_ref.shape[1]):
            found = (list_ref[0, slot] == index_ref[0] + offset) & (slot < count_ref[0])
            listed = jnp.where(found, 1, listed)
        flags = jnp.where(lane == offset + REACH, listed.astype(F32), flags)
    keep_q_ref[rows:, :] = flags.astype(BF16)
    send_ref[3 * rows :, :] = flags.astype(BF16)
    for each in copies:
        each.wait()


def stage_kernel(keep_q_ref, keep_kv_ref, q_ref, kv_ref):
    q_ref[...] = keep_q_ref[...]
    kv_ref[...] = keep_kv_ref[...]


def cut_kernel(w_ref, common_ref, *, first):
    common_ref[...] = w_ref[:, first : first + common_ref.shape[1]]


def merge_kernel(
    index_ref, keep_q_ref, keep_kv_ref, came_ref, flag_ref, q_ref, kv_ref, odd_ref, even_ref
):
    parity = index_ref[0] & 1
    rows = q_ref.shape[1]
    kv_ref[...] = came_ref[0 : 2 * rows, :]
    up = (index_ref[0] & 4) == 0

    def place(out, own):
        @pl.when(own)
        def _():
            out[...] = keep_kv_ref[...]

        @pl.when(jnp.logical_not(own))
        def _():
            out[...] = came_ref[0 : 2 * rows, :]

    place(odd_ref, up == (parity == 1))
    if even_ref is not None:
        place(even_ref, up == (parity == 0))
    q_ref[parity] = keep_q_ref[0:rows, :]
    q_ref[1 - parity] = came_ref[2 * rows : 3 * rows, :]
    own = keep_q_ref[rows:, :].astype(F32)
    other = came_ref[3 * rows :, :].astype(F32)
    even = jnp.where(parity == 0, own, other)[0:8]
    odd = jnp.where(parity == 0, other, own)[0:8]
    row = lax.broadcasted_iota(jnp.int32, (8, HD), 0)
    flag_ref[...] = jnp.where(row == 0, even, odd).astype(jnp.int32)


def step(query, key, value, state_ref, a):
    scores = lax.dot_general(
        key, query, (((1,), (1,)), ((), ())), preferred_element_type=F32
    )
    old = state_ref[a, HD : HD + 1, :]
    new = jnp.maximum(old, jnp.max(scores, axis=0, keepdims=True))
    weights = jnp.exp2((scores - new) * EXPONENT)
    shrink = jnp.exp2((old - new) * EXPONENT)
    state_ref[a, HD : HD + 1, :] = new
    state_ref[a, HD + 1 : HD + 2, :] = state_ref[a, HD + 1 : HD + 2, :] * shrink + jnp.sum(
        weights, axis=0, keepdims=True
    )
    state_ref[a, 0:HD, :] = state_ref[a, 0:HD, :] * shrink + lax.dot_general(
        value, weights.astype(BF16), (((0,), (0,)), ((), ())), preferred_element_type=F32
    )


def visit(flag_ref, q_ref, state_ref, pairs):
    rows = q_ref.shape[1]
    for a, tile, ref in pairs:

        @pl.when(flag_ref[a, tile - a + REACH] > 0)
        def _():
            step(q_ref[a], ref[0:rows, :], ref[rows : 2 * rows, :], state_ref, a)


def visit_pairs(flag_ref, index_ref, q_ref, state_ref, tiles):
    parity = index_ref[0] & 1
    for base, own, ref in tiles:
        tile = base + (parity if own else 1 - parity)
        visit(flag_ref, q_ref, state_ref, [(a, tile, ref) for a in range(2)])


def first_kernel(
    flag_ref, index_ref, q_ref, own_ref, came_ref, kept_first_ref, kept_second_ref, state_ref
):
    state_ref[...] = jnp.zeros_like(state_ref)
    for a in range(2):
        state_ref[a, HD : HD + 1, :] = jnp.full((1, state_ref.shape[2]), NEG, F32)
    base = jnp.where((index_ref[0] & 2) == 0, 2, -2)
    tiles = [(0, True, own_ref), (0, False, came_ref)]
    tiles += [(base, True, kept_first_ref), (-base, True, kept_second_ref)]
    visit_pairs(flag_ref, index_ref, q_ref, state_ref, tiles)


def second_kernel(flag_ref, index_ref, q_ref, first_ref, second_ref, _, state_ref):
    base = jnp.where((index_ref[0] & 2) == 0, 2, -2)
    tiles = [(base, False, first_ref), (-base, False, second_ref)]
    visit_pairs(flag_ref, index_ref, q_ref, state_ref, tiles)


def third_kernel(flag_ref, index_ref, q_ref, state_ref, *refs, far):
    outs, last = refs[far:-1], refs[-1]
    last[...] = state_ref[...]
    for i in range(far):
        above = ((index_ref[0] & 4) == 0) == (i == 0)
        which = (jnp.where(above, 1, 0), jnp.where(above, 4, -3), refs[i])
        visit(flag_ref, q_ref, last, [which])
    parity = index_ref[0] & 1
    core = index_ref[1] & 1
    for i, a in enumerate((parity, 1 - parity)):
        done = last[a, 0:HD, :] / last[a, HD + 1 : HD + 2, :]
        rows = done.T.astype(BF16)
        if len(outs) == 2:
            outs[i][...] = rows
        else:
            half = outs[0].shape[1]
            for chip in range(2):
                even = rows[(2 * chip) * half : (2 * chip + 1) * half]
                odd = rows[(2 * chip + 1) * half : (2 * chip + 2) * half]
                outs[2 * i][chip] = jnp.where(core == 0, even, odd)
                outs[2 * i + 1][chip] = jnp.where(core == 0, odd, even)


CHUNK = 512


def multiply(left, weights, start, stop):
    depth = weights[0].shape[0]
    return sum(
        jnp.dot(
            left[:, i * depth : (i + 1) * depth], w[:, start:stop], preferred_element_type=F32
        )
        for i, w in enumerate(weights)
    )


def send_kernel(
    index_ref, own_ref, y_ref, core_ref, cross_ref, w_ref, wp_ref, a_ref, far_ref
):
    parity = index_ref[0] & 1
    chip = index_ref[1] >> 1
    deep = a_ref.shape[1]
    for out, which in ((a_ref, chip), (far_ref, 1 - chip)):
        for group, (mine, others) in enumerate(((own_ref, y_ref), (core_ref, cross_ref))):
            base = group * 2 * HD
            out[:, pl.ds(pl.multiple_of(base + parity * HD, HD), HD)] = mine[which]
            out[:, pl.ds(pl.multiple_of(base + (1 - parity) * HD, HD), HD)] = others[which]
    far = far_ref[:, 0:deep]
    term = far_ref.shape[1] - deep
    gathered = w_ref.shape[1] - term
    for start in range(0, term, CHUNK):
        stop = min(start + CHUNK, term)
        far_ref[:, deep + start : deep + stop] = multiply(
            far, (w_ref, wp_ref), gathered + start, gathered + stop
        ).astype(BF16)


def near_kernel(a_ref, w_ref, wp_ref, near_ref):
    own = a_ref[...]
    for start in range(0, w_ref.shape[1], CHUNK):
        near_ref[:, start : start + CHUNK] = multiply(own, (w_ref, wp_ref), start, start + CHUNK)


def last_kernel(index_ref, near_ref, far_ref, *refs):
    weights, out_ref = refs[:-1], refs[-1]
    parity = index_ref[0] & 1
    deep = 2 * weights[0].shape[0]
    far = far_ref[:, 0:deep]
    side = weights[0].shape[1]
    for i, first in enumerate((parity * side, (1 - parity) * side, 2 * side)):
        pair = weights[2 * i : 2 * i + 2]
        for start in range(0, pair[0].shape[1], CHUNK):
            stop = min(start + CHUNK, pair[0].shape[1])
            columns = pl.ds(pl.multiple_of(first + start, HD), stop - start)
            out_ref[:, columns] = (
                near_ref[:, columns] + multiply(far, pair, start, stop)
            ).astype(BF16)
    gathered = 2 * side + weights[4].shape[1]
    out_ref[:, gathered:] = (near_ref[:, gathered:] + far_ref[:, deep:].astype(F32)).astype(BF16)


def swap_pairs(value, distance, phase):
    count = lax.axis_size("ctx")
    pairs = []
    for i in range(count - 2 * distance):
        if (i // 2 // distance) % 2 == phase:
            pairs += [(i, i + 2 * distance), (i + 2 * distance, i)]
    return lax.ppermute(value, "ctx", pairs)


def swap_tiles(value):
    return lax.ppermute(value, "ctx", [(i, i ^ 1) for i in range(lax.axis_size("ctx"))])


def swap_cores(value):
    return lax.ppermute(value, "head", [(i, i ^ 1) for i in range(lax.axis_size("head"))])


def swap_both(value):
    heads = lax.axis_size("head")
    count = lax.axis_size("ctx") * heads
    pairs = [(i, ((i // heads) ^ 1) * heads + ((i % heads) ^ 1)) for i in range(count)]
    return lax.ppermute(value, ("ctx", "head"), pairs)


def from_chip(value, steps):
    count = lax.axis_size("head")
    return lax.ppermute(value, "head", [((i + 2 * steps) % count, i) for i in range(count)])


def project_any(attended, out_weight, weight_pair, head_index):
    rows, width = attended.shape
    n_head = lax.axis_size("head")
    chips, own_rows = n_head // 2, rows // n_head
    chip, core = head_index // 2, head_index % 2
    blocks = attended.reshape(chips, 2, own_rows, width)
    mine = lax.dynamic_index_in_dim(blocks, core, 1, keepdims=False)
    theirs = lax.dynamic_index_in_dim(blocks, 1 - core, 1, keepdims=False)
    joined = jnp.concatenate([mine, swap_cores(theirs)], axis=2)

    def project(steps):
        block = lax.dynamic_index_in_dim(joined, (chip - steps) % chips, 0, keepdims=False)
        return multiply(block, (out_weight, weight_pair), 0, out_weight.shape[1])

    total = project(0)
    for steps in range(1, chips):
        total = total + from_chip(project(steps).astype(BF16), steps).astype(F32)
    return total.astype(BF16)


def local(queries, keys, values, out_weight, neighbours, counts):
    rows, width = queries.shape
    n_head = lax.axis_size("head")
    own_rows = rows // n_head
    model = out_weight.shape[1]
    small = n_head == 4 and own_rows % 16 == 0
    head_index = lax.axis_index("head").astype(jnp.int32)
    index = jnp.stack([lax.axis_index("ctx").astype(jnp.int32), head_index])

    one = (rows, HD)
    payload, kv_shape = shape((3 * rows + FLAGS, HD)), shape((2 * rows, HD))
    keep_q, keep_kv, send, side_weight = call(
        pack_kernel,
        (shape((rows + FLAGS, HD)), kv_shape, payload, shape((width, SIDE))),
        (index, neighbours, counts, queries, keys, values, out_weight),
        scratch=(pltpu.SemaphoreType.DMA((7,)),),
        in_hbm=(3, 4, 5, 6),
        vmem=58,
    )
    weight_ready, _ = lax.optimization_barrier((out_weight, keep_kv))
    weight_pair = swap_cores(weight_ready)
    came = swap_tiles(send)
    kept_near = [swap_pairs(keep_kv, 1, phase) for phase in range(2)]
    if small:
        side_own = from_chip(side_weight, 1)

    held_q, held_kv = call(stage_kernel, (shape((rows + FLAGS, HD)), kv_shape), (keep_q, keep_kv))
    cut = []
    if small:
        ready, _ = lax.optimization_barrier((out_weight, held_q))
        cut.append(
            call(functools.partial(cut_kernel, first=2 * SIDE), shape((width, COMMON)), (ready,))
        )
    came, weight_pair, held_q, held_kv, kept_near, cut = lax.optimization_barrier(
        (came, weight_pair, held_q, held_kv, kept_near, cut)
    )
    far = 1 if lax.axis_size("ctx") <= 8 else 2
    flags, q_pair, came_kv, *to_far = call(
        merge_kernel if far == 2 else functools.partial(merge_kernel, even_ref=None),
        (shape((8, HD), jnp.int32), shape((2,) + one), kv_shape) + (kv_shape,) * far,
        (index, held_q, held_kv, came),
    )
    came_near = [swap_pairs(came_kv, 1, phase) for phase in range(2)]
    farther = [swap_pairs(to_far[i], 2, i) for i in range(far)]

    state = shape((2, STATE, rows), F32)
    area = rows * rows
    held = call(
        first_kernel,
        state,
        (flags, index, q_pair, held_kv, came_kv, *kept_near),
        32 * area * HD,
        8 * area,
    )
    q_again = q_pair
    if small:
        side_own, q_again = lax.optimization_barrier((side_own, q_pair))
        side_other = swap_tiles(side_own)
        ready, _ = lax.optimization_barrier((cut[0], side_own))
        common = from_chip(ready, 1)
    held = call(
        second_kernel,
        state,
        (flags, index, q_again, *came_near, held),
        16 * area * HD,
        4 * area,
        alias={5: 0},
    )
    if small:
        held, side_other = lax.optimization_barrier((held, side_other))
    block = (2, own_rows, HD)
    attended = call(
        functools.partial(third_kernel, far=far),
        (shape(block),) * 4 if small else (shape(one),) * 2,
        (flags, index, q_pair, held, *farther),
        4 * area * HD,
        area,
        scratch=(pltpu.VMEM(state.shape, F32),),
    )
    if not small:
        mine, theirs = attended
        got = swap_tiles(theirs)
        even_tile = index[0] % 2 == 0
        joined = jnp.concatenate(
            [jnp.where(even_tile, mine, got), jnp.where(even_tile, got, mine)], axis=1
        )
        return project_any(joined, out_weight, weight_pair, head_index)

    mine, mine_other, theirs, theirs_other = attended
    from_cross = swap_both(theirs_other)
    from_y = swap_tiles(theirs)
    from_core = swap_cores(mine_other)
    from_cross, from_y, from_core, common = lax.optimization_barrier(
        (from_cross, from_y, from_core, common)
    )

    flops = 2 * own_rows * 2 * width * model
    near_weights = (out_weight, weight_pair)
    deep, gathered = 2 * width, 2 * SIDE + COMMON
    own_a, far_a = call(
        send_kernel,
        (shape((own_rows, deep)), shape((own_rows, deep + model - gathered))),
        (index, mine, from_y, from_core, from_cross) + near_weights,
        flops // 4,
        vmem=16,
    )
    got = from_chip(far_a, 1)
    pieces = [side_own, side_other, common]
    *ready, _ = lax.optimization_barrier((*pieces, own_a))
    far_weights = [each for piece, to in zip(pieces, ready) for each in (piece, swap_cores(to))]
    near = call(near_kernel, shape((own_rows, model), F32), (own_a,) + near_weights, flops, vmem=16)
    return call(
        last_kernel, shape((own_rows, model)), (index, near, got, *far_weights), flops, vmem=20
    )


def solution(mesh):
    placed = (
        P("ctx", "head"),
        P("ctx", "head"),
        P("ctx", "head"),
        P("head", None),
        P("ctx", None),
        P("ctx"),
    )
    return jax.shard_map(
        local, mesh=mesh, in_specs=placed, out_specs=P(("ctx", "head"), None), check_vma=False
    )
```

```python
import functools
import math

import jax
import jax.numpy as jnp
from jax import lax
from jax.experimental import pallas as pl
from jax.experimental.pallas import tpu as pltpu
from jax.sharding import PartitionSpec as P

HD = 128
REACH = 3
NEG = -1e30
MERGE = 0
FLAGS = 16
SIDE = 1024
COMMON = 1408
STATE = HD + 8
EXPONENT = math.log2(math.e) / math.sqrt(HD)
BF16, F32 = jnp.bfloat16, jnp.float32

SMEM = pl.BlockSpec(memory_space=pltpu.SMEM)
VMEM = pl.BlockSpec(memory_space=pltpu.VMEM)
HBM = pl.BlockSpec(memory_space=pltpu.HBM)


def call(
    kernel, outs, ins, flops=0, exps=0, moved=1 << 20, scratch=(), alias=None, in_hbm=(), out_hbm=False, vmem=8
):
    scalars = [x.dtype == jnp.int32 for x in ins]
    return pl.pallas_call(
        kernel,
        out_shape=outs,
        in_specs=[SMEM if s else (HBM if i in in_hbm else VMEM) for i, s in enumerate(scalars)],
        out_specs=jax.tree.map(lambda _: HBM if out_hbm else VMEM, outs),
        scratch_shapes=list(scratch),
        input_output_aliases=alias or {},
        compiler_params=pltpu.CompilerParams(vmem_limit_bytes=vmem << 20),
        cost_estimate=pl.CostEstimate(flops=flops, bytes_accessed=moved, transcendentals=exps),
    )(*ins)


def shape(dims, dtype=BF16):
    return jax.ShapeDtypeStruct(dims, dtype)


def pack_kernel(
    tile_ref, _, list_ref, count_ref, q_ref, k_ref, v_ref, w_ref,
    keep_q_ref, keep_kv_ref, send_ref, side_ref, sems,
):
    parity = tile_ref[0] & 1
    rows = q_ref.shape[0]
    copies = []

    def copy(source, target):
        copies.append(pltpu.make_async_copy(source, target, sems.at[len(copies)]))
        copies[-1].start()

    for head, kv_out, q_out, q_at in (
        (1 - parity, send_ref, send_ref, 2 * rows),
        (parity, keep_kv_ref, keep_q_ref, 0),
    ):
        columns = pl.ds(pl.multiple_of(head * HD, HD), HD)
        for ref, out, at in ((k_ref, kv_out, 0), (v_ref, kv_out, rows), (q_ref, q_out, q_at)):
            copy(ref.at[:, columns], out.at[pl.ds(at, rows)])
    side = side_ref.shape[1]
    copy(w_ref.at[:, pl.ds(pl.multiple_of(parity * side, HD), side)], side_ref)
    lane = lax.broadcasted_iota(jnp.int32, (FLAGS, HD), 1)
    flags = jnp.zeros((FLAGS, HD), F32)
    for offset in range(-REACH, REACH + 1):
        listed = jnp.int32(0)
        for slot in range(list_ref.shape[1]):
            found = (list_ref[0, slot] == tile_ref[0] + offset) & (slot < count_ref[0, 0])
            listed = jnp.where(found, 1, listed)
        flags = jnp.where(lane == offset + REACH, listed.astype(F32), flags)
    keep_q_ref[rows:, :] = flags.astype(BF16)
    send_ref[3 * rows :, :] = flags.astype(BF16)
    for each in copies:
        each.wait()


def stage_kernel(keep_q_ref, keep_kv_ref, q_ref, kv_ref):
    q_ref[...] = keep_q_ref[...]
    kv_ref[...] = keep_kv_ref[...]


def cut_kernel(w_ref, common_ref, *, first):
    common_ref[...] = w_ref[:, first : first + common_ref.shape[1]]


def merge_kernel(
    tile_ref, keep_q_ref, keep_kv_ref, came_ref, flag_ref, q_ref, kv_ref, odd_ref, even_ref
):
    parity = tile_ref[0] & 1
    rows = q_ref.shape[1]
    kv_ref[...] = came_ref[0 : 2 * rows, :]
    up = (tile_ref[0] & 4) == 0

    def place(out, own):
        @pl.when(own)
        def _():
            out[...] = keep_kv_ref[...]

        @pl.when(jnp.logical_not(own))
        def _():
            out[...] = came_ref[0 : 2 * rows, :]

    place(odd_ref, up == (parity == 1))
    if even_ref is not None:
        place(even_ref, up == (parity == 0))
    q_ref[parity] = keep_q_ref[0:rows, :]
    q_ref[1 - parity] = came_ref[2 * rows : 3 * rows, :]
    own = keep_q_ref[rows:, :].astype(F32)
    other = came_ref[3 * rows :, :].astype(F32)
    even = jnp.where(parity == 0, own, other)[0:8]
    odd = jnp.where(parity == 0, other, own)[0:8]
    row = lax.broadcasted_iota(jnp.int32, (8, HD), 0)
    flag_ref[...] = jnp.where(row == 0, even, odd).astype(jnp.int32)


def step(query, key, value, state_ref, a):
    scores = lax.dot_general(
        key, query, (((1,), (1,)), ((), ())), preferred_element_type=F32
    )
    old = state_ref[a, HD : HD + 1, :]
    new = jnp.maximum(old, jnp.max(scores, axis=0, keepdims=True))
    weights = jnp.exp2((scores - new) * EXPONENT)
    shrink = jnp.exp2((old - new) * EXPONENT)
    state_ref[a, HD : HD + 1, :] = new
    state_ref[a, HD + 1 : HD + 2, :] = state_ref[a, HD + 1 : HD + 2, :] * shrink + jnp.sum(
        weights, axis=0, keepdims=True
    )
    state_ref[a, 0:HD, :] = state_ref[a, 0:HD, :] * shrink + lax.dot_general(
        value, weights.astype(BF16), (((0,), (0,)), ((), ())), preferred_element_type=F32
    )


def visit(flag_ref, q_ref, state_ref, pairs):
    rows = q_ref.shape[1]
    for a, tile, ref in pairs:

        @pl.when(flag_ref[a, tile - a + REACH] > 0)
        def _():
            step(q_ref[a], ref[0:rows, :], ref[rows : 2 * rows, :], state_ref, a)


def visit_pairs(flag_ref, tile_ref, q_ref, state_ref, tiles):
    parity = tile_ref[0] & 1
    for base, own, ref in tiles:
        tile = base + (parity if own else 1 - parity)
        visit(flag_ref, q_ref, state_ref, [(a, tile, ref) for a in range(2)])


def first_kernel(
    flag_ref, tile_ref, q_ref, own_ref, came_ref, kept_first_ref, kept_second_ref, state_ref
):
    state_ref[...] = jnp.zeros_like(state_ref)
    for a in range(2):
        state_ref[a, HD : HD + 1, :] = jnp.full((1, state_ref.shape[2]), NEG, F32)
    base = jnp.where((tile_ref[0] & 2) == 0, 2, -2)
    tiles = [(0, True, own_ref), (0, False, came_ref)]
    tiles += [(base, True, kept_first_ref), (-base, True, kept_second_ref)]
    visit_pairs(flag_ref, tile_ref, q_ref, state_ref, tiles)


def second_kernel(flag_ref, tile_ref, q_ref, first_ref, second_ref, _, state_ref):
    base = jnp.where((tile_ref[0] & 2) == 0, 2, -2)
    tiles = [(base, False, first_ref), (-base, False, second_ref)]
    visit_pairs(flag_ref, tile_ref, q_ref, state_ref, tiles)


def third_kernel(flag_ref, tile_ref, head_ref, q_ref, state_ref, *refs, far):
    outs, last = refs[far:-1], refs[-1]
    last[...] = state_ref[...]
    for i in range(far):
        above = ((tile_ref[0] & 4) == 0) == (i == 0)
        which = (jnp.where(above, 1, 0), jnp.where(above, 4, -3), refs[i])
        visit(flag_ref, q_ref, last, [which])
    parity = tile_ref[0] & 1
    core = head_ref[0] & 1
    for i, a in enumerate((parity, 1 - parity)):
        done = last[a, 0:HD, :] / last[a, HD + 1 : HD + 2, :]
        rows = done.T.astype(BF16)
        if len(outs) == 2:
            outs[i][...] = rows
        else:
            half = outs[0].shape[1]
            for chip in range(2):
                even = rows[(2 * chip) * half : (2 * chip + 1) * half]
                odd = rows[(2 * chip + 1) * half : (2 * chip + 2) * half]
                outs[2 * i][chip] = jnp.where(core == 0, even, odd)
                outs[2 * i + 1][chip] = jnp.where(core == 0, odd, even)


CHUNK = 512


def multiply(left, weights, start, stop):
    depth = weights[0].shape[0]
    return sum(
        jnp.dot(
            left[:, i * depth : (i + 1) * depth], w[:, start:stop], preferred_element_type=F32
        )
        for i, w in enumerate(weights)
    )


def send_kernel(
    tile_ref, head_ref, own_ref, y_ref, core_ref, cross_ref, w_ref, wp_ref, a_ref, far_ref
):
    parity = tile_ref[0] & 1
    chip = head_ref[0] >> 1
    deep = a_ref.shape[1]
    for out, which in ((a_ref, chip), (far_ref, 1 - chip)):
        for group, (mine, others) in enumerate(((own_ref, y_ref), (core_ref, cross_ref))):
            base = group * 2 * HD
            out[:, pl.ds(pl.multiple_of(base + parity * HD, HD), HD)] = mine[which]
            out[:, pl.ds(pl.multiple_of(base + (1 - parity) * HD, HD), HD)] = others[which]
    far = far_ref[:, 0:deep]
    term = far_ref.shape[1] - deep
    gathered = w_ref.shape[1] - term
    for start in range(0, term, CHUNK):
        stop = min(start + CHUNK, term)
        far_ref[:, deep + start : deep + stop] = multiply(
            far, (w_ref, wp_ref), gathered + start, gathered + stop
        ).astype(BF16)


def near_kernel(a_ref, w_ref, wp_ref, near_ref):
    own = a_ref[...]
    for start in range(0, w_ref.shape[1], CHUNK):
        near_ref[:, start : start + CHUNK] = multiply(own, (w_ref, wp_ref), start, start + CHUNK)


def last_kernel(tile_ref, near_ref, far_ref, *refs):
    weights, out_ref = refs[:-1], refs[-1]
    parity = tile_ref[0] & 1
    deep = 2 * weights[0].shape[0]
    far = far_ref[:, 0:deep]
    side = weights[0].shape[1]
    for i, first in enumerate((parity * side, (1 - parity) * side, 2 * side)):
        pair = weights[2 * i : 2 * i + 2]
        for start in range(0, pair[0].shape[1], CHUNK):
            stop = min(start + CHUNK, pair[0].shape[1])
            columns = pl.ds(pl.multiple_of(first + start, HD), stop - start)
            out_ref[:, columns] = (
                near_ref[:, columns] + multiply(far, pair, start, stop)
            ).astype(BF16)
    gathered = 2 * side + weights[4].shape[1]
    out_ref[:, gathered:] = (near_ref[:, gathered:] + far_ref[:, deep:].astype(F32)).astype(BF16)


def swap_pairs(value, distance, phase):
    count = lax.axis_size("ctx")
    pairs = []
    for i in range(count - 2 * distance):
        if (i // 2 // distance) % 2 == phase:
            pairs += [(i, i + 2 * distance), (i + 2 * distance, i)]
    return lax.ppermute(value, "ctx", pairs)


def swap_tiles(value):
    return lax.ppermute(value, "ctx", [(i, i ^ 1) for i in range(lax.axis_size("ctx"))])


def swap_cores(value):
    return lax.ppermute(value, "head", [(i, i ^ 1) for i in range(lax.axis_size("head"))])


def swap_both(value):
    heads = lax.axis_size("head")
    count = lax.axis_size("ctx") * heads
    pairs = [(i, ((i // heads) ^ 1) * heads + ((i % heads) ^ 1)) for i in range(count)]
    return lax.ppermute(value, ("ctx", "head"), pairs)


def from_chip(value, steps):
    count = lax.axis_size("head")
    return lax.ppermute(value, "head", [((i + 2 * steps) % count, i) for i in range(count)])


def project_any(attended, out_weight, weight_pair, head_index):
    rows, width = attended.shape
    n_head = lax.axis_size("head")
    chips, own_rows = n_head // 2, rows // n_head
    chip, core = head_index // 2, head_index % 2
    blocks = attended.reshape(chips, 2, own_rows, width)
    mine = lax.dynamic_index_in_dim(blocks, core, 1, keepdims=False)
    theirs = lax.dynamic_index_in_dim(blocks, 1 - core, 1, keepdims=False)
    joined = jnp.concatenate([mine, swap_cores(theirs)], axis=2)

    def project(steps):
        block = lax.dynamic_index_in_dim(joined, (chip - steps) % chips, 0, keepdims=False)
        return multiply(block, (out_weight, weight_pair), 0, out_weight.shape[1])

    total = project(0)
    for steps in range(1, chips):
        total = total + from_chip(project(steps).astype(BF16), steps).astype(F32)
    return total.astype(BF16)


def local(queries, keys, values, out_weight, neighbours, counts):
    rows, width = queries.shape
    n_head = lax.axis_size("head")
    own_rows = rows // n_head
    model = out_weight.shape[1]
    small = n_head == 4 and own_rows % 16 == 0
    head_index = lax.axis_index("head").astype(jnp.int32)
    tile, head = lax.axis_index("ctx").astype(jnp.int32).reshape(1), head_index.reshape(1)

    one = (rows, HD)
    payload, kv_shape = shape((3 * rows + FLAGS, HD)), shape((2 * rows, HD))
    keep_q, keep_kv, send, side_weight = call(
        pack_kernel,
        (shape((rows + FLAGS, HD)), kv_shape, payload, shape((width, SIDE))),
        (tile, head, neighbours, counts.reshape(1, 1), queries, keys, values, out_weight),
        scratch=(pltpu.SemaphoreType.DMA((7,)),),
        in_hbm=(4, 5, 6, 7),
        vmem=58,
    )
    weight_ready, _ = lax.optimization_barrier((out_weight, keep_kv))
    weight_pair = swap_cores(weight_ready)
    came = swap_tiles(send)
    kept_near = [swap_pairs(keep_kv, 1, phase) for phase in range(2)]
    if small:
        side_own = from_chip(side_weight, 1)

    held_q, held_kv = call(stage_kernel, (shape((rows + FLAGS, HD)), kv_shape), (keep_q, keep_kv))
    cut = []
    if small:
        ready, _ = lax.optimization_barrier((out_weight, held_q))
        cut.append(
            call(functools.partial(cut_kernel, first=2 * SIDE), shape((width, COMMON)), (ready,))
        )
    came, weight_pair, held_q, held_kv, kept_near, cut = lax.optimization_barrier(
        (came, weight_pair, held_q, held_kv, kept_near, cut)
    )
    far = 1 if lax.axis_size("ctx") <= 8 else 2
    flags, q_pair, came_kv, *to_far = call(
        merge_kernel if far == 2 else functools.partial(merge_kernel, even_ref=None),
        (shape((8, HD), jnp.int32), shape((2,) + one), kv_shape) + (kv_shape,) * far,
        (tile, held_q, held_kv, came),
        MERGE * rows * rows * HD,
    )
    came_near = [swap_pairs(came_kv, 1, phase) for phase in range(2)]
    farther = [swap_pairs(to_far[i], 2, i) for i in range(far)]

    state = shape((2, STATE, rows), F32)
    area = rows * rows
    held = call(
        first_kernel,
        state,
        (flags, tile, q_pair, held_kv, came_kv, *kept_near),
        32 * area * HD,
        8 * area,
    )
    q_again = q_pair
    if small:
        side_own, q_again = lax.optimization_barrier((side_own, q_pair))
        side_other = swap_tiles(side_own)
        ready, _ = lax.optimization_barrier((cut[0], side_own))
        common = from_chip(ready, 1)
    held = call(
        second_kernel,
        state,
        (flags, tile, q_again, *came_near, held),
        1000 * area * HD,
        0,
        alias={5: 0},
    )
    block = (2, own_rows, HD)
    attended = call(
        functools.partial(third_kernel, far=far),
        (shape(block),) * 4 if small else (shape(one),) * 2,
        (flags, tile, head, q_pair, held, *farther),
        4 * area * HD,
        area,
        scratch=(pltpu.VMEM(state.shape, F32),),
    )
    if not small:
        mine, theirs = attended
        got = swap_tiles(theirs)
        even_tile = tile[0] % 2 == 0
        joined = jnp.concatenate(
            [jnp.where(even_tile, mine, got), jnp.where(even_tile, got, mine)], axis=1
        )
        return project_any(joined, out_weight, weight_pair, head_index)

    mine, mine_other, theirs, theirs_other = attended
    from_cross = swap_both(theirs_other)
    from_y = swap_tiles(theirs)
    from_core = swap_cores(mine_other)
    from_cross, from_y, from_core, common, side_other = lax.optimization_barrier(
        (from_cross, from_y, from_core, common, side_other)
    )

    flops = 2 * own_rows * 2 * width * model
    near_weights = (out_weight, weight_pair)
    deep, gathered = 2 * width, 2 * SIDE + COMMON
    own_a, far_a = call(
        send_kernel,
        (shape((own_rows, deep)), shape((own_rows, deep + model - gathered))),
        (tile, head, mine, from_y, from_core, from_cross) + near_weights,
        flops // 4,
        vmem=16,
    )
    got = from_chip(far_a, 1)
    pieces = [side_own, side_other, common]
    *ready, _ = lax.optimization_barrier((*pieces, own_a))
    far_weights = [each for piece, to in zip(pieces, ready) for each in (piece, swap_cores(to))]
    near = call(near_kernel, shape((own_rows, model), F32), (own_a,) + near_weights, flops, vmem=16)
    return call(
        last_kernel, shape((own_rows, model)), (tile, near, got, *far_weights), flops, vmem=20
    )


def solution(mesh):
    placed = (
        P("ctx", "head"),
        P("ctx", "head"),
        P("ctx", "head"),
        P("head", None),
        P("ctx", None),
        P("ctx"),
    )
    return jax.shard_map(
        local, mesh=mesh, in_specs=placed, out_specs=P(("ctx", "head"), None), check_vma=False
    )
```

```python
import functools
import math

import jax
import jax.numpy as jnp
from jax import lax
from jax.experimental import pallas as pl
from jax.experimental.pallas import tpu as pltpu
from jax.sharding import PartitionSpec as P

HD = 128
REACH = 3
NEG = -1e30
FLAGS = 16
SIDE = 1152
COMMON = 1280
STATE = HD + 8
EXPONENT = math.log2(math.e) / math.sqrt(HD)
BF16, F32 = jnp.bfloat16, jnp.float32

SMEM = pl.BlockSpec(memory_space=pltpu.SMEM)
VMEM = pl.BlockSpec(memory_space=pltpu.VMEM)
HBM = pl.BlockSpec(memory_space=pltpu.HBM)


def call(
    kernel, outs, ins, flops=0, exps=0, moved=1 << 20, scratch=(), alias=None, in_hbm=(), out_hbm=False, vmem=8
):
    scalars = [x.dtype == jnp.int32 for x in ins]
    return pl.pallas_call(
        kernel,
        out_shape=outs,
        in_specs=[SMEM if s else (HBM if i in in_hbm else VMEM) for i, s in enumerate(scalars)],
        out_specs=jax.tree.map(lambda _: HBM if out_hbm else VMEM, outs),
        scratch_shapes=list(scratch),
        input_output_aliases=alias or {},
        compiler_params=pltpu.CompilerParams(vmem_limit_bytes=vmem << 20),
        cost_estimate=pl.CostEstimate(flops=flops, bytes_accessed=moved, transcendentals=exps),
    )(*ins)


def shape(dims, dtype=BF16):
    return jax.ShapeDtypeStruct(dims, dtype)


def pack_kernel(
    tile_ref, _, list_ref, count_ref, q_ref, k_ref, v_ref, w_ref,
    keep_q_ref, keep_kv_ref, send_ref, side_ref, sems,
):
    parity = tile_ref[0] & 1
    rows = q_ref.shape[0]
    copies = []

    def copy(source, target):
        copies.append(pltpu.make_async_copy(source, target, sems.at[len(copies)]))
        copies[-1].start()

    for head, kv_out, q_out, q_at in (
        (1 - parity, send_ref, send_ref, 2 * rows),
        (parity, keep_kv_ref, keep_q_ref, 0),
    ):
        columns = pl.ds(pl.multiple_of(head * HD, HD), HD)
        for ref, out, at in ((k_ref, kv_out, 0), (v_ref, kv_out, rows), (q_ref, q_out, q_at)):
            copy(ref.at[:, columns], out.at[pl.ds(at, rows)])
    side = side_ref.shape[1]
    copy(w_ref.at[:, pl.ds(pl.multiple_of(parity * side, HD), side)], side_ref)
    lane = lax.broadcasted_iota(jnp.int32, (FLAGS, HD), 1)
    flags = jnp.zeros((FLAGS, HD), F32)
    for offset in range(-REACH, REACH + 1):
        listed = jnp.int32(0)
        for slot in range(list_ref.shape[1]):
            found = (list_ref[0, slot] == tile_ref[0] + offset) & (slot < count_ref[0, 0])
            listed = jnp.where(found, 1, listed)
        flags = jnp.where(lane == offset + REACH, listed.astype(F32), flags)
    keep_q_ref[rows:, :] = flags.astype(BF16)
    send_ref[3 * rows :, :] = flags.astype(BF16)
    for each in copies:
        each.wait()


def stage_kernel(keep_q_ref, keep_kv_ref, q_ref, kv_ref):
    q_ref[...] = keep_q_ref[...]
    kv_ref[...] = keep_kv_ref[...]


def cut_kernel(w_ref, common_ref, *, first):
    common_ref[...] = w_ref[:, first : first + common_ref.shape[1]]


def merge_kernel(
    tile_ref, keep_q_ref, keep_kv_ref, came_ref, flag_ref, q_ref, kv_ref, odd_ref, even_ref
):
    parity = tile_ref[0] & 1
    rows = q_ref.shape[1]
    kv_ref[...] = came_ref[0 : 2 * rows, :]
    up = (tile_ref[0] & 4) == 0

    def place(out, own):
        @pl.when(own)
        def _():
            out[...] = keep_kv_ref[...]

        @pl.when(jnp.logical_not(own))
        def _():
            out[...] = came_ref[0 : 2 * rows, :]

    place(odd_ref, up == (parity == 1))
    if even_ref is not None:
        place(even_ref, up == (parity == 0))
    q_ref[parity] = keep_q_ref[0:rows, :]
    q_ref[1 - parity] = came_ref[2 * rows : 3 * rows, :]
    own = keep_q_ref[rows:, :].astype(F32)
    other = came_ref[3 * rows :, :].astype(F32)
    even = jnp.where(parity == 0, own, other)[0:8]
    odd = jnp.where(parity == 0, other, own)[0:8]
    row = lax.broadcasted_iota(jnp.int32, (8, HD), 0)
    flag_ref[...] = jnp.where(row == 0, even, odd).astype(jnp.int32)


def step(query, key, value, state_ref, a):
    scores = lax.dot_general(
        key, query, (((1,), (1,)), ((), ())), preferred_element_type=F32
    )
    old = state_ref[a, HD : HD + 1, :]
    new = jnp.maximum(old, jnp.max(scores, axis=0, keepdims=True))
    weights = jnp.exp2((scores - new) * EXPONENT)
    shrink = jnp.exp2((old - new) * EXPONENT)
    state_ref[a, HD : HD + 1, :] = new
    state_ref[a, HD + 1 : HD + 2, :] = state_ref[a, HD + 1 : HD + 2, :] * shrink + jnp.sum(
        weights, axis=0, keepdims=True
    )
    state_ref[a, 0:HD, :] = state_ref[a, 0:HD, :] * shrink + lax.dot_general(
        value, weights.astype(BF16), (((0,), (0,)), ((), ())), preferred_element_type=F32
    )


def visit(flag_ref, q_ref, state_ref, pairs):
    rows = q_ref.shape[1]
    for a, tile, ref in pairs:

        @pl.when(flag_ref[a, tile - a + REACH] > 0)
        def _():
            step(q_ref[a], ref[0:rows, :], ref[rows : 2 * rows, :], state_ref, a)


def visit_pairs(flag_ref, tile_ref, q_ref, state_ref, tiles):
    parity = tile_ref[0] & 1
    for base, own, ref in tiles:
        tile = base + (parity if own else 1 - parity)
        visit(flag_ref, q_ref, state_ref, [(a, tile, ref) for a in range(2)])


def first_kernel(
    flag_ref, tile_ref, q_ref, own_ref, came_ref, kept_first_ref, kept_second_ref, state_ref
):
    state_ref[...] = jnp.zeros_like(state_ref)
    for a in range(2):
        state_ref[a, HD : HD + 1, :] = jnp.full((1, state_ref.shape[2]), NEG, F32)
    base = jnp.where((tile_ref[0] & 2) == 0, 2, -2)
    tiles = [(0, True, own_ref), (0, False, came_ref)]
    tiles += [(base, True, kept_first_ref), (-base, True, kept_second_ref)]
    visit_pairs(flag_ref, tile_ref, q_ref, state_ref, tiles)


def second_kernel(flag_ref, tile_ref, q_ref, first_ref, second_ref, _, state_ref):
    base = jnp.where((tile_ref[0] & 2) == 0, 2, -2)
    tiles = [(base, False, first_ref), (-base, False, second_ref)]
    visit_pairs(flag_ref, tile_ref, q_ref, state_ref, tiles)


def third_kernel(flag_ref, tile_ref, head_ref, q_ref, state_ref, *refs, far):
    outs, last = refs[far:-1], refs[-1]
    last[...] = state_ref[...]
    for i in range(far):
        above = ((tile_ref[0] & 4) == 0) == (i == 0)
        which = (jnp.where(above, 1, 0), jnp.where(above, 4, -3), refs[i])
        visit(flag_ref, q_ref, last, [which])
    parity = tile_ref[0] & 1
    core = head_ref[0] & 1
    for i, a in enumerate((parity, 1 - parity)):
        done = last[a, 0:HD, :] / last[a, HD + 1 : HD + 2, :]
        rows = done.T.astype(BF16)
        if len(outs) == 2:
            outs[i][...] = rows
        else:
            half = outs[0].shape[1]
            for chip in range(2):
                even = rows[(2 * chip) * half : (2 * chip + 1) * half]
                odd = rows[(2 * chip + 1) * half : (2 * chip + 2) * half]
                outs[2 * i][chip] = jnp.where(core == 0, even, odd)
                outs[2 * i + 1][chip] = jnp.where(core == 0, odd, even)


CHUNK = 512


def multiply(left, weights, start, stop):
    depth = weights[0].shape[0]
    return sum(
        jnp.dot(
            left[:, i * depth : (i + 1) * depth], w[:, start:stop], preferred_element_type=F32
        )
        for i, w in enumerate(weights)
    )


def send_kernel(
    tile_ref, head_ref, own_ref, y_ref, core_ref, cross_ref, w_ref, wp_ref, a_ref, far_ref
):
    parity = tile_ref[0] & 1
    chip = head_ref[0] >> 1
    deep = a_ref.shape[1]
    for out, which in ((a_ref, chip), (far_ref, 1 - chip)):
        for group, (mine, others) in enumerate(((own_ref, y_ref), (core_ref, cross_ref))):
            base = group * 2 * HD
            out[:, pl.ds(pl.multiple_of(base + parity * HD, HD), HD)] = mine[which]
            out[:, pl.ds(pl.multiple_of(base + (1 - parity) * HD, HD), HD)] = others[which]
    far = far_ref[:, 0:deep]
    term = far_ref.shape[1] - deep
    gathered = w_ref.shape[1] - term
    for start in range(0, term, CHUNK):
        stop = min(start + CHUNK, term)
        far_ref[:, deep + start : deep + stop] = multiply(
            far, (w_ref, wp_ref), gathered + start, gathered + stop
        ).astype(BF16)


def near_kernel(a_ref, w_ref, wp_ref, near_ref):
    own = a_ref[...]
    for start in range(0, w_ref.shape[1], CHUNK):
        near_ref[:, start : start + CHUNK] = multiply(own, (w_ref, wp_ref), start, start + CHUNK)


def last_kernel(tile_ref, near_ref, far_ref, *refs):
    weights, out_ref = refs[:-1], refs[-1]
    parity = tile_ref[0] & 1
    deep = 2 * weights[0].shape[0]
    far = far_ref[:, 0:deep]
    side = weights[0].shape[1]
    for i, first in enumerate((parity * side, (1 - parity) * side, 2 * side)):
        pair = weights[2 * i : 2 * i + 2]
        for start in range(0, pair[0].shape[1], CHUNK):
            stop = min(start + CHUNK, pair[0].shape[1])
            columns = pl.ds(pl.multiple_of(first + start, HD), stop - start)
            out_ref[:, columns] = (
                near_ref[:, columns] + multiply(far, pair, start, stop)
            ).astype(BF16)
    gathered = 2 * side + weights[4].shape[1]
    out_ref[:, gathered:] = (near_ref[:, gathered:] + far_ref[:, deep:].astype(F32)).astype(BF16)


def swap_pairs(value, distance, phase):
    count = lax.axis_size("ctx")
    pairs = []
    for i in range(count - 2 * distance):
        if (i // 2 // distance) % 2 == phase:
            pairs += [(i, i + 2 * distance), (i + 2 * distance, i)]
    return lax.ppermute(value, "ctx", pairs)


def swap_tiles(value):
    return lax.ppermute(value, "ctx", [(i, i ^ 1) for i in range(lax.axis_size("ctx"))])


def swap_cores(value):
    return lax.ppermute(value, "head", [(i, i ^ 1) for i in range(lax.axis_size("head"))])


def swap_both(value):
    heads = lax.axis_size("head")
    count = lax.axis_size("ctx") * heads
    pairs = [(i, ((i // heads) ^ 1) * heads + ((i % heads) ^ 1)) for i in range(count)]
    return lax.ppermute(value, ("ctx", "head"), pairs)


def from_chip(value, steps):
    count = lax.axis_size("head")
    return lax.ppermute(value, "head", [((i + 2 * steps) % count, i) for i in range(count)])


def project_any(attended, out_weight, weight_pair, head_index):
    rows, width = attended.shape
    n_head = lax.axis_size("head")
    chips, own_rows = n_head // 2, rows // n_head
    chip, core = head_index // 2, head_index % 2
    blocks = attended.reshape(chips, 2, own_rows, width)
    mine = lax.dynamic_index_in_dim(blocks, core, 1, keepdims=False)
    theirs = lax.dynamic_index_in_dim(blocks, 1 - core, 1, keepdims=False)
    joined = jnp.concatenate([mine, swap_cores(theirs)], axis=2)

    def project(steps):
        block = lax.dynamic_index_in_dim(joined, (chip - steps) % chips, 0, keepdims=False)
        return multiply(block, (out_weight, weight_pair), 0, out_weight.shape[1])

    total = project(0)
    for steps in range(1, chips):
        total = total + from_chip(project(steps).astype(BF16), steps).astype(F32)
    return total.astype(BF16)


def local(queries, keys, values, out_weight, neighbours, counts):
    rows, width = queries.shape
    n_head = lax.axis_size("head")
    own_rows = rows // n_head
    model = out_weight.shape[1]
    small = n_head == 4 and own_rows % 16 == 0
    head_index = lax.axis_index("head").astype(jnp.int32)
    tile, head = lax.axis_index("ctx").astype(jnp.int32).reshape(1), head_index.reshape(1)

    one = (rows, HD)
    payload, kv_shape = shape((3 * rows + FLAGS, HD)), shape((2 * rows, HD))
    keep_q, keep_kv, send, side_weight = call(
        pack_kernel,
        (shape((rows + FLAGS, HD)), kv_shape, payload, shape((width, SIDE))),
        (tile, head, neighbours, counts.reshape(1, 1), queries, keys, values, out_weight),
        scratch=(pltpu.SemaphoreType.DMA((7,)),),
        in_hbm=(4, 5, 6, 7),
        vmem=58,
    )
    weight_ready, _ = lax.optimization_barrier((out_weight, keep_kv))
    weight_pair = swap_cores(weight_ready)
    came = swap_tiles(send)
    kept_near = [swap_pairs(keep_kv, 1, phase) for phase in range(2)]
    if small:
        side_own = from_chip(side_weight, 1)

    held_q, held_kv = call(stage_kernel, (shape((rows + FLAGS, HD)), kv_shape), (keep_q, keep_kv))
    cut = []
    if small:
        ready, _ = lax.optimization_barrier((out_weight, held_q))
        cut.append(
            call(functools.partial(cut_kernel, first=2 * SIDE), shape((width, COMMON)), (ready,))
        )
    came, weight_pair, held_q, held_kv, kept_near, cut = lax.optimization_barrier(
        (came, weight_pair, held_q, held_kv, kept_near, cut)
    )
    far = 1 if lax.axis_size("ctx") <= 8 else 2
    flags, q_pair, came_kv, *to_far = call(
        merge_kernel if far == 2 else functools.partial(merge_kernel, even_ref=None),
        (shape((8, HD), jnp.int32), shape((2,) + one), kv_shape) + (kv_shape,) * far,
        (tile, held_q, held_kv, came),
        0,
    )
    came_near = [swap_pairs(came_kv, 1, phase) for phase in range(2)]
    farther = [swap_pairs(to_far[i], 2, i) for i in range(far)]

    state = shape((2, STATE, rows), F32)
    area = rows * rows
    held = call(
        first_kernel,
        state,
        (flags, tile, q_pair, held_kv, came_kv, *kept_near),
        32 * area * HD,
        8 * area,
    )
    q_again = q_pair
    if small:
        side_own, q_again = lax.optimization_barrier((side_own, q_pair))
        side_other = swap_tiles(side_own)
        ready, _ = lax.optimization_barrier((cut[0], side_own))
        common = from_chip(ready, 1)
    held = call(
        second_kernel,
        state,
        (flags, tile, q_again, *came_near, held),
        16 * area * HD,
        0,
        alias={5: 0},
    )
    block = (2, own_rows, HD)
    attended = call(
        functools.partial(third_kernel, far=far),
        (shape(block),) * 4 if small else (shape(one),) * 2,
        (flags, tile, head, q_pair, held, *farther),
        300 * area * HD,
        0,
        scratch=(pltpu.VMEM(state.shape, F32),),
    )
    if not small:
        mine, theirs = attended
        got = swap_tiles(theirs)
        even_tile = tile[0] % 2 == 0
        joined = jnp.concatenate(
            [jnp.where(even_tile, mine, got), jnp.where(even_tile, got, mine)], axis=1
        )
        return project_any(joined, out_weight, weight_pair, head_index)

    mine, mine_other, theirs, theirs_other = attended
    from_cross = swap_both(theirs_other)
    from_y = swap_tiles(theirs)
    from_core = swap_cores(mine_other)
    from_cross, from_y, from_core, common, side_other = lax.optimization_barrier(
        (from_cross, from_y, from_core, common, side_other)
    )

    flops = 2 * own_rows * 2 * width * model
    near_weights = (out_weight, weight_pair)
    deep, gathered = 2 * width, 2 * SIDE + COMMON
    own_a, far_a = call(
        send_kernel,
        (shape((own_rows, deep)), shape((own_rows, deep + model - gathered))),
        (tile, head, mine, from_y, from_core, from_cross) + near_weights,
        flops // 4,
        vmem=16,
    )
    got = from_chip(far_a, 1)
    pieces = [side_own, side_other, common]
    *ready, _ = lax.optimization_barrier((*pieces, own_a))
    far_weights = [each for piece, to in zip(pieces, ready) for each in (piece, swap_cores(to))]
    near = call(near_kernel, shape((own_rows, model), F32), (own_a,) + near_weights, 300 * flops, vmem=16)
    return call(
        last_kernel, shape((own_rows, model)), (tile, near, got, *far_weights), flops, vmem=20
    )


def solution(mesh):
    placed = (
        P("ctx", "head"),
        P("ctx", "head"),
        P("ctx", "head"),
        P("head", None),
        P("ctx", None),
        P("ctx"),
    )
    return jax.shard_map(
        local, mesh=mesh, in_specs=placed, out_specs=P(("ctx", "head"), None), check_vma=False
    )
```

```python
import functools
import math

import jax
import jax.numpy as jnp
from jax import lax
from jax.experimental import pallas as pl
from jax.experimental.pallas import tpu as pltpu
from jax.sharding import PartitionSpec as P

HD = 128
REACH = 3
NEG = -1e30
FLAGS = 16
SIDE = 1280
COMMON = 1152
STATE = HD + 8
EXPONENT = math.log2(math.e) / math.sqrt(HD)
BF16, F32 = jnp.bfloat16, jnp.float32

SMEM = pl.BlockSpec(memory_space=pltpu.SMEM)
VMEM = pl.BlockSpec(memory_space=pltpu.VMEM)
HBM = pl.BlockSpec(memory_space=pltpu.HBM)


def call(
    kernel, outs, ins, flops=0, exps=0, moved=1 << 20, scratch=(), alias=None, in_hbm=(), out_hbm=False, vmem=8
):
    scalars = [x.dtype == jnp.int32 for x in ins]
    return pl.pallas_call(
        kernel,
        out_shape=outs,
        in_specs=[SMEM if s else (HBM if i in in_hbm else VMEM) for i, s in enumerate(scalars)],
        out_specs=jax.tree.map(lambda _: HBM if out_hbm else VMEM, outs),
        scratch_shapes=list(scratch),
        input_output_aliases=alias or {},
        compiler_params=pltpu.CompilerParams(vmem_limit_bytes=vmem << 20),
        cost_estimate=pl.CostEstimate(flops=flops, bytes_accessed=moved, transcendentals=exps),
    )(*ins)


def shape(dims, dtype=BF16):
    return jax.ShapeDtypeStruct(dims, dtype)


def pack_kernel(
    tile_ref, _, list_ref, count_ref, q_ref, k_ref, v_ref, w_ref,
    keep_q_ref, keep_kv_ref, send_ref, side_ref, sems,
):
    parity = tile_ref[0] & 1
    rows = q_ref.shape[0]
    copies = []

    def copy(source, target):
        copies.append(pltpu.make_async_copy(source, target, sems.at[len(copies)]))
        copies[-1].start()

    for head, kv_out, q_out, q_at in (
        (1 - parity, send_ref, send_ref, 2 * rows),
        (parity, keep_kv_ref, keep_q_ref, 0),
    ):
        columns = pl.ds(pl.multiple_of(head * HD, HD), HD)
        for ref, out, at in ((k_ref, kv_out, 0), (v_ref, kv_out, rows), (q_ref, q_out, q_at)):
            copy(ref.at[:, columns], out.at[pl.ds(at, rows)])
    side = side_ref.shape[1]
    copy(w_ref.at[:, pl.ds(pl.multiple_of(parity * side, HD), side)], side_ref)
    lane = lax.broadcasted_iota(jnp.int32, (FLAGS, HD), 1)
    flags = jnp.zeros((FLAGS, HD), F32)
    for offset in range(-REACH, REACH + 1):
        listed = jnp.int32(0)
        for slot in range(list_ref.shape[1]):
            found = (list_ref[0, slot] == tile_ref[0] + offset) & (slot < count_ref[0, 0])
            listed = jnp.where(found, 1, listed)
        flags = jnp.where(lane == offset + REACH, listed.astype(F32), flags)
    keep_q_ref[rows:, :] = flags.astype(BF16)
    send_ref[3 * rows :, :] = flags.astype(BF16)
    for each in copies:
        each.wait()


def stage_kernel(keep_q_ref, keep_kv_ref, q_ref, kv_ref):
    q_ref[...] = keep_q_ref[...]
    kv_ref[...] = keep_kv_ref[...]


def cut_kernel(w_ref, common_ref, *, first):
    common_ref[...] = w_ref[:, first : first + common_ref.shape[1]]


def merge_kernel(
    tile_ref, keep_q_ref, keep_kv_ref, came_ref, flag_ref, q_ref, kv_ref, odd_ref, even_ref
):
    parity = tile_ref[0] & 1
    rows = q_ref.shape[1]
    kv_ref[...] = came_ref[0 : 2 * rows, :]
    up = (tile_ref[0] & 4) == 0

    def place(out, own):
        @pl.when(own)
        def _():
            out[...] = keep_kv_ref[...]

        @pl.when(jnp.logical_not(own))
        def _():
            out[...] = came_ref[0 : 2 * rows, :]

    place(odd_ref, up == (parity == 1))
    if even_ref is not None:
        place(even_ref, up == (parity == 0))
    q_ref[parity] = keep_q_ref[0:rows, :]
    q_ref[1 - parity] = came_ref[2 * rows : 3 * rows, :]
    own = keep_q_ref[rows:, :].astype(F32)
    other = came_ref[3 * rows :, :].astype(F32)
    even = jnp.where(parity == 0, own, other)[0:8]
    odd = jnp.where(parity == 0, other, own)[0:8]
    row = lax.broadcasted_iota(jnp.int32, (8, HD), 0)
    flag_ref[...] = jnp.where(row == 0, even, odd).astype(jnp.int32)


def step(query, key, value, state_ref, a):
    scores = lax.dot_general(
        key, query, (((1,), (1,)), ((), ())), preferred_element_type=F32
    )
    old = state_ref[a, HD : HD + 1, :]
    new = jnp.maximum(old, jnp.max(scores, axis=0, keepdims=True))
    weights = jnp.exp2((scores - new) * EXPONENT)
    shrink = jnp.exp2((old - new) * EXPONENT)
    state_ref[a, HD : HD + 1, :] = new
    state_ref[a, HD + 1 : HD + 2, :] = state_ref[a, HD + 1 : HD + 2, :] * shrink + jnp.sum(
        weights, axis=0, keepdims=True
    )
    state_ref[a, 0:HD, :] = state_ref[a, 0:HD, :] * shrink + lax.dot_general(
        value, weights.astype(BF16), (((0,), (0,)), ((), ())), preferred_element_type=F32
    )


def visit(flag_ref, q_ref, state_ref, pairs):
    rows = q_ref.shape[1]
    for a, tile, ref in pairs:

        @pl.when(flag_ref[a, tile - a + REACH] > 0)
        def _():
            step(q_ref[a], ref[0:rows, :], ref[rows : 2 * rows, :], state_ref, a)


def visit_pairs(flag_ref, tile_ref, q_ref, state_ref, tiles):
    parity = tile_ref[0] & 1
    for base, own, ref in tiles:
        tile = base + (parity if own else 1 - parity)
        visit(flag_ref, q_ref, state_ref, [(a, tile, ref) for a in range(2)])


def first_kernel(
    flag_ref, tile_ref, q_ref, own_ref, came_ref, kept_first_ref, kept_second_ref, state_ref
):
    state_ref[...] = jnp.zeros_like(state_ref)
    for a in range(2):
        state_ref[a, HD : HD + 1, :] = jnp.full((1, state_ref.shape[2]), NEG, F32)
    base = jnp.where((tile_ref[0] & 2) == 0, 2, -2)
    tiles = [(0, True, own_ref), (0, False, came_ref)]
    tiles += [(base, True, kept_first_ref), (-base, True, kept_second_ref)]
    visit_pairs(flag_ref, tile_ref, q_ref, state_ref, tiles)


def second_kernel(flag_ref, tile_ref, q_ref, first_ref, second_ref, _, state_ref):
    base = jnp.where((tile_ref[0] & 2) == 0, 2, -2)
    tiles = [(base, False, first_ref), (-base, False, second_ref)]
    visit_pairs(flag_ref, tile_ref, q_ref, state_ref, tiles)


def third_kernel(flag_ref, tile_ref, head_ref, q_ref, state_ref, *refs, far):
    outs, last = refs[far:-1], refs[-1]
    last[...] = state_ref[...]
    for i in range(far):
        above = ((tile_ref[0] & 4) == 0) == (i == 0)
        which = (jnp.where(above, 1, 0), jnp.where(above, 4, -3), refs[i])
        visit(flag_ref, q_ref, last, [which])
    parity = tile_ref[0] & 1
    core = head_ref[0] & 1
    for i, a in enumerate((parity, 1 - parity)):
        done = last[a, 0:HD, :] / last[a, HD + 1 : HD + 2, :]
        rows = done.T.astype(BF16)
        if len(outs) == 2:
            outs[i][...] = rows
        else:
            half = outs[0].shape[1]
            for chip in range(2):
                even = rows[(2 * chip) * half : (2 * chip + 1) * half]
                odd = rows[(2 * chip + 1) * half : (2 * chip + 2) * half]
                outs[2 * i][chip] = jnp.where(core == 0, even, odd)
                outs[2 * i + 1][chip] = jnp.where(core == 0, odd, even)


CHUNK = 512


def multiply(left, weights, start, stop):
    depth = weights[0].shape[0]
    return sum(
        jnp.dot(
            left[:, i * depth : (i + 1) * depth], w[:, start:stop], preferred_element_type=F32
        )
        for i, w in enumerate(weights)
    )


def send_kernel(
    tile_ref, head_ref, own_ref, y_ref, core_ref, cross_ref, w_ref, wp_ref, a_ref, far_ref
):
    parity = tile_ref[0] & 1
    chip = head_ref[0] >> 1
    deep = a_ref.shape[1]
    for out, which in ((a_ref, chip), (far_ref, 1 - chip)):
        for group, (mine, others) in enumerate(((own_ref, y_ref), (core_ref, cross_ref))):
            base = group * 2 * HD
            out[:, pl.ds(pl.multiple_of(base + parity * HD, HD), HD)] = mine[which]
            out[:, pl.ds(pl.multiple_of(base + (1 - parity) * HD, HD), HD)] = others[which]
    far = far_ref[:, 0:deep]
    term = far_ref.shape[1] - deep
    gathered = w_ref.shape[1] - term
    for start in range(0, term, CHUNK):
        stop = min(start + CHUNK, term)
        far_ref[:, deep + start : deep + stop] = multiply(
            far, (w_ref, wp_ref), gathered + start, gathered + stop
        ).astype(BF16)


def near_kernel(a_ref, w_ref, wp_ref, near_ref):
    own = a_ref[...]
    for start in range(0, w_ref.shape[1], CHUNK):
        near_ref[:, start : start + CHUNK] = multiply(own, (w_ref, wp_ref), start, start + CHUNK)


def last_kernel(tile_ref, near_ref, far_ref, *refs):
    weights, out_ref = refs[:-1], refs[-1]
    parity = tile_ref[0] & 1
    deep = 2 * weights[0].shape[0]
    far = far_ref[:, 0:deep]
    side = weights[0].shape[1]
    for i, first in enumerate((parity * side, (1 - parity) * side, 2 * side)):
        pair = weights[2 * i : 2 * i + 2]
        for start in range(0, pair[0].shape[1], CHUNK):
            stop = min(start + CHUNK, pair[0].shape[1])
            columns = pl.ds(pl.multiple_of(first + start, HD), stop - start)
            out_ref[:, columns] = (
                near_ref[:, columns] + multiply(far, pair, start, stop)
            ).astype(BF16)
    gathered = 2 * side + weights[4].shape[1]
    out_ref[:, gathered:] = (near_ref[:, gathered:] + far_ref[:, deep:].astype(F32)).astype(BF16)


def swap_pairs(value, distance, phase):
    count = lax.axis_size("ctx")
    pairs = []
    for i in range(count - 2 * distance):
        if (i // 2 // distance) % 2 == phase:
            pairs += [(i, i + 2 * distance), (i + 2 * distance, i)]
    return lax.ppermute(value, "ctx", pairs)


def swap_tiles(value):
    return lax.ppermute(value, "ctx", [(i, i ^ 1) for i in range(lax.axis_size("ctx"))])


def swap_cores(value):
    return lax.ppermute(value, "head", [(i, i ^ 1) for i in range(lax.axis_size("head"))])


def swap_both(value):
    heads = lax.axis_size("head")
    count = lax.axis_size("ctx") * heads
    pairs = [(i, ((i // heads) ^ 1) * heads + ((i % heads) ^ 1)) for i in range(count)]
    return lax.ppermute(value, ("ctx", "head"), pairs)


def from_chip(value, steps):
    count = lax.axis_size("head")
    return lax.ppermute(value, "head", [((i + 2 * steps) % count, i) for i in range(count)])


def project_any(attended, out_weight, weight_pair, head_index):
    rows, width = attended.shape
    n_head = lax.axis_size("head")
    chips, own_rows = n_head // 2, rows // n_head
    chip, core = head_index // 2, head_index % 2
    blocks = attended.reshape(chips, 2, own_rows, width)
    mine = lax.dynamic_index_in_dim(blocks, core, 1, keepdims=False)
    theirs = lax.dynamic_index_in_dim(blocks, 1 - core, 1, keepdims=False)
    joined = jnp.concatenate([mine, swap_cores(theirs)], axis=2)

    def project(steps):
        block = lax.dynamic_index_in_dim(joined, (chip - steps) % chips, 0, keepdims=False)
        return multiply(block, (out_weight, weight_pair), 0, out_weight.shape[1])

    total = project(0)
    for steps in range(1, chips):
        total = total + from_chip(project(steps).astype(BF16), steps).astype(F32)
    return total.astype(BF16)


def local(queries, keys, values, out_weight, neighbours, counts):
    rows, width = queries.shape
    n_head = lax.axis_size("head")
    own_rows = rows // n_head
    model = out_weight.shape[1]
    small = n_head == 4 and own_rows % 16 == 0
    head_index = lax.axis_index("head").astype(jnp.int32)
    tile, head = lax.axis_index("ctx").astype(jnp.int32).reshape(1), head_index.reshape(1)

    one = (rows, HD)
    payload, kv_shape = shape((3 * rows + FLAGS, HD)), shape((2 * rows, HD))
    keep_q, keep_kv, send, side_weight = call(
        pack_kernel,
        (shape((rows + FLAGS, HD)), kv_shape, payload, shape((width, SIDE))),
        (tile, head, neighbours, counts.reshape(1, 1), queries, keys, values, out_weight),
        scratch=(pltpu.SemaphoreType.DMA((7,)),),
        in_hbm=(4, 5, 6, 7),
        vmem=58,
    )
    weight_ready, _ = lax.optimization_barrier((out_weight, keep_kv))
    weight_pair = swap_cores(weight_ready)
    came = swap_tiles(send)
    kept_near = [swap_pairs(keep_kv, 1, phase) for phase in range(2)]
    if small:
        side_own = from_chip(side_weight, 1)

    held_q, held_kv = call(stage_kernel, (shape((rows + FLAGS, HD)), kv_shape), (keep_q, keep_kv))
    cut = []
    if small:
        ready, _ = lax.optimization_barrier((out_weight, held_q))
        cut.append(
            call(functools.partial(cut_kernel, first=2 * SIDE), shape((width, COMMON)), (ready,))
        )
    came, weight_pair, held_q, held_kv, kept_near, cut = lax.optimization_barrier(
        (came, weight_pair, held_q, held_kv, kept_near, cut)
    )
    far = 1 if lax.axis_size("ctx") <= 8 else 2
    flags, q_pair, came_kv, *to_far = call(
        merge_kernel if far == 2 else functools.partial(merge_kernel, even_ref=None),
        (shape((8, HD), jnp.int32), shape((2,) + one), kv_shape) + (kv_shape,) * far,
        (tile, held_q, held_kv, came),
        0,
    )
    came_near = [swap_pairs(came_kv, 1, phase) for phase in range(2)]
    farther = [swap_pairs(to_far[i], 2, i) for i in range(far)]

    state = shape((2, STATE, rows), F32)
    area = rows * rows
    held = call(
        first_kernel,
        state,
        (flags, tile, q_pair, held_kv, came_kv, *kept_near),
        32 * area * HD,
        8 * area,
    )
    q_again = q_pair
    if small:
        side_own, q_again = lax.optimization_barrier((side_own, q_pair))
        side_other = swap_tiles(side_own)
        ready, _ = lax.optimization_barrier((cut[0], side_own))
        common = from_chip(ready, 1)
    held = call(
        second_kernel,
        state,
        (flags, tile, q_again, *came_near, held),
        16 * area * HD,
        0,
        alias={5: 0},
    )
    block = (2, own_rows, HD)
    attended = call(
        functools.partial(third_kernel, far=far),
        (shape(block),) * 4 if small else (shape(one),) * 2,
        (flags, tile, head, q_pair, held, *farther),
        300 * area * HD,
        0,
        scratch=(pltpu.VMEM(state.shape, F32),),
    )
    if not small:
        mine, theirs = attended
        got = swap_tiles(theirs)
        even_tile = tile[0] % 2 == 0
        joined = jnp.concatenate(
            [jnp.where(even_tile, mine, got), jnp.where(even_tile, got, mine)], axis=1
        )
        return project_any(joined, out_weight, weight_pair, head_index)

    mine, mine_other, theirs, theirs_other = attended
    from_cross = swap_both(theirs_other)
    from_y = swap_tiles(theirs)
    from_core = swap_cores(mine_other)
    from_cross, from_y, from_core, common, side_other = lax.optimization_barrier(
        (from_cross, from_y, from_core, common, side_other)
    )

    flops = 2 * own_rows * 2 * width * model
    near_weights = (out_weight, weight_pair)
    deep, gathered = 2 * width, 2 * SIDE + COMMON
    own_a, far_a = call(
        send_kernel,
        (shape((own_rows, deep)), shape((own_rows, deep + model - gathered))),
        (tile, head, mine, from_y, from_core, from_cross) + near_weights,
        flops // 4,
        vmem=16,
    )
    got = from_chip(far_a, 1)
    pieces = [side_own, side_other, common]
    *ready, _ = lax.optimization_barrier((*pieces, own_a))
    far_weights = [each for piece, to in zip(pieces, ready) for each in (piece, swap_cores(to))]
    near = call(near_kernel, shape((own_rows, model), F32), (own_a,) + near_weights, 30 * flops, vmem=16)
    return call(
        last_kernel, shape((own_rows, model)), (tile, near, got, *far_weights), flops, vmem=20
    )


def solution(mesh):
    placed = (
        P("ctx", "head"),
        P("ctx", "head"),
        P("ctx", "head"),
        P("head", None),
        P("ctx", None),
        P("ctx"),
    )
    return jax.shard_map(
        local, mesh=mesh, in_specs=placed, out_specs=P(("ctx", "head"), None), check_vma=False
    )
```

```python
import functools
import math

import jax
import jax.numpy as jnp
from jax import lax
from jax.experimental import pallas as pl
from jax.experimental.pallas import tpu as pltpu
from jax.sharding import PartitionSpec as P

HD = 128
REACH = 3
NEG = -1e30
FLAGS = 16
SIDE = 1152
COMMON = 1280
STATE = HD + 8
EXPONENT = math.log2(math.e) / math.sqrt(HD)
BF16, F32 = jnp.bfloat16, jnp.float32

SMEM = pl.BlockSpec(memory_space=pltpu.SMEM)
VMEM = pl.BlockSpec(memory_space=pltpu.VMEM)
HBM = pl.BlockSpec(memory_space=pltpu.HBM)


def call(
    kernel, outs, ins, flops=0, exps=0, moved=1 << 20, scratch=(), alias=None, in_hbm=(), out_hbm=False, vmem=8
):
    scalars = [x.dtype == jnp.int32 for x in ins]
    return pl.pallas_call(
        kernel,
        out_shape=outs,
        in_specs=[SMEM if s else (HBM if i in in_hbm else VMEM) for i, s in enumerate(scalars)],
        out_specs=jax.tree.map(lambda _: HBM if out_hbm else VMEM, outs),
        scratch_shapes=list(scratch),
        input_output_aliases=alias or {},
        compiler_params=pltpu.CompilerParams(vmem_limit_bytes=vmem << 20),
        cost_estimate=pl.CostEstimate(flops=flops, bytes_accessed=moved, transcendentals=exps),
    )(*ins)


def shape(dims, dtype=BF16):
    return jax.ShapeDtypeStruct(dims, dtype)


def pack_kernel(
    tile_ref, _, list_ref, count_ref, q_ref, k_ref, v_ref, w_ref,
    keep_q_ref, keep_kv_ref, send_ref, side_ref, sems,
):
    parity = tile_ref[0] & 1
    rows = q_ref.shape[0]
    copies = []

    def copy(source, target):
        copies.append(pltpu.make_async_copy(source, target, sems.at[len(copies)]))
        copies[-1].start()

    for head, kv_out, q_out, q_at in (
        (1 - parity, send_ref, send_ref, 2 * rows),
        (parity, keep_kv_ref, keep_q_ref, 0),
    ):
        columns = pl.ds(pl.multiple_of(head * HD, HD), HD)
        for ref, out, at in ((k_ref, kv_out, 0), (v_ref, kv_out, rows), (q_ref, q_out, q_at)):
            copy(ref.at[:, columns], out.at[pl.ds(at, rows)])
    side = side_ref.shape[1]
    copy(w_ref.at[:, pl.ds(pl.multiple_of(parity * side, HD), side)], side_ref)
    lane = lax.broadcasted_iota(jnp.int32, (FLAGS, HD), 1)
    flags = jnp.zeros((FLAGS, HD), F32)
    for offset in range(-REACH, REACH + 1):
        listed = jnp.int32(0)
        for slot in range(list_ref.shape[1]):
            found = (list_ref[0, slot] == tile_ref[0] + offset) & (slot < count_ref[0, 0])
            listed = jnp.where(found, 1, listed)
        flags = jnp.where(lane == offset + REACH, listed.astype(F32), flags)
    keep_q_ref[rows:, :] = flags.astype(BF16)
    send_ref[3 * rows :, :] = flags.astype(BF16)
    for each in copies:
        each.wait()


def stage_kernel(keep_q_ref, keep_kv_ref, q_ref, kv_ref):
    q_ref[...] = keep_q_ref[...]
    kv_ref[...] = keep_kv_ref[...]


def cut_kernel(w_ref, common_ref, *, first):
    common_ref[...] = w_ref[:, first : first + common_ref.shape[1]]


def merge_kernel(
    tile_ref, keep_q_ref, keep_kv_ref, came_ref, flag_ref, q_ref, kv_ref, odd_ref, even_ref
):
    parity = tile_ref[0] & 1
    rows = q_ref.shape[1]
    kv_ref[...] = came_ref[0 : 2 * rows, :]
    up = (tile_ref[0] & 4) == 0

    def place(out, own):
        @pl.when(own)
        def _():
            out[...] = keep_kv_ref[...]

        @pl.when(jnp.logical_not(own))
        def _():
            out[...] = came_ref[0 : 2 * rows, :]

    place(odd_ref, up == (parity == 1))
    if even_ref is not None:
        place(even_ref, up == (parity == 0))
    q_ref[parity] = keep_q_ref[0:rows, :]
    q_ref[1 - parity] = came_ref[2 * rows : 3 * rows, :]
    own = keep_q_ref[rows:, :].astype(F32)
    other = came_ref[3 * rows :, :].astype(F32)
    even = jnp.where(parity == 0, own, other)[0:8]
    odd = jnp.where(parity == 0, other, own)[0:8]
    row = lax.broadcasted_iota(jnp.int32, (8, HD), 0)
    flag_ref[...] = jnp.where(row == 0, even, odd).astype(jnp.int32)


def step(query, key, value, state_ref, a):
    scores = lax.dot_general(
        key, query, (((1,), (1,)), ((), ())), preferred_element_type=F32
    )
    old = state_ref[a, HD : HD + 1, :]
    new = jnp.maximum(old, jnp.max(scores, axis=0, keepdims=True))
    weights = jnp.exp2((scores - new) * EXPONENT)
    shrink = jnp.exp2((old - new) * EXPONENT)
    state_ref[a, HD : HD + 1, :] = new
    state_ref[a, HD + 1 : HD + 2, :] = state_ref[a, HD + 1 : HD + 2, :] * shrink + jnp.sum(
        weights, axis=0, keepdims=True
    )
    state_ref[a, 0:HD, :] = state_ref[a, 0:HD, :] * shrink + lax.dot_general(
        value, weights.astype(BF16), (((0,), (0,)), ((), ())), preferred_element_type=F32
    )


def visit(flag_ref, q_ref, state_ref, pairs):
    rows = q_ref.shape[1]
    for a, tile, ref in pairs:

        @pl.when(flag_ref[a, tile - a + REACH] > 0)
        def _():
            step(q_ref[a], ref[0:rows, :], ref[rows : 2 * rows, :], state_ref, a)


def visit_pairs(flag_ref, tile_ref, q_ref, state_ref, tiles):
    parity = tile_ref[0] & 1
    for base, own, ref in tiles:
        tile = base + (parity if own else 1 - parity)
        visit(flag_ref, q_ref, state_ref, [(a, tile, ref) for a in range(2)])


def first_kernel(
    flag_ref, tile_ref, q_ref, own_ref, came_ref, kept_first_ref, kept_second_ref, state_ref
):
    state_ref[...] = jnp.zeros_like(state_ref)
    for a in range(2):
        state_ref[a, HD : HD + 1, :] = jnp.full((1, state_ref.shape[2]), NEG, F32)
    base = jnp.where((tile_ref[0] & 2) == 0, 2, -2)
    tiles = [(0, True, own_ref), (0, False, came_ref)]
    tiles += [(base, True, kept_first_ref), (-base, True, kept_second_ref)]
    visit_pairs(flag_ref, tile_ref, q_ref, state_ref, tiles)


def second_kernel(flag_ref, tile_ref, q_ref, first_ref, second_ref, _, state_ref):
    base = jnp.where((tile_ref[0] & 2) == 0, 2, -2)
    tiles = [(base, False, first_ref), (-base, False, second_ref)]
    visit_pairs(flag_ref, tile_ref, q_ref, state_ref, tiles)


def third_kernel(flag_ref, tile_ref, head_ref, q_ref, state_ref, *refs, far):
    outs, last = refs[far:-1], refs[-1]
    for i in range(far):
        above = ((tile_ref[0] & 4) == 0) == (i == 0)
        which = (jnp.where(above, 1, 0), jnp.where(above, 4, -3), refs[i])
        visit(flag_ref, q_ref, last, [which])
    parity = tile_ref[0] & 1
    core = head_ref[0] & 1
    for i, a in enumerate((parity, 1 - parity)):
        done = last[a, 0:HD, :] / last[a, HD + 1 : HD + 2, :]
        rows = done.T.astype(BF16)
        if len(outs) == 2:
            outs[i][...] = rows
        else:
            half = outs[0].shape[1]
            for chip in range(2):
                even = rows[(2 * chip) * half : (2 * chip + 1) * half]
                odd = rows[(2 * chip + 1) * half : (2 * chip + 2) * half]
                outs[2 * i][chip] = jnp.where(core == 0, even, odd)
                outs[2 * i + 1][chip] = jnp.where(core == 0, odd, even)


CHUNK = 512


def multiply(left, weights, start, stop):
    depth = weights[0].shape[0]
    return sum(
        jnp.dot(
            left[:, i * depth : (i + 1) * depth], w[:, start:stop], preferred_element_type=F32
        )
        for i, w in enumerate(weights)
    )


def send_kernel(
    tile_ref, head_ref, own_ref, y_ref, core_ref, cross_ref, w_ref, wp_ref, a_ref, far_ref
):
    parity = tile_ref[0] & 1
    chip = head_ref[0] >> 1
    deep = a_ref.shape[1]
    for out, which in ((a_ref, chip), (far_ref, 1 - chip)):
        for group, (mine, others) in enumerate(((own_ref, y_ref), (core_ref, cross_ref))):
            base = group * 2 * HD
            out[:, pl.ds(pl.multiple_of(base + parity * HD, HD), HD)] = mine[which]
            out[:, pl.ds(pl.multiple_of(base + (1 - parity) * HD, HD), HD)] = others[which]
    far = far_ref[:, 0:deep]
    term = far_ref.shape[1] - deep
    gathered = w_ref.shape[1] - term
    for start in range(0, term, CHUNK):
        stop = min(start + CHUNK, term)
        far_ref[:, deep + start : deep + stop] = multiply(
            far, (w_ref, wp_ref), gathered + start, gathered + stop
        ).astype(BF16)


def near_kernel(a_ref, w_ref, wp_ref, near_ref):
    own = a_ref[...]
    for start in range(0, w_ref.shape[1], CHUNK):
        near_ref[:, start : start + CHUNK] = multiply(own, (w_ref, wp_ref), start, start + CHUNK)


def last_kernel(tile_ref, near_ref, far_ref, *refs):
    weights, (out_ref, done_ref, sems) = refs[:6], refs[6:]
    parity = tile_ref[0] & 1
    deep = 2 * weights[0].shape[0]
    side = weights[0].shape[1]
    far = far_ref[:, 0:deep]
    gathered = 2 * side + weights[4].shape[1]
    copies = []

    def write(columns):
        copies.append(
            pltpu.make_async_copy(
                done_ref.at[:, columns], out_ref.at[:, columns], sems.at[len(copies)]
            )
        )
        copies[-1].start()

    done_ref[:, gathered:] = (near_ref[:, gathered:] + far_ref[:, deep:].astype(F32)).astype(BF16)
    write(pl.ds(gathered, near_ref.shape[1] - gathered))
    for i, first in enumerate((2 * side, parity * side, (1 - parity) * side)):
        pair = weights[4:6] if i == 0 else weights[2 * i - 2 : 2 * i]
        width = pair[0].shape[1]
        for start in range(0, width, CHUNK):
            stop = min(start + CHUNK, width)
            columns = pl.ds(pl.multiple_of(first + start, HD), stop - start)
            done_ref[:, columns] = (
                near_ref[:, columns] + multiply(far, pair, start, stop)
            ).astype(BF16)
        write(pl.ds(pl.multiple_of(first, HD), width))
    for each in copies:
        each.wait()


def swap_pairs(value, distance, phase):
    count = lax.axis_size("ctx")
    pairs = []
    for i in range(count - 2 * distance):
        if (i // 2 // distance) % 2 == phase:
            pairs += [(i, i + 2 * distance), (i + 2 * distance, i)]
    return lax.ppermute(value, "ctx", pairs)


def swap_tiles(value):
    return lax.ppermute(value, "ctx", [(i, i ^ 1) for i in range(lax.axis_size("ctx"))])


def swap_cores(value):
    return lax.ppermute(value, "head", [(i, i ^ 1) for i in range(lax.axis_size("head"))])


def swap_both(value):
    heads = lax.axis_size("head")
    count = lax.axis_size("ctx") * heads
    pairs = [(i, ((i // heads) ^ 1) * heads + ((i % heads) ^ 1)) for i in range(count)]
    return lax.ppermute(value, ("ctx", "head"), pairs)


def from_chip(value, steps):
    count = lax.axis_size("head")
    return lax.ppermute(value, "head", [((i + 2 * steps) % count, i) for i in range(count)])


def project_any(attended, out_weight, weight_pair, head_index):
    rows, width = attended.shape
    n_head = lax.axis_size("head")
    chips, own_rows = n_head // 2, rows // n_head
    chip, core = head_index // 2, head_index % 2
    blocks = attended.reshape(chips, 2, own_rows, width)
    mine = lax.dynamic_index_in_dim(blocks, core, 1, keepdims=False)
    theirs = lax.dynamic_index_in_dim(blocks, 1 - core, 1, keepdims=False)
    joined = jnp.concatenate([mine, swap_cores(theirs)], axis=2)

    def project(steps):
        block = lax.dynamic_index_in_dim(joined, (chip - steps) % chips, 0, keepdims=False)
        return multiply(block, (out_weight, weight_pair), 0, out_weight.shape[1])

    total = project(0)
    for steps in range(1, chips):
        total = total + from_chip(project(steps).astype(BF16), steps).astype(F32)
    return total.astype(BF16)


def local(queries, keys, values, out_weight, neighbours, counts):
    rows, width = queries.shape
    n_head = lax.axis_size("head")
    own_rows = rows // n_head
    model = out_weight.shape[1]
    small = n_head == 4 and own_rows % 16 == 0
    head_index = lax.axis_index("head").astype(jnp.int32)
    tile, head = lax.axis_index("ctx").astype(jnp.int32).reshape(1), head_index.reshape(1)

    one = (rows, HD)
    payload, kv_shape = shape((3 * rows + FLAGS, HD)), shape((2 * rows, HD))
    keep_q, keep_kv, send, side_weight = call(
        pack_kernel,
        (shape((rows + FLAGS, HD)), kv_shape, payload, shape((width, SIDE))),
        (tile, head, neighbours, counts.reshape(1, 1), queries, keys, values, out_weight),
        scratch=(pltpu.SemaphoreType.DMA((7,)),),
        in_hbm=(4, 5, 6, 7),
        vmem=58,
    )
    weight_ready, _ = lax.optimization_barrier((out_weight, keep_kv))
    weight_pair = swap_cores(weight_ready)
    came = swap_tiles(send)
    kept_near = [swap_pairs(keep_kv, 1, phase) for phase in range(2)]
    if small:
        side_own = from_chip(side_weight, 1)

    held_q, held_kv = call(stage_kernel, (shape((rows + FLAGS, HD)), kv_shape), (keep_q, keep_kv))
    cut = []
    if small:
        ready, _ = lax.optimization_barrier((out_weight, held_q))
        cut.append(
            call(functools.partial(cut_kernel, first=2 * SIDE), shape((width, COMMON)), (ready,))
        )
    came, weight_pair, held_q, held_kv, kept_near, cut = lax.optimization_barrier(
        (came, weight_pair, held_q, held_kv, kept_near, cut)
    )
    far = 1 if lax.axis_size("ctx") <= 8 else 2
    flags, q_pair, came_kv, *to_far = call(
        merge_kernel if far == 2 else functools.partial(merge_kernel, even_ref=None),
        (shape((8, HD), jnp.int32), shape((2,) + one), kv_shape) + (kv_shape,) * far,
        (tile, held_q, held_kv, came),
        0,
    )
    came_near = [swap_pairs(came_kv, 1, phase) for phase in range(2)]
    farther = [swap_pairs(to_far[i], 2, i) for i in range(far)]

    state = shape((2, STATE, rows), F32)
    area = rows * rows
    held = call(
        first_kernel,
        state,
        (flags, tile, q_pair, held_kv, came_kv, *kept_near),
        32 * area * HD,
        8 * area,
    )
    q_again = q_pair
    if small:
        side_own, q_again = lax.optimization_barrier((side_own, q_pair))
        side_other = swap_tiles(side_own)
        ready, _ = lax.optimization_barrier((cut[0], side_own))
        common = from_chip(ready, 1)
    held = call(
        second_kernel,
        state,
        (flags, tile, q_again, *came_near, held),
        16 * area * HD,
        0,
        alias={5: 0},
    )
    block = (2, own_rows, HD)
    attended = call(
        functools.partial(third_kernel, far=far),
        ((shape(block),) * 4 if small else (shape(one),) * 2) + (state,),
        (flags, tile, head, q_pair, held, *farther),
        300 * area * HD,
        0,
        alias={4: 4 if small else 2},
    )[:-1]
    if not small:
        mine, theirs = attended
        got = swap_tiles(theirs)
        even_tile = tile[0] % 2 == 0
        joined = jnp.concatenate(
            [jnp.where(even_tile, mine, got), jnp.where(even_tile, got, mine)], axis=1
        )
        return project_any(joined, out_weight, weight_pair, head_index)

    mine, mine_other, theirs, theirs_other = attended
    from_cross = swap_both(theirs_other)
    from_y = swap_tiles(theirs)
    from_core = swap_cores(mine_other)
    from_cross, from_y, from_core, common, side_other = lax.optimization_barrier(
        (from_cross, from_y, from_core, common, side_other)
    )

    flops = 2 * own_rows * 2 * width * model
    near_weights = (out_weight, weight_pair)
    deep, gathered = 2 * width, 2 * SIDE + COMMON
    own_a, far_a = call(
        send_kernel,
        (shape((own_rows, deep)), shape((own_rows, deep + model - gathered))),
        (tile, head, mine, from_y, from_core, from_cross) + near_weights,
        flops // 4,
        vmem=16,
    )
    got = from_chip(far_a, 1)
    pieces = [side_own, side_other, common]
    *ready, _ = lax.optimization_barrier((*pieces, own_a))
    far_weights = [each for piece, to in zip(pieces, ready) for each in (piece, swap_cores(to))]
    near = call(near_kernel, shape((own_rows, model), F32), (own_a,) + near_weights, 30 * flops, vmem=16)
    return call(
        last_kernel,
        shape((own_rows, model)),
        (tile, near, got, *far_weights),
        flops,
        scratch=(pltpu.VMEM((own_rows, model), BF16), pltpu.SemaphoreType.DMA((4,))),
        out_hbm=True,
        vmem=20,
    )


def solution(mesh):
    placed = (
        P("ctx", "head"),
        P("ctx", "head"),
        P("ctx", "head"),
        P("head", None),
        P("ctx", None),
        P("ctx"),
    )
    return jax.shard_map(
        local, mesh=mesh, in_specs=placed, out_specs=P(("ctx", "head"), None), check_vma=False
    )
```

```python
import functools
import math

import jax
import jax.numpy as jnp
from jax import lax
from jax.experimental import pallas as pl
from jax.experimental.pallas import tpu as pltpu
from jax.sharding import PartitionSpec as P

HD = 128
REACH = 3
NEG = -1e30
FLAGS = 16
SIDE = 1408
COMMON = 1152
STATE = HD + 8
EXPONENT = math.log2(math.e) / math.sqrt(HD)
BF16, F32 = jnp.bfloat16, jnp.float32

SMEM = pl.BlockSpec(memory_space=pltpu.SMEM)
VMEM = pl.BlockSpec(memory_space=pltpu.VMEM)
HBM = pl.BlockSpec(memory_space=pltpu.HBM)


def call(
    kernel, outs, ins, flops=0, exps=0, moved=1 << 20, scratch=(), alias=None, in_hbm=(), out_hbm=False, vmem=8
):
    scalars = [x.dtype == jnp.int32 for x in ins]
    return pl.pallas_call(
        kernel,
        out_shape=outs,
        in_specs=[SMEM if s else (HBM if i in in_hbm else VMEM) for i, s in enumerate(scalars)],
        out_specs=jax.tree.map(lambda _: HBM if out_hbm else VMEM, outs),
        scratch_shapes=list(scratch),
        input_output_aliases=alias or {},
        compiler_params=pltpu.CompilerParams(vmem_limit_bytes=vmem << 20),
        cost_estimate=pl.CostEstimate(flops=flops, bytes_accessed=moved, transcendentals=exps),
    )(*ins)


def shape(dims, dtype=BF16):
    return jax.ShapeDtypeStruct(dims, dtype)


def pack_kernel(
    tile_ref, _, list_ref, count_ref, q_ref, k_ref, v_ref, w_ref,
    keep_q_ref, keep_kv_ref, send_ref, side_ref, sems,
):
    parity = tile_ref[0] & 1
    rows = q_ref.shape[0]
    copies = []

    def copy(source, target):
        copies.append(pltpu.make_async_copy(source, target, sems.at[len(copies)]))
        copies[-1].start()

    for head, kv_out, q_out, q_at in (
        (1 - parity, send_ref, send_ref, 2 * rows),
        (parity, keep_kv_ref, keep_q_ref, 0),
    ):
        columns = pl.ds(pl.multiple_of(head * HD, HD), HD)
        for ref, out, at in ((k_ref, kv_out, 0), (v_ref, kv_out, rows), (q_ref, q_out, q_at)):
            copy(ref.at[:, columns], out.at[pl.ds(at, rows)])
    side = side_ref.shape[1]
    copy(w_ref.at[:, pl.ds(pl.multiple_of(parity * side, HD), side)], side_ref)
    lane = lax.broadcasted_iota(jnp.int32, (FLAGS, HD), 1)
    flags = jnp.zeros((FLAGS, HD), F32)
    for offset in range(-REACH, REACH + 1):
        listed = jnp.int32(0)
        for slot in range(list_ref.shape[1]):
            found = (list_ref[0, slot] == tile_ref[0] + offset) & (slot < count_ref[0, 0])
            listed = jnp.where(found, 1, listed)
        flags = jnp.where(lane == offset + REACH, listed.astype(F32), flags)
    keep_q_ref[rows:, :] = flags.astype(BF16)
    send_ref[3 * rows :, :] = flags.astype(BF16)
    for each in copies:
        each.wait()


def stage_kernel(keep_q_ref, keep_kv_ref, q_ref, kv_ref):
    q_ref[...] = keep_q_ref[...]
    kv_ref[...] = keep_kv_ref[...]


def cut_kernel(w_ref, common_ref, *, first):
    common_ref[...] = w_ref[:, first : first + common_ref.shape[1]]


def merge_kernel(
    tile_ref, keep_q_ref, keep_kv_ref, came_ref, flag_ref, q_ref, kv_ref, odd_ref, even_ref
):
    parity = tile_ref[0] & 1
    rows = q_ref.shape[1]
    kv_ref[...] = came_ref[0 : 2 * rows, :]
    up = (tile_ref[0] & 4) == 0

    def place(out, own):
        @pl.when(own)
        def _():
            out[...] = keep_kv_ref[...]

        @pl.when(jnp.logical_not(own))
        def _():
            out[...] = came_ref[0 : 2 * rows, :]

    place(odd_ref, up == (parity == 1))
    if even_ref is not None:
        place(even_ref, up == (parity == 0))
    q_ref[parity] = keep_q_ref[0:rows, :]
    q_ref[1 - parity] = came_ref[2 * rows : 3 * rows, :]
    own = keep_q_ref[rows:, :].astype(F32)
    other = came_ref[3 * rows :, :].astype(F32)
    even = jnp.where(parity == 0, own, other)[0:8]
    odd = jnp.where(parity == 0, other, own)[0:8]
    row = lax.broadcasted_iota(jnp.int32, (8, HD), 0)
    flag_ref[...] = jnp.where(row == 0, even, odd).astype(jnp.int32)


def step(query, key, value, state_ref, a):
    scores = lax.dot_general(
        key, query, (((1,), (1,)), ((), ())), preferred_element_type=F32
    )
    old = state_ref[a, HD : HD + 1, :]
    new = jnp.maximum(old, jnp.max(scores, axis=0, keepdims=True))
    weights = jnp.exp2((scores - new) * EXPONENT)
    shrink = jnp.exp2((old - new) * EXPONENT)
    state_ref[a, HD : HD + 1, :] = new
    state_ref[a, HD + 1 : HD + 2, :] = state_ref[a, HD + 1 : HD + 2, :] * shrink + jnp.sum(
        weights, axis=0, keepdims=True
    )
    state_ref[a, 0:HD, :] = state_ref[a, 0:HD, :] * shrink + lax.dot_general(
        value, weights.astype(BF16), (((0,), (0,)), ((), ())), preferred_element_type=F32
    )


def visit(flag_ref, q_ref, state_ref, pairs):
    rows = q_ref.shape[1]
    for a, tile, ref in pairs:

        @pl.when(flag_ref[a, tile - a + REACH] > 0)
        def _():
            step(q_ref[a], ref[0:rows, :], ref[rows : 2 * rows, :], state_ref, a)


def visit_pairs(flag_ref, tile_ref, q_ref, state_ref, tiles):
    parity = tile_ref[0] & 1
    for base, own, ref in tiles:
        tile = base + (parity if own else 1 - parity)
        visit(flag_ref, q_ref, state_ref, [(a, tile, ref) for a in range(2)])


def first_kernel(
    flag_ref, tile_ref, q_ref, own_ref, came_ref, kept_first_ref, kept_second_ref, state_ref
):
    state_ref[...] = jnp.zeros_like(state_ref)
    for a in range(2):
        state_ref[a, HD : HD + 1, :] = jnp.full((1, state_ref.shape[2]), NEG, F32)
    base = jnp.where((tile_ref[0] & 2) == 0, 2, -2)
    tiles = [(0, True, own_ref), (0, False, came_ref)]
    tiles += [(base, True, kept_first_ref), (-base, True, kept_second_ref)]
    visit_pairs(flag_ref, tile_ref, q_ref, state_ref, tiles)


def second_kernel(flag_ref, tile_ref, q_ref, first_ref, second_ref, _, state_ref):
    base = jnp.where((tile_ref[0] & 2) == 0, 2, -2)
    tiles = [(base, False, first_ref), (-base, False, second_ref)]
    visit_pairs(flag_ref, tile_ref, q_ref, state_ref, tiles)


def third_kernel(flag_ref, tile_ref, head_ref, q_ref, state_ref, *refs, far):
    outs, last = refs[far:-1], refs[-1]
    for i in range(far):
        above = ((tile_ref[0] & 4) == 0) == (i == 0)
        which = (jnp.where(above, 1, 0), jnp.where(above, 4, -3), refs[i])
        visit(flag_ref, q_ref, last, [which])
    parity = tile_ref[0] & 1
    core = head_ref[0] & 1
    for i, a in enumerate((parity, 1 - parity)):
        done = last[a, 0:HD, :] / last[a, HD + 1 : HD + 2, :]
        rows = done.T.astype(BF16)
        if len(outs) == 2:
            outs[i][...] = rows
        else:
            half = outs[0].shape[1]
            for chip in range(2):
                even = rows[(2 * chip) * half : (2 * chip + 1) * half]
                odd = rows[(2 * chip + 1) * half : (2 * chip + 2) * half]
                outs[2 * i][chip] = jnp.where(core == 0, even, odd)
                outs[2 * i + 1][chip] = jnp.where(core == 0, odd, even)


CHUNK = 512


def multiply(left, weights, start, stop):
    depth = weights[0].shape[0]
    return sum(
        jnp.dot(
            left[:, i * depth : (i + 1) * depth], w[:, start:stop], preferred_element_type=F32
        )
        for i, w in enumerate(weights)
    )


def send_kernel(
    tile_ref, head_ref, own_ref, y_ref, core_ref, cross_ref, w_ref, wp_ref, a_ref, far_ref
):
    parity = tile_ref[0] & 1
    chip = head_ref[0] >> 1
    deep = a_ref.shape[1]
    for out, which in ((a_ref, chip), (far_ref, 1 - chip)):
        for group, (mine, others) in enumerate(((own_ref, y_ref), (core_ref, cross_ref))):
            base = group * 2 * HD
            out[:, pl.ds(pl.multiple_of(base + parity * HD, HD), HD)] = mine[which]
            out[:, pl.ds(pl.multiple_of(base + (1 - parity) * HD, HD), HD)] = others[which]
    far = far_ref[:, 0:deep]
    term = far_ref.shape[1] - deep
    gathered = w_ref.shape[1] - term
    for start in range(0, term, CHUNK):
        stop = min(start + CHUNK, term)
        far_ref[:, deep + start : deep + stop] = multiply(
            far, (w_ref, wp_ref), gathered + start, gathered + stop
        ).astype(BF16)


def near_kernel(a_ref, w_ref, wp_ref, near_ref):
    own = a_ref[...]
    for start in range(0, w_ref.shape[1], CHUNK):
        near_ref[:, start : start + CHUNK] = multiply(own, (w_ref, wp_ref), start, start + CHUNK)


def last_kernel(tile_ref, near_ref, far_ref, *refs):
    weights, (out_ref, done_ref, sems) = refs[:6], refs[6:]
    parity = tile_ref[0] & 1
    deep = 2 * weights[0].shape[0]
    side = weights[0].shape[1]
    far = far_ref[:, 0:deep]
    gathered = 2 * side + weights[4].shape[1]
    copies = []

    def write(columns):
        copies.append(
            pltpu.make_async_copy(
                done_ref.at[:, columns], out_ref.at[:, columns], sems.at[len(copies)]
            )
        )
        copies[-1].start()

    done_ref[:, gathered:] = (near_ref[:, gathered:] + far_ref[:, deep:].astype(F32)).astype(BF16)
    write(pl.ds(gathered, near_ref.shape[1] - gathered))
    for i, first in enumerate((2 * side, parity * side, (1 - parity) * side)):
        pair = weights[4:6] if i == 0 else weights[2 * i - 2 : 2 * i]
        width = pair[0].shape[1]
        for start in range(0, width, CHUNK):
            stop = min(start + CHUNK, width)
            columns = pl.ds(pl.multiple_of(first + start, HD), stop - start)
            done_ref[:, columns] = (
                near_ref[:, columns] + multiply(far, pair, start, stop)
            ).astype(BF16)
        write(pl.ds(pl.multiple_of(first, HD), width))
    for each in copies:
        each.wait()


def swap_pairs(value, distance, phase):
    count = lax.axis_size("ctx")
    pairs = []
    for i in range(count - 2 * distance):
        if (i // 2 // distance) % 2 == phase:
            pairs += [(i, i + 2 * distance), (i + 2 * distance, i)]
    return lax.ppermute(value, "ctx", pairs)


def swap_tiles(value):
    return lax.ppermute(value, "ctx", [(i, i ^ 1) for i in range(lax.axis_size("ctx"))])


def swap_cores(value):
    return lax.ppermute(value, "head", [(i, i ^ 1) for i in range(lax.axis_size("head"))])


def swap_both(value):
    heads = lax.axis_size("head")
    count = lax.axis_size("ctx") * heads
    pairs = [(i, ((i // heads) ^ 1) * heads + ((i % heads) ^ 1)) for i in range(count)]
    return lax.ppermute(value, ("ctx", "head"), pairs)


def from_chip(value, steps):
    count = lax.axis_size("head")
    return lax.ppermute(value, "head", [((i + 2 * steps) % count, i) for i in range(count)])


def project_any(attended, out_weight, weight_pair, head_index):
    rows, width = attended.shape
    n_head = lax.axis_size("head")
    chips, own_rows = n_head // 2, rows // n_head
    chip, core = head_index // 2, head_index % 2
    blocks = attended.reshape(chips, 2, own_rows, width)
    mine = lax.dynamic_index_in_dim(blocks, core, 1, keepdims=False)
    theirs = lax.dynamic_index_in_dim(blocks, 1 - core, 1, keepdims=False)
    joined = jnp.concatenate([mine, swap_cores(theirs)], axis=2)

    def project(steps):
        block = lax.dynamic_index_in_dim(joined, (chip - steps) % chips, 0, keepdims=False)
        return multiply(block, (out_weight, weight_pair), 0, out_weight.shape[1])

    total = project(0)
    for steps in range(1, chips):
        total = total + from_chip(project(steps).astype(BF16), steps).astype(F32)
    return total.astype(BF16)


def local(queries, keys, values, out_weight, neighbours, counts):
    rows, width = queries.shape
    n_head = lax.axis_size("head")
    own_rows = rows // n_head
    model = out_weight.shape[1]
    small = n_head == 4 and own_rows % 16 == 0
    head_index = lax.axis_index("head").astype(jnp.int32)
    tile, head = lax.axis_index("ctx").astype(jnp.int32).reshape(1), head_index.reshape(1)

    one = (rows, HD)
    payload, kv_shape = shape((3 * rows + FLAGS, HD)), shape((2 * rows, HD))
    keep_q, keep_kv, send, side_weight = call(
        pack_kernel,
        (shape((rows + FLAGS, HD)), kv_shape, payload, shape((width, SIDE))),
        (tile, head, neighbours, counts.reshape(1, 1), queries, keys, values, out_weight),
        scratch=(pltpu.SemaphoreType.DMA((7,)),),
        in_hbm=(4, 5, 6, 7),
        vmem=58,
    )
    weight_ready, _ = lax.optimization_barrier((out_weight, keep_kv))
    weight_pair = swap_cores(weight_ready)
    came = swap_tiles(send)
    kept_near = [swap_pairs(keep_kv, 1, phase) for phase in range(2)]
    if small:
        side_own = from_chip(side_weight, 1)

    held_q, held_kv = call(stage_kernel, (shape((rows + FLAGS, HD)), kv_shape), (keep_q, keep_kv))
    cut = []
    if small:
        ready, _ = lax.optimization_barrier((out_weight, held_q))
        cut.append(
            call(functools.partial(cut_kernel, first=2 * SIDE), shape((width, COMMON)), (ready,))
        )
    came, weight_pair, held_q, held_kv, kept_near, cut = lax.optimization_barrier(
        (came, weight_pair, held_q, held_kv, kept_near, cut)
    )
    far = 1 if lax.axis_size("ctx") <= 8 else 2
    flags, q_pair, came_kv, *to_far = call(
        merge_kernel if far == 2 else functools.partial(merge_kernel, even_ref=None),
        (shape((8, HD), jnp.int32), shape((2,) + one), kv_shape) + (kv_shape,) * far,
        (tile, held_q, held_kv, came),
        0,
    )
    came_near = [swap_pairs(came_kv, 1, phase) for phase in range(2)]
    farther = [swap_pairs(to_far[i], 2, i) for i in range(far)]

    state = shape((2, STATE, rows), F32)
    area = rows * rows
    held = call(
        first_kernel,
        state,
        (flags, tile, q_pair, held_kv, came_kv, *kept_near),
        32 * area * HD,
        8 * area,
    )
    q_again = q_pair
    if small:
        side_own, q_again = lax.optimization_barrier((side_own, q_pair))
        side_other = swap_tiles(side_own)
        ready, _ = lax.optimization_barrier((cut[0], side_own))
        common = from_chip(ready, 1)
    held = call(
        second_kernel,
        state,
        (flags, tile, q_again, *came_near, held),
        16 * area * HD,
        0,
        alias={5: 0},
    )
    block = (2, own_rows, HD)
    attended = call(
        functools.partial(third_kernel, far=far),
        ((shape(block),) * 4 if small else (shape(one),) * 2) + (state,),
        (flags, tile, head, q_pair, held, *farther),
        300 * area * HD,
        0,
        alias={4: 4 if small else 2},
    )[:-1]
    if not small:
        mine, theirs = attended
        got = swap_tiles(theirs)
        even_tile = tile[0] % 2 == 0
        joined = jnp.concatenate(
            [jnp.where(even_tile, mine, got), jnp.where(even_tile, got, mine)], axis=1
        )
        return project_any(joined, out_weight, weight_pair, head_index)

    mine, mine_other, theirs, theirs_other = attended
    from_cross = swap_both(theirs_other)
    from_y = swap_tiles(theirs)
    from_core = swap_cores(mine_other)
    from_cross, from_y, from_core, common = lax.optimization_barrier(
        (from_cross, from_y, from_core, common)
    )

    flops = 2 * own_rows * 2 * width * model
    near_weights = (out_weight, weight_pair)
    deep, gathered = 2 * width, 2 * SIDE + COMMON
    own_a, far_a = call(
        send_kernel,
        (shape((own_rows, deep)), shape((own_rows, deep + model - gathered))),
        (tile, head, mine, from_y, from_core, from_cross) + near_weights,
        flops // 4,
        vmem=16,
    )
    got = from_chip(far_a, 1)
    pieces = [side_own, side_other, common]
    *ready, _ = lax.optimization_barrier((*pieces, own_a))
    far_weights = [each for piece, to in zip(pieces, ready) for each in (piece, swap_cores(to))]
    near = call(near_kernel, shape((own_rows, model), F32), (own_a,) + near_weights, 30 * flops, vmem=16)
    return call(
        last_kernel,
        shape((own_rows, model)),
        (tile, near, got, *far_weights),
        flops,
        scratch=(pltpu.VMEM((own_rows, model), BF16), pltpu.SemaphoreType.DMA((4,))),
        out_hbm=True,
        vmem=20,
    )


def solution(mesh):
    placed = (
        P("ctx", "head"),
        P("ctx", "head"),
        P("ctx", "head"),
        P("head", None),
        P("ctx", None),
        P("ctx"),
    )
    return jax.shard_map(
        local, mesh=mesh, in_specs=placed, out_specs=P(("ctx", "head"), None), check_vma=False
    )
```

```python
import functools
import math

import jax
import jax.numpy as jnp
from jax import lax
from jax.experimental import pallas as pl
from jax.experimental.pallas import tpu as pltpu
from jax.sharding import PartitionSpec as P

HD = 128
REACH = 3
NEG = -1e30
FLAGS = 16
SIDE = 1280
COMMON = 1280
STATE = HD + 8
EXPONENT = math.log2(math.e) / math.sqrt(HD)
BF16, F32 = jnp.bfloat16, jnp.float32

SMEM = pl.BlockSpec(memory_space=pltpu.SMEM)
VMEM = pl.BlockSpec(memory_space=pltpu.VMEM)
HBM = pl.BlockSpec(memory_space=pltpu.HBM)


def call(
    kernel, outs, ins, flops=0, exps=0, moved=1 << 20, scratch=(), alias=None, in_hbm=(), out_hbm=False, vmem=8
):
    scalars = [x.dtype == jnp.int32 for x in ins]
    return pl.pallas_call(
        kernel,
        out_shape=outs,
        in_specs=[SMEM if s else (HBM if i in in_hbm else VMEM) for i, s in enumerate(scalars)],
        out_specs=jax.tree.map(lambda _: HBM if out_hbm else VMEM, outs),
        scratch_shapes=list(scratch),
        input_output_aliases=alias or {},
        compiler_params=pltpu.CompilerParams(vmem_limit_bytes=vmem << 20),
        cost_estimate=pl.CostEstimate(flops=flops, bytes_accessed=moved, transcendentals=exps),
    )(*ins)


def shape(dims, dtype=BF16):
    return jax.ShapeDtypeStruct(dims, dtype)


def pack_kernel(
    tile_ref, _, list_ref, count_ref, q_ref, k_ref, v_ref, w_ref,
    keep_q_ref, keep_kv_ref, send_ref, side_ref, sems,
):
    parity = tile_ref[0] & 1
    rows = q_ref.shape[0]
    copies = []

    def copy(source, target):
        copies.append(pltpu.make_async_copy(source, target, sems.at[len(copies)]))
        copies[-1].start()

    for head, kv_out, q_out, q_at in (
        (1 - parity, send_ref, send_ref, 2 * rows),
        (parity, keep_kv_ref, keep_q_ref, 0),
    ):
        columns = pl.ds(pl.multiple_of(head * HD, HD), HD)
        for ref, out, at in ((k_ref, kv_out, 0), (v_ref, kv_out, rows), (q_ref, q_out, q_at)):
            copy(ref.at[:, columns], out.at[pl.ds(at, rows)])
    side = side_ref.shape[1]
    copy(w_ref.at[:, pl.ds(pl.multiple_of(parity * side, HD), side)], side_ref)
    lane = lax.broadcasted_iota(jnp.int32, (FLAGS, HD), 1)
    flags = jnp.zeros((FLAGS, HD), F32)
    for offset in range(-REACH, REACH + 1):
        listed = jnp.int32(0)
        for slot in range(list_ref.shape[1]):
            found = (list_ref[0, slot] == tile_ref[0] + offset) & (slot < count_ref[0, 0])
            listed = jnp.where(found, 1, listed)
        flags = jnp.where(lane == offset + REACH, listed.astype(F32), flags)
    keep_q_ref[rows:, :] = flags.astype(BF16)
    send_ref[3 * rows :, :] = flags.astype(BF16)
    for each in copies:
        each.wait()


def stage_kernel(keep_q_ref, keep_kv_ref, q_ref, kv_ref):
    q_ref[...] = keep_q_ref[...]
    kv_ref[...] = keep_kv_ref[...]


def cut_kernel(w_ref, common_ref, *, first):
    common_ref[...] = w_ref[:, first : first + common_ref.shape[1]]


def merge_kernel(
    tile_ref, keep_q_ref, keep_kv_ref, came_ref, flag_ref, q_ref, kv_ref, odd_ref, even_ref
):
    parity = tile_ref[0] & 1
    rows = q_ref.shape[1]
    kv_ref[...] = came_ref[0 : 2 * rows, :]
    up = (tile_ref[0] & 4) == 0

    def place(out, own):
        @pl.when(own)
        def _():
            out[...] = keep_kv_ref[...]

        @pl.when(jnp.logical_not(own))
        def _():
            out[...] = came_ref[0 : 2 * rows, :]

    place(odd_ref, up == (parity == 1))
    if even_ref is not None:
        place(even_ref, up == (parity == 0))
    q_ref[parity] = keep_q_ref[0:rows, :]
    q_ref[1 - parity] = came_ref[2 * rows : 3 * rows, :]
    own = keep_q_ref[rows:, :].astype(F32)
    other = came_ref[3 * rows :, :].astype(F32)
    even = jnp.where(parity == 0, own, other)[0:8]
    odd = jnp.where(parity == 0, other, own)[0:8]
    row = lax.broadcasted_iota(jnp.int32, (8, HD), 0)
    flag_ref[...] = jnp.where(row == 0, even, odd).astype(jnp.int32)


def step(query, key, value, state_ref, a):
    scores = lax.dot_general(
        key, query, (((1,), (1,)), ((), ())), preferred_element_type=F32
    )
    old = state_ref[a, HD : HD + 1, :]
    new = jnp.maximum(old, jnp.max(scores, axis=0, keepdims=True))
    weights = jnp.exp2((scores - new) * EXPONENT)
    shrink = jnp.exp2((old - new) * EXPONENT)
    state_ref[a, HD : HD + 1, :] = new
    state_ref[a, HD + 1 : HD + 2, :] = state_ref[a, HD + 1 : HD + 2, :] * shrink + jnp.sum(
        weights, axis=0, keepdims=True
    )
    state_ref[a, 0:HD, :] = state_ref[a, 0:HD, :] * shrink + lax.dot_general(
        value, weights.astype(BF16), (((0,), (0,)), ((), ())), preferred_element_type=F32
    )


def visit(flag_ref, q_ref, state_ref, pairs):
    rows = q_ref.shape[1]
    for a, tile, ref in pairs:

        @pl.when(flag_ref[a, tile - a + REACH] > 0)
        def _():
            step(q_ref[a], ref[0:rows, :], ref[rows : 2 * rows, :], state_ref, a)


def visit_pairs(flag_ref, tile_ref, q_ref, state_ref, tiles):
    parity = tile_ref[0] & 1
    for base, own, ref in tiles:
        tile = base + (parity if own else 1 - parity)
        visit(flag_ref, q_ref, state_ref, [(a, tile, ref) for a in range(2)])


def first_kernel(
    flag_ref, tile_ref, q_ref, own_ref, came_ref, kept_first_ref, kept_second_ref, state_ref
):
    state_ref[...] = jnp.zeros_like(state_ref)
    for a in range(2):
        state_ref[a, HD : HD + 1, :] = jnp.full((1, state_ref.shape[2]), NEG, F32)
    base = jnp.where((tile_ref[0] & 2) == 0, 2, -2)
    tiles = [(0, True, own_ref), (0, False, came_ref)]
    tiles += [(base, True, kept_first_ref), (-base, True, kept_second_ref)]
    visit_pairs(flag_ref, tile_ref, q_ref, state_ref, tiles)


def second_kernel(flag_ref, tile_ref, q_ref, first_ref, second_ref, _, state_ref):
    base = jnp.where((tile_ref[0] & 2) == 0, 2, -2)
    tiles = [(base, False, first_ref), (-base, False, second_ref)]
    visit_pairs(flag_ref, tile_ref, q_ref, state_ref, tiles)


def third_kernel(flag_ref, tile_ref, head_ref, q_ref, state_ref, *refs, far):
    outs, last = refs[far:-1], refs[-1]
    for i in range(far):
        above = ((tile_ref[0] & 4) == 0) == (i == 0)
        which = (jnp.where(above, 1, 0), jnp.where(above, 4, -3), refs[i])
        visit(flag_ref, q_ref, last, [which])
    parity = tile_ref[0] & 1
    core = head_ref[0] & 1
    for i, a in enumerate((parity, 1 - parity)):
        done = last[a, 0:HD, :] / last[a, HD + 1 : HD + 2, :]
        rows = done.T.astype(BF16)
        if len(outs) == 2:
            outs[i][...] = rows
        else:
            half = outs[0].shape[1]
            for chip in range(2):
                even = rows[(2 * chip) * half : (2 * chip + 1) * half]
                odd = rows[(2 * chip + 1) * half : (2 * chip + 2) * half]
                outs[2 * i][chip] = jnp.where(core == 0, even, odd)
                outs[2 * i + 1][chip] = jnp.where(core == 0, odd, even)


CHUNK = 512


def multiply(left, weights, start, stop):
    depth = weights[0].shape[0]
    return sum(
        jnp.dot(
            left[:, i * depth : (i + 1) * depth], w[:, start:stop], preferred_element_type=F32
        )
        for i, w in enumerate(weights)
    )


def send_kernel(
    tile_ref, head_ref, own_ref, y_ref, core_ref, cross_ref, w_ref, wp_ref, a_ref, far_ref
):
    parity = tile_ref[0] & 1
    chip = head_ref[0] >> 1
    deep = a_ref.shape[1]
    for out, which in ((a_ref, chip), (far_ref, 1 - chip)):
        for group, (mine, others) in enumerate(((own_ref, y_ref), (core_ref, cross_ref))):
            base = group * 2 * HD
            out[:, pl.ds(pl.multiple_of(base + parity * HD, HD), HD)] = mine[which]
            out[:, pl.ds(pl.multiple_of(base + (1 - parity) * HD, HD), HD)] = others[which]
    far = far_ref[:, 0:deep]
    term = far_ref.shape[1] - deep
    gathered = w_ref.shape[1] - term
    for start in range(0, term, CHUNK):
        stop = min(start + CHUNK, term)
        far_ref[:, deep + start : deep + stop] = multiply(
            far, (w_ref, wp_ref), gathered + start, gathered + stop
        ).astype(BF16)


def near_kernel(a_ref, w_ref, wp_ref, near_ref):
    own = a_ref[...]
    for start in range(0, w_ref.shape[1], CHUNK):
        near_ref[:, start : start + CHUNK] = multiply(own, (w_ref, wp_ref), start, start + CHUNK)


def last_kernel(tile_ref, near_ref, far_ref, *refs):
    weights, (out_ref, done_ref, sems) = refs[:6], refs[6:]
    parity = tile_ref[0] & 1
    deep = 2 * weights[0].shape[0]
    side = weights[0].shape[1]
    far = far_ref[:, 0:deep]
    gathered = 2 * side + weights[4].shape[1]
    copies = []

    def write(columns):
        copies.append(
            pltpu.make_async_copy(
                done_ref.at[:, columns], out_ref.at[:, columns], sems.at[len(copies)]
            )
        )
        copies[-1].start()

    done_ref[:, gathered:] = (near_ref[:, gathered:] + far_ref[:, deep:].astype(F32)).astype(BF16)
    write(pl.ds(gathered, near_ref.shape[1] - gathered))
    for i, first in enumerate((2 * side, parity * side, (1 - parity) * side)):
        pair = weights[4:6] if i == 0 else weights[2 * i - 2 : 2 * i]
        width = pair[0].shape[1]
        for start in range(0, width, CHUNK):
            stop = min(start + CHUNK, width)
            columns = pl.ds(pl.multiple_of(first + start, HD), stop - start)
            done_ref[:, columns] = (
                near_ref[:, columns] + multiply(far, pair, start, stop)
            ).astype(BF16)
        write(pl.ds(pl.multiple_of(first, HD), width))
    for each in copies:
        each.wait()


def swap_pairs(value, distance, phase):
    count = lax.axis_size("ctx")
    pairs = []
    for i in range(count - 2 * distance):
        if (i // 2 // distance) % 2 == phase:
            pairs += [(i, i + 2 * distance), (i + 2 * distance, i)]
    return lax.ppermute(value, "ctx", pairs)


def swap_tiles(value):
    return lax.ppermute(value, "ctx", [(i, i ^ 1) for i in range(lax.axis_size("ctx"))])


def swap_cores(value):
    return lax.ppermute(value, "head", [(i, i ^ 1) for i in range(lax.axis_size("head"))])


def swap_both(value):
    heads = lax.axis_size("head")
    count = lax.axis_size("ctx") * heads
    pairs = [(i, ((i // heads) ^ 1) * heads + ((i % heads) ^ 1)) for i in range(count)]
    return lax.ppermute(value, ("ctx", "head"), pairs)


def from_chip(value, steps):
    count = lax.axis_size("head")
    return lax.ppermute(value, "head", [((i + 2 * steps) % count, i) for i in range(count)])


def project_any(attended, out_weight, weight_pair, head_index):
    rows, width = attended.shape
    n_head = lax.axis_size("head")
    chips, own_rows = n_head // 2, rows // n_head
    chip, core = head_index // 2, head_index % 2
    blocks = attended.reshape(chips, 2, own_rows, width)
    mine = lax.dynamic_index_in_dim(blocks, core, 1, keepdims=False)
    theirs = lax.dynamic_index_in_dim(blocks, 1 - core, 1, keepdims=False)
    joined = jnp.concatenate([mine, swap_cores(theirs)], axis=2)

    def project(steps):
        block = lax.dynamic_index_in_dim(joined, (chip - steps) % chips, 0, keepdims=False)
        return multiply(block, (out_weight, weight_pair), 0, out_weight.shape[1])

    total = project(0)
    for steps in range(1, chips):
        total = total + from_chip(project(steps).astype(BF16), steps).astype(F32)
    return total.astype(BF16)


def local(queries, keys, values, out_weight, neighbours, counts):
    rows, width = queries.shape
    n_head = lax.axis_size("head")
    own_rows = rows // n_head
    model = out_weight.shape[1]
    small = n_head == 4 and own_rows % 16 == 0
    head_index = lax.axis_index("head").astype(jnp.int32)
    tile, head = lax.axis_index("ctx").astype(jnp.int32).reshape(1), head_index.reshape(1)

    one = (rows, HD)
    payload, kv_shape = shape((3 * rows + FLAGS, HD)), shape((2 * rows, HD))
    keep_q, keep_kv, send, side_weight = call(
        pack_kernel,
        (shape((rows + FLAGS, HD)), kv_shape, payload, shape((width, SIDE))),
        (tile, head, neighbours, counts.reshape(1, 1), queries, keys, values, out_weight),
        scratch=(pltpu.SemaphoreType.DMA((7,)),),
        in_hbm=(4, 5, 6, 7),
        vmem=58,
    )
    weight_ready, _ = lax.optimization_barrier((out_weight, keep_kv))
    weight_pair = swap_cores(weight_ready)
    came = swap_tiles(send)
    kept_near = [swap_pairs(keep_kv, 1, phase) for phase in range(2)]
    if small:
        side_own = from_chip(side_weight, 1)

    held_q, held_kv = call(stage_kernel, (shape((rows + FLAGS, HD)), kv_shape), (keep_q, keep_kv))
    cut = []
    if small:
        ready, _ = lax.optimization_barrier((out_weight, held_q))
        cut.append(
            call(functools.partial(cut_kernel, first=2 * SIDE), shape((width, COMMON)), (ready,))
        )
    came, weight_pair, held_q, held_kv, kept_near, cut = lax.optimization_barrier(
        (came, weight_pair, held_q, held_kv, kept_near, cut)
    )
    far = 1 if lax.axis_size("ctx") <= 8 else 2
    flags, q_pair, came_kv, *to_far = call(
        merge_kernel if far == 2 else functools.partial(merge_kernel, even_ref=None),
        (shape((8, HD), jnp.int32), shape((2,) + one), kv_shape) + (kv_shape,) * far,
        (tile, held_q, held_kv, came),
        0,
    )
    came_near = [swap_pairs(came_kv, 1, phase) for phase in range(2)]
    farther = [swap_pairs(to_far[i], 2, i) for i in range(far)]

    state = shape((2, STATE, rows), F32)
    area = rows * rows
    held = call(
        first_kernel,
        state,
        (flags, tile, q_pair, held_kv, came_kv, *kept_near),
        32 * area * HD,
        8 * area,
    )
    q_again = q_pair
    if small:
        side_own, q_again = lax.optimization_barrier((side_own, q_pair))
        side_other = swap_tiles(side_own)
        ready, _ = lax.optimization_barrier((cut[0], side_own))
        common = from_chip(ready, 1)
    held = call(
        second_kernel,
        state,
        (flags, tile, q_again, *came_near, held),
        16 * area * HD,
        0,
        alias={5: 0},
    )
    block = (2, own_rows, HD)
    attended = call(
        functools.partial(third_kernel, far=far),
        ((shape(block),) * 4 if small else (shape(one),) * 2) + (state,),
        (flags, tile, head, q_pair, held, *farther),
        300 * area * HD,
        0,
        alias={4: 4 if small else 2},
    )[:-1]
    if not small:
        mine, theirs = attended
        got = swap_tiles(theirs)
        even_tile = tile[0] % 2 == 0
        joined = jnp.concatenate(
            [jnp.where(even_tile, mine, got), jnp.where(even_tile, got, mine)], axis=1
        )
        return project_any(joined, out_weight, weight_pair, head_index)

    mine, mine_other, theirs, theirs_other = attended
    from_cross = swap_both(theirs_other)
    from_y = swap_tiles(theirs)
    from_core = swap_cores(mine_other)
    from_cross, from_y, from_core, common = lax.optimization_barrier(
        (from_cross, from_y, from_core, common)
    )

    flops = 2 * own_rows * 2 * width * model
    near_weights = (out_weight, weight_pair)
    deep, gathered = 2 * width, 2 * SIDE + COMMON
    own_a, far_a = call(
        send_kernel,
        (shape((own_rows, deep)), shape((own_rows, deep + model - gathered))),
        (tile, head, mine, from_y, from_core, from_cross) + near_weights,
        flops // 4,
        vmem=16,
    )
    got = from_chip(far_a, 1)
    pieces = [side_own, side_other, common]
    *ready, _ = lax.optimization_barrier((*pieces, own_a))
    far_weights = [each for piece, to in zip(pieces, ready) for each in (piece, swap_cores(to))]
    near = call(near_kernel, shape((own_rows, model), F32), (own_a,) + near_weights, 30 * flops, vmem=16)
    return call(
        last_kernel,
        shape((own_rows, model)),
        (tile, near, got, *far_weights),
        flops,
        scratch=(pltpu.VMEM((own_rows, model), BF16), pltpu.SemaphoreType.DMA((4,))),
        out_hbm=True,
        vmem=20,
    )


def solution(mesh):
    placed = (
        P("ctx", "head"),
        P("ctx", "head"),
        P("ctx", "head"),
        P("head", None),
        P("ctx", None),
        P("ctx"),
    )
    return jax.shard_map(
        local, mesh=mesh, in_specs=placed, out_specs=P(("ctx", "head"), None), check_vma=False
    )
```

```python
import functools
import math

import jax
import jax.numpy as jnp
from jax import lax
from jax.experimental import pallas as pl
from jax.experimental.pallas import tpu as pltpu
from jax.sharding import PartitionSpec as P

HD = 128
REACH = 3
NEG = -1e30
FLAGS = 16
SIDE = 1280
COMMON = 1280
STATE = HD + 8
EXPONENT = math.log2(math.e) / math.sqrt(HD)
BF16, F32 = jnp.bfloat16, jnp.float32

SMEM = pl.BlockSpec(memory_space=pltpu.SMEM)
VMEM = pl.BlockSpec(memory_space=pltpu.VMEM)
HBM = pl.BlockSpec(memory_space=pltpu.HBM)


def call(
    kernel, outs, ins, flops=0, exps=0, moved=1 << 20, scratch=(), alias=None, in_hbm=(), out_hbm=False, vmem=8
):
    scalars = [x.dtype == jnp.int32 for x in ins]
    return pl.pallas_call(
        kernel,
        out_shape=outs,
        in_specs=[SMEM if s else (HBM if i in in_hbm else VMEM) for i, s in enumerate(scalars)],
        out_specs=jax.tree.map(lambda _: HBM if out_hbm else VMEM, outs),
        scratch_shapes=list(scratch),
        input_output_aliases=alias or {},
        compiler_params=pltpu.CompilerParams(vmem_limit_bytes=vmem << 20),
        cost_estimate=pl.CostEstimate(flops=flops, bytes_accessed=moved, transcendentals=exps),
    )(*ins)


def shape(dims, dtype=BF16):
    return jax.ShapeDtypeStruct(dims, dtype)


def pack_kernel(
    tile_ref, _, list_ref, count_ref, q_ref, k_ref, v_ref, w_ref,
    keep_q_ref, keep_kv_ref, send_ref, side_ref,
    keep_q, keep_kv, send, side, in_sems, out_sems,
):
    parity = tile_ref[0] & 1
    rows = q_ref.shape[0]
    reads, writes = [], []

    def read(source, target):
        reads.append(pltpu.make_async_copy(source, target, in_sems.at[len(reads)]))
        reads[-1].start()

    def write(count, source, target):
        for each in reads[len(reads) - left[0] :][:count]:
            each.wait()
        left[0] -= count
        writes.append(pltpu.make_async_copy(source, target, out_sems.at[len(writes)]))
        writes[-1].start()

    for head, kv_out, q_out, q_at in ((1 - parity, send, send, 2 * rows), (parity, keep_kv, keep_q, 0)):
        columns = pl.ds(pl.multiple_of(head * HD, HD), HD)
        for ref, out, at in ((k_ref, kv_out, 0), (v_ref, kv_out, rows), (q_ref, q_out, q_at)):
            read(ref.at[:, columns], out.at[pl.ds(at, rows)])
    width = side.shape[1]
    read(w_ref.at[:, pl.ds(pl.multiple_of(parity * width, HD), width)], side)
    lane = lax.broadcasted_iota(jnp.int32, (FLAGS, HD), 1)
    flags = jnp.zeros((FLAGS, HD), F32)
    for offset in range(-REACH, REACH + 1):
        listed = jnp.int32(0)
        for slot in range(list_ref.shape[1]):
            found = (list_ref[0, slot] == tile_ref[0] + offset) & (slot < count_ref[0, 0])
            listed = jnp.where(found, 1, listed)
        flags = jnp.where(lane == offset + REACH, listed.astype(F32), flags)
    keep_q[rows:, :] = flags.astype(BF16)
    send[3 * rows :, :] = flags.astype(BF16)
    left = [len(reads)]
    write(3, send, send_ref)
    write(2, keep_kv, keep_kv_ref)
    write(1, keep_q, keep_q_ref)
    write(1, side, side_ref)
    for each in writes:
        each.wait()


def stage_kernel(keep_q_ref, keep_kv_ref, q_ref, kv_ref):
    q_ref[...] = keep_q_ref[...]
    kv_ref[...] = keep_kv_ref[...]


def cut_kernel(w_ref, common_ref, *, first):
    common_ref[...] = w_ref[:, first : first + common_ref.shape[1]]


def merge_kernel(
    tile_ref, keep_q_ref, keep_kv_ref, came_ref, flag_ref, q_ref, kv_ref, odd_ref, even_ref
):
    parity = tile_ref[0] & 1
    rows = q_ref.shape[1]
    kv_ref[...] = came_ref[0 : 2 * rows, :]
    up = (tile_ref[0] & 4) == 0

    def place(out, own):
        @pl.when(own)
        def _():
            out[...] = keep_kv_ref[...]

        @pl.when(jnp.logical_not(own))
        def _():
            out[...] = came_ref[0 : 2 * rows, :]

    place(odd_ref, up == (parity == 1))
    if even_ref is not None:
        place(even_ref, up == (parity == 0))
    q_ref[parity] = keep_q_ref[0:rows, :]
    q_ref[1 - parity] = came_ref[2 * rows : 3 * rows, :]
    own = keep_q_ref[rows:, :].astype(F32)
    other = came_ref[3 * rows :, :].astype(F32)
    even = jnp.where(parity == 0, own, other)[0:8]
    odd = jnp.where(parity == 0, other, own)[0:8]
    row = lax.broadcasted_iota(jnp.int32, (8, HD), 0)
    flag_ref[...] = jnp.where(row == 0, even, odd).astype(jnp.int32)


def step(query, key, value, state_ref, a):
    scores = lax.dot_general(
        key, query, (((1,), (1,)), ((), ())), preferred_element_type=F32
    )
    old = state_ref[a, HD : HD + 1, :]
    new = jnp.maximum(old, jnp.max(scores, axis=0, keepdims=True))
    weights = jnp.exp2((scores - new) * EXPONENT)
    shrink = jnp.exp2((old - new) * EXPONENT)
    state_ref[a, HD : HD + 1, :] = new
    state_ref[a, HD + 1 : HD + 2, :] = state_ref[a, HD + 1 : HD + 2, :] * shrink + jnp.sum(
        weights, axis=0, keepdims=True
    )
    state_ref[a, 0:HD, :] = state_ref[a, 0:HD, :] * shrink + lax.dot_general(
        value, weights.astype(BF16), (((0,), (0,)), ((), ())), preferred_element_type=F32
    )


def visit(flag_ref, q_ref, state_ref, pairs):
    rows = q_ref.shape[1]
    for a, tile, ref in pairs:

        @pl.when(flag_ref[a, tile - a + REACH] > 0)
        def _():
            step(q_ref[a], ref[0:rows, :], ref[rows : 2 * rows, :], state_ref, a)


def visit_pairs(flag_ref, tile_ref, q_ref, state_ref, tiles):
    parity = tile_ref[0] & 1
    for base, own, ref in tiles:
        tile = base + (parity if own else 1 - parity)
        visit(flag_ref, q_ref, state_ref, [(a, tile, ref) for a in range(2)])


def first_kernel(
    flag_ref, tile_ref, q_ref, own_ref, came_ref, kept_first_ref, kept_second_ref, state_ref
):
    state_ref[...] = jnp.zeros_like(state_ref)
    for a in range(2):
        state_ref[a, HD : HD + 1, :] = jnp.full((1, state_ref.shape[2]), NEG, F32)
    base = jnp.where((tile_ref[0] & 2) == 0, 2, -2)
    tiles = [(0, True, own_ref), (0, False, came_ref)]
    tiles += [(base, True, kept_first_ref), (-base, True, kept_second_ref)]
    visit_pairs(flag_ref, tile_ref, q_ref, state_ref, tiles)


def second_kernel(flag_ref, tile_ref, q_ref, first_ref, second_ref, _, state_ref):
    base = jnp.where((tile_ref[0] & 2) == 0, 2, -2)
    tiles = [(base, False, first_ref), (-base, False, second_ref)]
    visit_pairs(flag_ref, tile_ref, q_ref, state_ref, tiles)


def third_kernel(flag_ref, tile_ref, head_ref, q_ref, state_ref, *refs, far):
    outs, last = refs[far:-1], refs[-1]
    for i in range(far):
        above = ((tile_ref[0] & 4) == 0) == (i == 0)
        which = (jnp.where(above, 1, 0), jnp.where(above, 4, -3), refs[i])
        visit(flag_ref, q_ref, last, [which])
    parity = tile_ref[0] & 1
    core = head_ref[0] & 1
    for i, a in enumerate((parity, 1 - parity)):
        done = last[a, 0:HD, :] / last[a, HD + 1 : HD + 2, :]
        rows = done.T.astype(BF16)
        if len(outs) == 2:
            outs[i][...] = rows
        else:
            half = outs[0].shape[1]
            for chip in range(2):
                even = rows[(2 * chip) * half : (2 * chip + 1) * half]
                odd = rows[(2 * chip + 1) * half : (2 * chip + 2) * half]
                outs[2 * i][chip] = jnp.where(core == 0, even, odd)
                outs[2 * i + 1][chip] = jnp.where(core == 0, odd, even)


CHUNK = 512


def multiply(left, weights, start, stop):
    depth = weights[0].shape[0]
    return sum(
        jnp.dot(
            left[:, i * depth : (i + 1) * depth], w[:, start:stop], preferred_element_type=F32
        )
        for i, w in enumerate(weights)
    )


def send_kernel(
    tile_ref, head_ref, own_ref, y_ref, core_ref, cross_ref, w_ref, wp_ref, a_ref, far_ref
):
    parity = tile_ref[0] & 1
    chip = head_ref[0] >> 1
    deep = a_ref.shape[1]
    for out, which in ((a_ref, chip), (far_ref, 1 - chip)):
        for group, (mine, others) in enumerate(((own_ref, y_ref), (core_ref, cross_ref))):
            base = group * 2 * HD
            out[:, pl.ds(pl.multiple_of(base + parity * HD, HD), HD)] = mine[which]
            out[:, pl.ds(pl.multiple_of(base + (1 - parity) * HD, HD), HD)] = others[which]
    far = far_ref[:, 0:deep]
    term = far_ref.shape[1] - deep
    gathered = w_ref.shape[1] - term
    for start in range(0, term, CHUNK):
        stop = min(start + CHUNK, term)
        far_ref[:, deep + start : deep + stop] = multiply(
            far, (w_ref, wp_ref), gathered + start, gathered + stop
        ).astype(BF16)


def near_kernel(a_ref, w_ref, wp_ref, near_ref):
    own = a_ref[...]
    for start in range(0, w_ref.shape[1], CHUNK):
        near_ref[:, start : start + CHUNK] = multiply(own, (w_ref, wp_ref), start, start + CHUNK)


def last_kernel(tile_ref, near_ref, far_ref, *refs):
    weights, (out_ref, done_ref, sems) = refs[:6], refs[6:]
    parity = tile_ref[0] & 1
    deep = 2 * weights[0].shape[0]
    side = weights[0].shape[1]
    far = far_ref[:, 0:deep]
    gathered = 2 * side + weights[4].shape[1]
    copies = []

    def write(columns):
        copies.append(
            pltpu.make_async_copy(
                done_ref.at[:, columns], out_ref.at[:, columns], sems.at[len(copies)]
            )
        )
        copies[-1].start()

    done_ref[:, gathered:] = (near_ref[:, gathered:] + far_ref[:, deep:].astype(F32)).astype(BF16)
    write(pl.ds(gathered, near_ref.shape[1] - gathered))
    for i, first in enumerate((2 * side, parity * side, (1 - parity) * side)):
        pair = weights[4:6] if i == 0 else weights[2 * i - 2 : 2 * i]
        width = pair[0].shape[1]
        for start in range(0, width, CHUNK):
            stop = min(start + CHUNK, width)
            columns = pl.ds(pl.multiple_of(first + start, HD), stop - start)
            done_ref[:, columns] = (
                near_ref[:, columns] + multiply(far, pair, start, stop)
            ).astype(BF16)
        write(pl.ds(pl.multiple_of(first, HD), width))
    for each in copies:
        each.wait()


def swap_pairs(value, distance, phase):
    count = lax.axis_size("ctx")
    pairs = []
    for i in range(count - 2 * distance):
        if (i // 2 // distance) % 2 == phase:
            pairs += [(i, i + 2 * distance), (i + 2 * distance, i)]
    return lax.ppermute(value, "ctx", pairs)


def swap_tiles(value):
    return lax.ppermute(value, "ctx", [(i, i ^ 1) for i in range(lax.axis_size("ctx"))])


def swap_cores(value):
    return lax.ppermute(value, "head", [(i, i ^ 1) for i in range(lax.axis_size("head"))])


def swap_both(value):
    heads = lax.axis_size("head")
    count = lax.axis_size("ctx") * heads
    pairs = [(i, ((i // heads) ^ 1) * heads + ((i % heads) ^ 1)) for i in range(count)]
    return lax.ppermute(value, ("ctx", "head"), pairs)


def from_chip(value, steps):
    count = lax.axis_size("head")
    return lax.ppermute(value, "head", [((i + 2 * steps) % count, i) for i in range(count)])


def project_any(attended, out_weight, weight_pair, head_index):
    rows, width = attended.shape
    n_head = lax.axis_size("head")
    chips, own_rows = n_head // 2, rows // n_head
    chip, core = head_index // 2, head_index % 2
    blocks = attended.reshape(chips, 2, own_rows, width)
    mine = lax.dynamic_index_in_dim(blocks, core, 1, keepdims=False)
    theirs = lax.dynamic_index_in_dim(blocks, 1 - core, 1, keepdims=False)
    joined = jnp.concatenate([mine, swap_cores(theirs)], axis=2)

    def project(steps):
        block = lax.dynamic_index_in_dim(joined, (chip - steps) % chips, 0, keepdims=False)
        return multiply(block, (out_weight, weight_pair), 0, out_weight.shape[1])

    total = project(0)
    for steps in range(1, chips):
        total = total + from_chip(project(steps).astype(BF16), steps).astype(F32)
    return total.astype(BF16)


def local(queries, keys, values, out_weight, neighbours, counts):
    rows, width = queries.shape
    n_head = lax.axis_size("head")
    own_rows = rows // n_head
    model = out_weight.shape[1]
    small = n_head == 4 and own_rows % 16 == 0
    head_index = lax.axis_index("head").astype(jnp.int32)
    tile, head = lax.axis_index("ctx").astype(jnp.int32).reshape(1), head_index.reshape(1)

    one = (rows, HD)
    payload, kv_shape = shape((3 * rows + FLAGS, HD)), shape((2 * rows, HD))
    packed = (shape((rows + FLAGS, HD)), kv_shape, payload, shape((width, SIDE)))
    keep_q, keep_kv, send, side_weight = call(
        pack_kernel,
        packed,
        (tile, head, neighbours, counts.reshape(1, 1), queries, keys, values, out_weight),
        scratch=[pltpu.VMEM(each.shape, each.dtype) for each in packed]
        + [pltpu.SemaphoreType.DMA((7,)), pltpu.SemaphoreType.DMA((4,))],
        in_hbm=(4, 5, 6, 7),
        out_hbm=True,
        vmem=58,
    )
    weight_ready, _ = lax.optimization_barrier((out_weight, keep_kv))
    weight_pair = swap_cores(weight_ready)
    came = swap_tiles(send)
    kept_near = [swap_pairs(keep_kv, 1, phase) for phase in range(2)]
    if small:
        side_own = from_chip(side_weight, 1)

    held_q, held_kv = call(stage_kernel, (shape((rows + FLAGS, HD)), kv_shape), (keep_q, keep_kv))
    cut = []
    if small:
        ready, _ = lax.optimization_barrier((out_weight, held_q))
        cut.append(
            call(functools.partial(cut_kernel, first=2 * SIDE), shape((width, COMMON)), (ready,))
        )
    came, weight_pair, held_q, held_kv, kept_near, cut = lax.optimization_barrier(
        (came, weight_pair, held_q, held_kv, kept_near, cut)
    )
    far = 1 if lax.axis_size("ctx") <= 8 else 2
    flags, q_pair, came_kv, *to_far = call(
        merge_kernel if far == 2 else functools.partial(merge_kernel, even_ref=None),
        (shape((8, HD), jnp.int32), shape((2,) + one), kv_shape) + (kv_shape,) * far,
        (tile, held_q, held_kv, came),
        0,
    )
    came_near = [swap_pairs(came_kv, 1, phase) for phase in range(2)]
    farther = [swap_pairs(to_far[i], 2, i) for i in range(far)]

    state = shape((2, STATE, rows), F32)
    area = rows * rows
    held = call(
        first_kernel,
        state,
        (flags, tile, q_pair, held_kv, came_kv, *kept_near),
        32 * area * HD,
        8 * area,
    )
    q_again = q_pair
    if small:
        side_own, q_again = lax.optimization_barrier((side_own, q_pair))
        side_other = swap_tiles(side_own)
        ready, _ = lax.optimization_barrier((cut[0], side_own))
        common = from_chip(ready, 1)
    held = call(
        second_kernel,
        state,
        (flags, tile, q_again, *came_near, held),
        16 * area * HD,
        0,
        alias={5: 0},
    )
    block = (2, own_rows, HD)
    attended = call(
        functools.partial(third_kernel, far=far),
        ((shape(block),) * 4 if small else (shape(one),) * 2) + (state,),
        (flags, tile, head, q_pair, held, *farther),
        300 * area * HD,
        0,
        alias={4: 4 if small else 2},
    )[:-1]
    if not small:
        mine, theirs = attended
        got = swap_tiles(theirs)
        even_tile = tile[0] % 2 == 0
        joined = jnp.concatenate(
            [jnp.where(even_tile, mine, got), jnp.where(even_tile, got, mine)], axis=1
        )
        return project_any(joined, out_weight, weight_pair, head_index)

    mine, mine_other, theirs, theirs_other = attended
    from_cross = swap_both(theirs_other)
    from_y = swap_tiles(theirs)
    from_core = swap_cores(mine_other)
    from_cross, from_y, from_core, common = lax.optimization_barrier(
        (from_cross, from_y, from_core, common)
    )

    flops = 2 * own_rows * 2 * width * model
    near_weights = (out_weight, weight_pair)
    deep, gathered = 2 * width, 2 * SIDE + COMMON
    own_a, far_a = call(
        send_kernel,
        (shape((own_rows, deep)), shape((own_rows, deep + model - gathered))),
        (tile, head, mine, from_y, from_core, from_cross) + near_weights,
        flops // 4,
        vmem=16,
    )
    got = from_chip(far_a, 1)
    pieces = [side_own, side_other, common]
    *ready, _ = lax.optimization_barrier((*pieces, own_a))
    far_weights = [each for piece, to in zip(pieces, ready) for each in (piece, swap_cores(to))]
    near = call(near_kernel, shape((own_rows, model), F32), (own_a,) + near_weights, 30 * flops, vmem=16)
    return call(
        last_kernel,
        shape((own_rows, model)),
        (tile, near, got, *far_weights),
        flops,
        scratch=(pltpu.VMEM((own_rows, model), BF16), pltpu.SemaphoreType.DMA((4,))),
        out_hbm=True,
        vmem=20,
    )


def solution(mesh):
    placed = (
        P("ctx", "head"),
        P("ctx", "head"),
        P("ctx", "head"),
        P("head", None),
        P("ctx", None),
        P("ctx"),
    )
    return jax.shard_map(
        local, mesh=mesh, in_specs=placed, out_specs=P(("ctx", "head"), None), check_vma=False
    )
```

```python
import functools
import math

import jax
import jax.numpy as jnp
from jax import lax
from jax.experimental import pallas as pl
from jax.experimental.pallas import tpu as pltpu
from jax.sharding import PartitionSpec as P

HD = 128
REACH = 3
NEG = -1e30
FLAGS = 16
SIDE = 1280
COMMON = 1280
STATE = HD + 8
EXPONENT = math.log2(math.e) / math.sqrt(HD)
BF16, F32 = jnp.bfloat16, jnp.float32

SMEM = pl.BlockSpec(memory_space=pltpu.SMEM)
VMEM = pl.BlockSpec(memory_space=pltpu.VMEM)
HBM = pl.BlockSpec(memory_space=pltpu.HBM)


def call(
    kernel, outs, ins, flops=0, exps=0, moved=1 << 20, scratch=(), alias=None, in_hbm=(), out_hbm=False, vmem=8
):
    scalars = [x.dtype == jnp.int32 for x in ins]
    return pl.pallas_call(
        kernel,
        out_shape=outs,
        in_specs=[SMEM if s else (HBM if i in in_hbm else VMEM) for i, s in enumerate(scalars)],
        out_specs=jax.tree.map(lambda _: HBM if out_hbm else VMEM, outs),
        scratch_shapes=list(scratch),
        input_output_aliases=alias or {},
        compiler_params=pltpu.CompilerParams(vmem_limit_bytes=vmem << 20),
        cost_estimate=pl.CostEstimate(flops=flops, bytes_accessed=moved, transcendentals=exps),
    )(*ins)


def shape(dims, dtype=BF16):
    return jax.ShapeDtypeStruct(dims, dtype)


def pack_kernel(
    tile_ref, _, list_ref, count_ref, q_ref, k_ref, v_ref, __,
    keep_q_ref, keep_kv_ref, send_ref,
    keep_q, keep_kv, send, in_sems, out_sems,
):
    parity = tile_ref[0] & 1
    rows = q_ref.shape[0]
    reads, writes = [], []

    def read(source, target):
        reads.append(pltpu.make_async_copy(source, target, in_sems.at[len(reads)]))
        reads[-1].start()

    def write(count, source, target):
        for each in reads[len(reads) - left[0] :][:count]:
            each.wait()
        left[0] -= count
        writes.append(pltpu.make_async_copy(source, target, out_sems.at[len(writes)]))
        writes[-1].start()

    for head, kv_out, q_out, q_at in ((1 - parity, send, send, 2 * rows), (parity, keep_kv, keep_q, 0)):
        columns = pl.ds(pl.multiple_of(head * HD, HD), HD)
        for ref, out, at in ((k_ref, kv_out, 0), (v_ref, kv_out, rows), (q_ref, q_out, q_at)):
            read(ref.at[:, columns], out.at[pl.ds(at, rows)])
    lane = lax.broadcasted_iota(jnp.int32, (FLAGS, HD), 1)
    flags = jnp.zeros((FLAGS, HD), F32)
    for offset in range(-REACH, REACH + 1):
        listed = jnp.int32(0)
        for slot in range(list_ref.shape[1]):
            found = (list_ref[0, slot] == tile_ref[0] + offset) & (slot < count_ref[0, 0])
            listed = jnp.where(found, 1, listed)
        flags = jnp.where(lane == offset + REACH, listed.astype(F32), flags)
    keep_q[rows:, :] = flags.astype(BF16)
    send[3 * rows :, :] = flags.astype(BF16)
    left = [len(reads)]
    write(3, send, send_ref)
    write(2, keep_kv, keep_kv_ref)
    write(1, keep_q, keep_q_ref)
    for each in writes:
        each.wait()


def stage_kernel(keep_q_ref, keep_kv_ref, q_ref, kv_ref):
    q_ref[...] = keep_q_ref[...]
    kv_ref[...] = keep_kv_ref[...]


def side_kernel(tile_ref, w_ref, side_ref):
    side = side_ref.shape[1]
    side_ref[...] = w_ref[:, pl.ds(pl.multiple_of((tile_ref[0] & 1) * side, HD), side)]


def cut_kernel(w_ref, common_ref, *, first):
    common_ref[...] = w_ref[:, first : first + common_ref.shape[1]]


def merge_kernel(
    tile_ref, keep_q_ref, keep_kv_ref, came_ref, flag_ref, q_ref, kv_ref, odd_ref, even_ref
):
    parity = tile_ref[0] & 1
    rows = q_ref.shape[1]
    kv_ref[...] = came_ref[0 : 2 * rows, :]
    up = (tile_ref[0] & 4) == 0

    def place(out, own):
        @pl.when(own)
        def _():
            out[...] = keep_kv_ref[...]

        @pl.when(jnp.logical_not(own))
        def _():
            out[...] = came_ref[0 : 2 * rows, :]

    place(odd_ref, up == (parity == 1))
    if even_ref is not None:
        place(even_ref, up == (parity == 0))
    q_ref[parity] = keep_q_ref[0:rows, :]
    q_ref[1 - parity] = came_ref[2 * rows : 3 * rows, :]
    own = keep_q_ref[rows:, :].astype(F32)
    other = came_ref[3 * rows :, :].astype(F32)
    even = jnp.where(parity == 0, own, other)[0:8]
    odd = jnp.where(parity == 0, other, own)[0:8]
    row = lax.broadcasted_iota(jnp.int32, (8, HD), 0)
    flag_ref[...] = jnp.where(row == 0, even, odd).astype(jnp.int32)


def step(query, key, value, state_ref, a):
    scores = lax.dot_general(
        key, query, (((1,), (1,)), ((), ())), preferred_element_type=F32
    )
    old = state_ref[a, HD : HD + 1, :]
    new = jnp.maximum(old, jnp.max(scores, axis=0, keepdims=True))
    weights = jnp.exp2((scores - new) * EXPONENT)
    shrink = jnp.exp2((old - new) * EXPONENT)
    state_ref[a, HD : HD + 1, :] = new
    state_ref[a, HD + 1 : HD + 2, :] = state_ref[a, HD + 1 : HD + 2, :] * shrink + jnp.sum(
        weights, axis=0, keepdims=True
    )
    state_ref[a, 0:HD, :] = state_ref[a, 0:HD, :] * shrink + lax.dot_general(
        value, weights.astype(BF16), (((0,), (0,)), ((), ())), preferred_element_type=F32
    )


def visit(flag_ref, q_ref, state_ref, pairs):
    rows = q_ref.shape[1]
    for a, tile, ref in pairs:

        @pl.when(flag_ref[a, tile - a + REACH] > 0)
        def _():
            step(q_ref[a], ref[0:rows, :], ref[rows : 2 * rows, :], state_ref, a)


def visit_pairs(flag_ref, tile_ref, q_ref, state_ref, tiles):
    parity = tile_ref[0] & 1
    for base, own, ref in tiles:
        tile = base + (parity if own else 1 - parity)
        visit(flag_ref, q_ref, state_ref, [(a, tile, ref) for a in range(2)])


def first_kernel(
    flag_ref, tile_ref, q_ref, own_ref, came_ref, kept_first_ref, kept_second_ref, state_ref
):
    state_ref[...] = jnp.zeros_like(state_ref)
    for a in range(2):
        state_ref[a, HD : HD + 1, :] = jnp.full((1, state_ref.shape[2]), NEG, F32)
    base = jnp.where((tile_ref[0] & 2) == 0, 2, -2)
    tiles = [(0, True, own_ref), (0, False, came_ref)]
    tiles += [(base, True, kept_first_ref), (-base, True, kept_second_ref)]
    visit_pairs(flag_ref, tile_ref, q_ref, state_ref, tiles)


def second_kernel(flag_ref, tile_ref, q_ref, first_ref, second_ref, _, state_ref):
    base = jnp.where((tile_ref[0] & 2) == 0, 2, -2)
    tiles = [(base, False, first_ref), (-base, False, second_ref)]
    visit_pairs(flag_ref, tile_ref, q_ref, state_ref, tiles)


def third_kernel(flag_ref, tile_ref, head_ref, q_ref, state_ref, *refs, far):
    outs, last = refs[far:-1], refs[-1]
    for i in range(far):
        above = ((tile_ref[0] & 4) == 0) == (i == 0)
        which = (jnp.where(above, 1, 0), jnp.where(above, 4, -3), refs[i])
        visit(flag_ref, q_ref, last, [which])
    parity = tile_ref[0] & 1
    core = head_ref[0] & 1
    for i, a in enumerate((parity, 1 - parity)):
        done = last[a, 0:HD, :] / last[a, HD + 1 : HD + 2, :]
        rows = done.T.astype(BF16)
        if len(outs) == 2:
            outs[i][...] = rows
        else:
            half = outs[0].shape[1]
            for chip in range(2):
                even = rows[(2 * chip) * half : (2 * chip + 1) * half]
                odd = rows[(2 * chip + 1) * half : (2 * chip + 2) * half]
                outs[2 * i][chip] = jnp.where(core == 0, even, odd)
                outs[2 * i + 1][chip] = jnp.where(core == 0, odd, even)


CHUNK = 512


def multiply(left, weights, start, stop):
    depth = weights[0].shape[0]
    return sum(
        jnp.dot(
            left[:, i * depth : (i + 1) * depth], w[:, start:stop], preferred_element_type=F32
        )
        for i, w in enumerate(weights)
    )


def send_kernel(
    tile_ref, head_ref, own_ref, y_ref, core_ref, cross_ref, w_ref, wp_ref, a_ref, far_ref
):
    parity = tile_ref[0] & 1
    chip = head_ref[0] >> 1
    deep = a_ref.shape[1]
    for out, which in ((a_ref, chip), (far_ref, 1 - chip)):
        for group, (mine, others) in enumerate(((own_ref, y_ref), (core_ref, cross_ref))):
            base = group * 2 * HD
            out[:, pl.ds(pl.multiple_of(base + parity * HD, HD), HD)] = mine[which]
            out[:, pl.ds(pl.multiple_of(base + (1 - parity) * HD, HD), HD)] = others[which]
    far = far_ref[:, 0:deep]
    term = far_ref.shape[1] - deep
    gathered = w_ref.shape[1] - term
    for start in range(0, term, CHUNK):
        stop = min(start + CHUNK, term)
        far_ref[:, deep + start : deep + stop] = multiply(
            far, (w_ref, wp_ref), gathered + start, gathered + stop
        ).astype(BF16)


def near_kernel(a_ref, w_ref, wp_ref, near_ref):
    own = a_ref[...]
    for start in range(0, w_ref.shape[1], CHUNK):
        near_ref[:, start : start + CHUNK] = multiply(own, (w_ref, wp_ref), start, start + CHUNK)


def last_kernel(tile_ref, near_ref, far_ref, *refs):
    weights, (out_ref, done_ref, sems) = refs[:6], refs[6:]
    parity = tile_ref[0] & 1
    deep = 2 * weights[0].shape[0]
    side = weights[0].shape[1]
    far = far_ref[:, 0:deep]
    gathered = 2 * side + weights[4].shape[1]
    copies = []

    def write(columns):
        copies.append(
            pltpu.make_async_copy(
                done_ref.at[:, columns], out_ref.at[:, columns], sems.at[len(copies)]
            )
        )
        copies[-1].start()

    done_ref[:, gathered:] = (near_ref[:, gathered:] + far_ref[:, deep:].astype(F32)).astype(BF16)
    write(pl.ds(gathered, near_ref.shape[1] - gathered))
    for i, first in enumerate((2 * side, parity * side, (1 - parity) * side)):
        pair = weights[4:6] if i == 0 else weights[2 * i - 2 : 2 * i]
        width = pair[0].shape[1]
        for start in range(0, width, CHUNK):
            stop = min(start + CHUNK, width)
            columns = pl.ds(pl.multiple_of(first + start, HD), stop - start)
            done_ref[:, columns] = (
                near_ref[:, columns] + multiply(far, pair, start, stop)
            ).astype(BF16)
        write(pl.ds(pl.multiple_of(first, HD), width))
    for each in copies:
        each.wait()


def swap_pairs(value, distance, phase):
    count = lax.axis_size("ctx")
    pairs = []
    for i in range(count - 2 * distance):
        if (i // 2 // distance) % 2 == phase:
            pairs += [(i, i + 2 * distance), (i + 2 * distance, i)]
    return lax.ppermute(value, "ctx", pairs)


def swap_tiles(value):
    return lax.ppermute(value, "ctx", [(i, i ^ 1) for i in range(lax.axis_size("ctx"))])


def swap_cores(value):
    return lax.ppermute(value, "head", [(i, i ^ 1) for i in range(lax.axis_size("head"))])


def swap_both(value):
    heads = lax.axis_size("head")
    count = lax.axis_size("ctx") * heads
    pairs = [(i, ((i // heads) ^ 1) * heads + ((i % heads) ^ 1)) for i in range(count)]
    return lax.ppermute(value, ("ctx", "head"), pairs)


def from_chip(value, steps):
    count = lax.axis_size("head")
    return lax.ppermute(value, "head", [((i + 2 * steps) % count, i) for i in range(count)])


def project_any(attended, out_weight, weight_pair, head_index):
    rows, width = attended.shape
    n_head = lax.axis_size("head")
    chips, own_rows = n_head // 2, rows // n_head
    chip, core = head_index // 2, head_index % 2
    blocks = attended.reshape(chips, 2, own_rows, width)
    mine = lax.dynamic_index_in_dim(blocks, core, 1, keepdims=False)
    theirs = lax.dynamic_index_in_dim(blocks, 1 - core, 1, keepdims=False)
    joined = jnp.concatenate([mine, swap_cores(theirs)], axis=2)

    def project(steps):
        block = lax.dynamic_index_in_dim(joined, (chip - steps) % chips, 0, keepdims=False)
        return multiply(block, (out_weight, weight_pair), 0, out_weight.shape[1])

    total = project(0)
    for steps in range(1, chips):
        total = total + from_chip(project(steps).astype(BF16), steps).astype(F32)
    return total.astype(BF16)


def local(queries, keys, values, out_weight, neighbours, counts):
    rows, width = queries.shape
    n_head = lax.axis_size("head")
    own_rows = rows // n_head
    model = out_weight.shape[1]
    small = n_head == 4 and own_rows % 16 == 0
    head_index = lax.axis_index("head").astype(jnp.int32)
    tile, head = lax.axis_index("ctx").astype(jnp.int32).reshape(1), head_index.reshape(1)

    one = (rows, HD)
    payload, kv_shape = shape((3 * rows + FLAGS, HD)), shape((2 * rows, HD))
    packed = (shape((rows + FLAGS, HD)), kv_shape, payload)
    keep_q, keep_kv, send = call(
        pack_kernel,
        packed,
        (tile, head, neighbours, counts.reshape(1, 1), queries, keys, values, out_weight),
        scratch=[pltpu.VMEM(each.shape, each.dtype) for each in packed]
        + [pltpu.SemaphoreType.DMA((6,)), pltpu.SemaphoreType.DMA((3,))],
        in_hbm=(4, 5, 6, 7),
        out_hbm=True,
        vmem=58,
    )
    weight_ready, _ = lax.optimization_barrier((out_weight, keep_kv))
    weight_pair = swap_cores(weight_ready)
    came = swap_tiles(send)
    kept_near = [swap_pairs(keep_kv, 1, phase) for phase in range(2)]
    if small:
        side_weight = call(side_kernel, shape((width, SIDE)), (tile, weight_ready))
        side_own = from_chip(side_weight, 1)

    held_q, held_kv = call(stage_kernel, (shape((rows + FLAGS, HD)), kv_shape), (keep_q, keep_kv))
    cut = []
    if small:
        ready, _ = lax.optimization_barrier((out_weight, held_q))
        cut.append(
            call(functools.partial(cut_kernel, first=2 * SIDE), shape((width, COMMON)), (ready,))
        )
    came, weight_pair, held_q, held_kv, kept_near, cut = lax.optimization_barrier(
        (came, weight_pair, held_q, held_kv, kept_near, cut)
    )
    far = 1 if lax.axis_size("ctx") <= 8 else 2
    flags, q_pair, came_kv, *to_far = call(
        merge_kernel if far == 2 else functools.partial(merge_kernel, even_ref=None),
        (shape((8, HD), jnp.int32), shape((2,) + one), kv_shape) + (kv_shape,) * far,
        (tile, held_q, held_kv, came),
        0,
    )
    came_near = [swap_pairs(came_kv, 1, phase) for phase in range(2)]
    farther = [swap_pairs(to_far[i], 2, i) for i in range(far)]

    state = shape((2, STATE, rows), F32)
    area = rows * rows
    held = call(
        first_kernel,
        state,
        (flags, tile, q_pair, held_kv, came_kv, *kept_near),
        32 * area * HD,
        8 * area,
    )
    q_again = q_pair
    if small:
        side_own, q_again = lax.optimization_barrier((side_own, q_pair))
        side_other = swap_tiles(side_own)
        ready, _ = lax.optimization_barrier((cut[0], side_own))
        common = from_chip(ready, 1)
    held = call(
        second_kernel,
        state,
        (flags, tile, q_again, *came_near, held),
        16 * area * HD,
        0,
        alias={5: 0},
    )
    block = (2, own_rows, HD)
    attended = call(
        functools.partial(third_kernel, far=far),
        ((shape(block),) * 4 if small else (shape(one),) * 2) + (state,),
        (flags, tile, head, q_pair, held, *farther),
        300 * area * HD,
        0,
        alias={4: 4 if small else 2},
    )[:-1]
    if not small:
        mine, theirs = attended
        got = swap_tiles(theirs)
        even_tile = tile[0] % 2 == 0
        joined = jnp.concatenate(
            [jnp.where(even_tile, mine, got), jnp.where(even_tile, got, mine)], axis=1
        )
        return project_any(joined, out_weight, weight_pair, head_index)

    mine, mine_other, theirs, theirs_other = attended
    from_cross = swap_both(theirs_other)
    from_y = swap_tiles(theirs)
    from_core = swap_cores(mine_other)
    from_cross, from_y, from_core, common = lax.optimization_barrier(
        (from_cross, from_y, from_core, common)
    )

    flops = 2 * own_rows * 2 * width * model
    near_weights = (out_weight, weight_pair)
    deep, gathered = 2 * width, 2 * SIDE + COMMON
    own_a, far_a = call(
        send_kernel,
        (shape((own_rows, deep)), shape((own_rows, deep + model - gathered))),
        (tile, head, mine, from_y, from_core, from_cross) + near_weights,
        flops // 4,
        vmem=16,
    )
    got = from_chip(far_a, 1)
    pieces = [side_own, side_other, common]
    *ready, _ = lax.optimization_barrier((*pieces, own_a))
    far_weights = [each for piece, to in zip(pieces, ready) for each in (piece, swap_cores(to))]
    near = call(near_kernel, shape((own_rows, model), F32), (own_a,) + near_weights, 30 * flops, vmem=16)
    return call(
        last_kernel,
        shape((own_rows, model)),
        (tile, near, got, *far_weights),
        flops,
        scratch=(pltpu.VMEM((own_rows, model), BF16), pltpu.SemaphoreType.DMA((4,))),
        out_hbm=True,
        vmem=20,
    )


def solution(mesh):
    placed = (
        P("ctx", "head"),
        P("ctx", "head"),
        P("ctx", "head"),
        P("head", None),
        P("ctx", None),
        P("ctx"),
    )
    return jax.shard_map(
        local, mesh=mesh, in_specs=placed, out_specs=P(("ctx", "head"), None), check_vma=False
    )
```

```python
import functools
import math

import jax
import jax.numpy as jnp
from jax import lax
from jax.experimental import pallas as pl
from jax.experimental.pallas import tpu as pltpu
from jax.sharding import PartitionSpec as P

HD = 128
REACH = 3
NEG = -1e30
FLAGS = 16
SIDE = 1280
COMMON = 1280
STATE = HD + 8
EXPONENT = math.log2(math.e) / math.sqrt(HD)
BF16, F32 = jnp.bfloat16, jnp.float32

SMEM = pl.BlockSpec(memory_space=pltpu.SMEM)
VMEM = pl.BlockSpec(memory_space=pltpu.VMEM)
HBM = pl.BlockSpec(memory_space=pltpu.HBM)


def call(
    kernel, outs, ins, flops=0, exps=0, moved=1 << 20, scratch=(), alias=None, in_hbm=(), out_hbm=False, vmem=8
):
    scalars = [x.dtype == jnp.int32 for x in ins]
    return pl.pallas_call(
        kernel,
        out_shape=outs,
        in_specs=[SMEM if s else (HBM if i in in_hbm else VMEM) for i, s in enumerate(scalars)],
        out_specs=jax.tree.map(lambda _: HBM if out_hbm else VMEM, outs),
        scratch_shapes=list(scratch),
        input_output_aliases=alias or {},
        compiler_params=pltpu.CompilerParams(vmem_limit_bytes=vmem << 20),
        cost_estimate=pl.CostEstimate(flops=flops, bytes_accessed=moved, transcendentals=exps),
    )(*ins)


def shape(dims, dtype=BF16):
    return jax.ShapeDtypeStruct(dims, dtype)


def pack_kernel(
    tile_ref, _, list_ref, count_ref, q_ref, k_ref, v_ref, __,
    keep_q_ref, keep_kv_ref, send_ref,
    keep_q, keep_kv, send, in_sems, out_sems,
):
    parity = tile_ref[0] & 1
    rows = q_ref.shape[0]
    reads, writes = [], []

    def read(source, target):
        reads.append(pltpu.make_async_copy(source, target, in_sems.at[len(reads)]))
        reads[-1].start()

    def write(count, source, target):
        for each in reads[len(reads) - left[0] :][:count]:
            each.wait()
        left[0] -= count
        writes.append(pltpu.make_async_copy(source, target, out_sems.at[len(writes)]))
        writes[-1].start()

    for head, kv_out, q_out, q_at in ((1 - parity, send, send, 2 * rows), (parity, keep_kv, keep_q, 0)):
        columns = pl.ds(pl.multiple_of(head * HD, HD), HD)
        for ref, out, at in ((k_ref, kv_out, 0), (v_ref, kv_out, rows), (q_ref, q_out, q_at)):
            read(ref.at[:, columns], out.at[pl.ds(at, rows)])
    lane = lax.broadcasted_iota(jnp.int32, (FLAGS, HD), 1)
    flags = jnp.zeros((FLAGS, HD), F32)
    for slot in range(list_ref.shape[1]):
        place = jnp.where(slot < count_ref[0, 0], list_ref[0, slot] - tile_ref[0] + REACH, -1)
        flags = jnp.where(lane == place, 1.0, flags)
    keep_q[rows:, :] = flags.astype(BF16)
    send[3 * rows :, :] = flags.astype(BF16)
    left = [len(reads)]
    write(3, send, send_ref)
    write(2, keep_kv, keep_kv_ref)
    write(1, keep_q, keep_q_ref)
    for each in writes:
        each.wait()


def stage_kernel(keep_q_ref, keep_kv_ref, q_ref, kv_ref):
    q_ref[...] = keep_q_ref[...]
    kv_ref[...] = keep_kv_ref[...]


def side_kernel(tile_ref, w_ref, side_ref):
    side = side_ref.shape[1]
    side_ref[...] = w_ref[:, pl.ds(pl.multiple_of((tile_ref[0] & 1) * side, HD), side)]


def cut_kernel(w_ref, common_ref, *, first):
    common_ref[...] = w_ref[:, first : first + common_ref.shape[1]]


def merge_kernel(
    tile_ref, keep_q_ref, keep_kv_ref, came_ref, flag_ref, q_ref, kv_ref, odd_ref, even_ref
):
    parity = tile_ref[0] & 1
    rows = q_ref.shape[1]
    kv_ref[...] = came_ref[0 : 2 * rows, :]
    up = (tile_ref[0] & 4) == 0

    def place(out, own):
        @pl.when(own)
        def _():
            out[...] = keep_kv_ref[...]

        @pl.when(jnp.logical_not(own))
        def _():
            out[...] = came_ref[0 : 2 * rows, :]

    place(odd_ref, up == (parity == 1))
    if even_ref is not None:
        place(even_ref, up == (parity == 0))
    q_ref[parity] = keep_q_ref[0:rows, :]
    q_ref[1 - parity] = came_ref[2 * rows : 3 * rows, :]
    own = keep_q_ref[rows:, :].astype(F32)
    other = came_ref[3 * rows :, :].astype(F32)
    even = jnp.where(parity == 0, own, other)[0:8]
    odd = jnp.where(parity == 0, other, own)[0:8]
    row = lax.broadcasted_iota(jnp.int32, (8, HD), 0)
    flag_ref[...] = jnp.where(row == 0, even, odd).astype(jnp.int32)


def step(query, key, value, state_ref, a):
    scores = lax.dot_general(
        key, query, (((1,), (1,)), ((), ())), preferred_element_type=F32
    )
    old = state_ref[a, HD : HD + 1, :]
    new = jnp.maximum(old, jnp.max(scores, axis=0, keepdims=True))
    weights = jnp.exp2((scores - new) * EXPONENT)
    shrink = jnp.exp2((old - new) * EXPONENT)
    state_ref[a, HD : HD + 1, :] = new
    state_ref[a, HD + 1 : HD + 2, :] = state_ref[a, HD + 1 : HD + 2, :] * shrink + jnp.sum(
        weights, axis=0, keepdims=True
    )
    state_ref[a, 0:HD, :] = state_ref[a, 0:HD, :] * shrink + lax.dot_general(
        value, weights.astype(BF16), (((0,), (0,)), ((), ())), preferred_element_type=F32
    )


def visit(flag_ref, q_ref, state_ref, pairs):
    rows = q_ref.shape[1]
    for a, tile, ref in pairs:

        @pl.when(flag_ref[a, tile - a + REACH] > 0)
        def _():
            step(q_ref[a], ref[0:rows, :], ref[rows : 2 * rows, :], state_ref, a)


def visit_pairs(flag_ref, tile_ref, q_ref, state_ref, tiles):
    parity = tile_ref[0] & 1
    for base, own, ref in tiles:
        tile = base + (parity if own else 1 - parity)
        visit(flag_ref, q_ref, state_ref, [(a, tile, ref) for a in range(2)])


def first_kernel(
    flag_ref, tile_ref, q_ref, own_ref, came_ref, kept_first_ref, kept_second_ref, state_ref
):
    state_ref[...] = jnp.zeros_like(state_ref)
    for a in range(2):
        state_ref[a, HD : HD + 1, :] = jnp.full((1, state_ref.shape[2]), NEG, F32)
    base = jnp.where((tile_ref[0] & 2) == 0, 2, -2)
    tiles = [(0, True, own_ref), (0, False, came_ref)]
    tiles += [(base, True, kept_first_ref), (-base, True, kept_second_ref)]
    visit_pairs(flag_ref, tile_ref, q_ref, state_ref, tiles)


def second_kernel(flag_ref, tile_ref, q_ref, first_ref, second_ref, _, state_ref):
    base = jnp.where((tile_ref[0] & 2) == 0, 2, -2)
    tiles = [(base, False, first_ref), (-base, False, second_ref)]
    visit_pairs(flag_ref, tile_ref, q_ref, state_ref, tiles)


def third_kernel(flag_ref, tile_ref, head_ref, q_ref, state_ref, *refs, far):
    outs, last = refs[far:-1], refs[-1]
    for i in range(far):
        above = ((tile_ref[0] & 4) == 0) == (i == 0)
        which = (jnp.where(above, 1, 0), jnp.where(above, 4, -3), refs[i])
        visit(flag_ref, q_ref, last, [which])
    parity = tile_ref[0] & 1
    core = head_ref[0] & 1
    for i, a in enumerate((parity, 1 - parity)):
        done = last[a, 0:HD, :] / last[a, HD + 1 : HD + 2, :]
        rows = done.T.astype(BF16)
        if len(outs) == 2:
            outs[i][...] = rows
        else:
            half = outs[0].shape[1]
            for chip in range(2):
                even = rows[(2 * chip) * half : (2 * chip + 1) * half]
                odd = rows[(2 * chip + 1) * half : (2 * chip + 2) * half]
                outs[2 * i][chip] = jnp.where(core == 0, even, odd)
                outs[2 * i + 1][chip] = jnp.where(core == 0, odd, even)


CHUNK = 512


def multiply(left, weights, start, stop):
    depth = weights[0].shape[0]
    return sum(
        jnp.dot(
            left[:, i * depth : (i + 1) * depth], w[:, start:stop], preferred_element_type=F32
        )
        for i, w in enumerate(weights)
    )


def send_kernel(
    tile_ref, head_ref, own_ref, y_ref, core_ref, cross_ref, w_ref, wp_ref, a_ref, far_ref
):
    parity = tile_ref[0] & 1
    chip = head_ref[0] >> 1
    deep = a_ref.shape[1]
    for out, which in ((a_ref, chip), (far_ref, 1 - chip)):
        for group, (mine, others) in enumerate(((own_ref, y_ref), (core_ref, cross_ref))):
            base = group * 2 * HD
            out[:, pl.ds(pl.multiple_of(base + parity * HD, HD), HD)] = mine[which]
            out[:, pl.ds(pl.multiple_of(base + (1 - parity) * HD, HD), HD)] = others[which]
    far = far_ref[:, 0:deep]
    term = far_ref.shape[1] - deep
    gathered = w_ref.shape[1] - term
    for start in range(0, term, CHUNK):
        stop = min(start + CHUNK, term)
        far_ref[:, deep + start : deep + stop] = multiply(
            far, (w_ref, wp_ref), gathered + start, gathered + stop
        ).astype(BF16)


def near_kernel(a_ref, w_ref, wp_ref, near_ref):
    own = a_ref[...]
    for start in range(0, w_ref.shape[1], CHUNK):
        near_ref[:, start : start + CHUNK] = multiply(own, (w_ref, wp_ref), start, start + CHUNK)


def last_kernel(tile_ref, near_ref, far_ref, *refs):
    weights, (out_ref, done_ref, sems) = refs[:6], refs[6:]
    parity = tile_ref[0] & 1
    deep = 2 * weights[0].shape[0]
    side = weights[0].shape[1]
    far = far_ref[:, 0:deep]
    gathered = 2 * side + weights[4].shape[1]
    copies = []

    def write(columns):
        copies.append(
            pltpu.make_async_copy(
                done_ref.at[:, columns], out_ref.at[:, columns], sems.at[len(copies)]
            )
        )
        copies[-1].start()

    done_ref[:, gathered:] = (near_ref[:, gathered:] + far_ref[:, deep:].astype(F32)).astype(BF16)
    write(pl.ds(gathered, near_ref.shape[1] - gathered))
    for i, first in enumerate((2 * side, parity * side, (1 - parity) * side)):
        pair = weights[4:6] if i == 0 else weights[2 * i - 2 : 2 * i]
        width = pair[0].shape[1]
        for start in range(0, width, CHUNK):
            stop = min(start + CHUNK, width)
            columns = pl.ds(pl.multiple_of(first + start, HD), stop - start)
            done_ref[:, columns] = (
                near_ref[:, columns] + multiply(far, pair, start, stop)
            ).astype(BF16)
        write(pl.ds(pl.multiple_of(first, HD), width))
    for each in copies:
        each.wait()


def swap_pairs(value, distance, phase):
    count = lax.axis_size("ctx")
    pairs = []
    for i in range(count - 2 * distance):
        if (i // 2 // distance) % 2 == phase:
            pairs += [(i, i + 2 * distance), (i + 2 * distance, i)]
    return lax.ppermute(value, "ctx", pairs)


def swap_tiles(value):
    return lax.ppermute(value, "ctx", [(i, i ^ 1) for i in range(lax.axis_size("ctx"))])


def swap_cores(value):
    return lax.ppermute(value, "head", [(i, i ^ 1) for i in range(lax.axis_size("head"))])


def swap_both(value):
    heads = lax.axis_size("head")
    count = lax.axis_size("ctx") * heads
    pairs = [(i, ((i // heads) ^ 1) * heads + ((i % heads) ^ 1)) for i in range(count)]
    return lax.ppermute(value, ("ctx", "head"), pairs)


def from_chip(value, steps):
    count = lax.axis_size("head")
    return lax.ppermute(value, "head", [((i + 2 * steps) % count, i) for i in range(count)])


def project_any(attended, out_weight, weight_pair, head_index):
    rows, width = attended.shape
    n_head = lax.axis_size("head")
    chips, own_rows = n_head // 2, rows // n_head
    chip, core = head_index // 2, head_index % 2
    blocks = attended.reshape(chips, 2, own_rows, width)
    mine = lax.dynamic_index_in_dim(blocks, core, 1, keepdims=False)
    theirs = lax.dynamic_index_in_dim(blocks, 1 - core, 1, keepdims=False)
    joined = jnp.concatenate([mine, swap_cores(theirs)], axis=2)

    def project(steps):
        block = lax.dynamic_index_in_dim(joined, (chip - steps) % chips, 0, keepdims=False)
        return multiply(block, (out_weight, weight_pair), 0, out_weight.shape[1])

    total = project(0)
    for steps in range(1, chips):
        total = total + from_chip(project(steps).astype(BF16), steps).astype(F32)
    return total.astype(BF16)


def local(queries, keys, values, out_weight, neighbours, counts):
    rows, width = queries.shape
    n_head = lax.axis_size("head")
    own_rows = rows // n_head
    model = out_weight.shape[1]
    small = n_head == 4 and own_rows % 16 == 0
    head_index = lax.axis_index("head").astype(jnp.int32)
    tile, head = lax.axis_index("ctx").astype(jnp.int32).reshape(1), head_index.reshape(1)

    one = (rows, HD)
    payload, kv_shape = shape((3 * rows + FLAGS, HD)), shape((2 * rows, HD))
    packed = (shape((rows + FLAGS, HD)), kv_shape, payload)
    keep_q, keep_kv, send = call(
        pack_kernel,
        packed,
        (tile, head, neighbours, counts.reshape(1, 1), queries, keys, values, out_weight),
        scratch=[pltpu.VMEM(each.shape, each.dtype) for each in packed]
        + [pltpu.SemaphoreType.DMA((6,)), pltpu.SemaphoreType.DMA((3,))],
        in_hbm=(4, 5, 6, 7),
        out_hbm=True,
        vmem=58,
    )
    weight_ready, _ = lax.optimization_barrier((out_weight, keep_kv))
    weight_pair = swap_cores(weight_ready)
    came = swap_tiles(send)
    kept_near = [swap_pairs(keep_kv, 1, phase) for phase in range(2)]
    if small:
        side_weight = call(side_kernel, shape((width, SIDE)), (tile, weight_ready))
        side_own = from_chip(side_weight, 1)

    held_q, held_kv = call(stage_kernel, (shape((rows + FLAGS, HD)), kv_shape), (keep_q, keep_kv))
    cut = []
    if small:
        ready, _ = lax.optimization_barrier((out_weight, held_q))
        cut.append(
            call(functools.partial(cut_kernel, first=2 * SIDE), shape((width, COMMON)), (ready,))
        )
    came, weight_pair, held_q, held_kv, kept_near, cut = lax.optimization_barrier(
        (came, weight_pair, held_q, held_kv, kept_near, cut)
    )
    far = 1 if lax.axis_size("ctx") <= 8 else 2
    flags, q_pair, came_kv, *to_far = call(
        merge_kernel if far == 2 else functools.partial(merge_kernel, even_ref=None),
        (shape((8, HD), jnp.int32), shape((2,) + one), kv_shape) + (kv_shape,) * far,
        (tile, held_q, held_kv, came),
        0,
    )
    came_near = [swap_pairs(came_kv, 1, phase) for phase in range(2)]
    farther = [swap_pairs(to_far[i], 2, i) for i in range(far)]

    state = shape((2, STATE, rows), F32)
    area = rows * rows
    held = call(
        first_kernel,
        state,
        (flags, tile, q_pair, held_kv, came_kv, *kept_near),
        32 * area * HD,
        8 * area,
    )
    q_again = q_pair
    if small:
        side_own, q_again = lax.optimization_barrier((side_own, q_pair))
        side_other = swap_tiles(side_own)
        ready, _ = lax.optimization_barrier((cut[0], side_own))
        common = from_chip(ready, 1)
    held = call(
        second_kernel,
        state,
        (flags, tile, q_again, *came_near, held),
        16 * area * HD,
        0,
        alias={5: 0},
    )
    block = (2, own_rows, HD)
    attended = call(
        functools.partial(third_kernel, far=far),
        ((shape(block),) * 4 if small else (shape(one),) * 2) + (state,),
        (flags, tile, head, q_pair, held, *farther),
        300 * area * HD,
        0,
        alias={4: 4 if small else 2},
    )[:-1]
    if not small:
        mine, theirs = attended
        got = swap_tiles(theirs)
        even_tile = tile[0] % 2 == 0
        joined = jnp.concatenate(
            [jnp.where(even_tile, mine, got), jnp.where(even_tile, got, mine)], axis=1
        )
        return project_any(joined, out_weight, weight_pair, head_index)

    mine, mine_other, theirs, theirs_other = attended
    from_cross = swap_both(theirs_other)
    from_y = swap_tiles(theirs)
    from_core = swap_cores(mine_other)
    from_cross, from_y, from_core, common = lax.optimization_barrier(
        (from_cross, from_y, from_core, common)
    )

    flops = 2 * own_rows * 2 * width * model
    near_weights = (out_weight, weight_pair)
    deep, gathered = 2 * width, 2 * SIDE + COMMON
    own_a, far_a = call(
        send_kernel,
        (shape((own_rows, deep)), shape((own_rows, deep + model - gathered))),
        (tile, head, mine, from_y, from_core, from_cross) + near_weights,
        flops // 4,
        vmem=16,
    )
    got = from_chip(far_a, 1)
    pieces = [side_own, side_other, common]
    *ready, _ = lax.optimization_barrier((*pieces, own_a))
    far_weights = [each for piece, to in zip(pieces, ready) for each in (piece, swap_cores(to))]
    near = call(near_kernel, shape((own_rows, model), F32), (own_a,) + near_weights, 30 * flops, vmem=16)
    return call(
        last_kernel,
        shape((own_rows, model)),
        (tile, near, got, *far_weights),
        flops,
        scratch=(pltpu.VMEM((own_rows, model), BF16), pltpu.SemaphoreType.DMA((4,))),
        out_hbm=True,
        vmem=20,
    )


def solution(mesh):
    placed = (
        P("ctx", "head"),
        P("ctx", "head"),
        P("ctx", "head"),
        P("head", None),
        P("ctx", None),
        P("ctx"),
    )
    return jax.shard_map(
        local, mesh=mesh, in_specs=placed, out_specs=P(("ctx", "head"), None), check_vma=False
    )
```
